32 devices in a mesh: section: 8 (over y, x, core), tensor: 4 (over z).
Axes of the slice: x: 2, y: 2, z: 4, core: 2. Of those that a mesh axis runs over, the one named last changes fastest.
Arguments:
- weights: bfloat16 [8, 4096, 4096], P('section', 'tensor'), may hold values from -0.09375 to 0.09375
- filters: float32 [8, 32, 128], P('section'), may hold values from -0.5 to 0.5
- down_input: bfloat16 [8, 512, 4096], P('section', 'tensor'), may hold values from -6 to 6
- down_cot: bfloat16 [8, 512, 4096], P('section', 'tensor'), may hold values from -6 to 6
- up_input: bfloat16 [8, 512, 4096], P('section', 'tensor'), may hold values from -6 to 6
- up_cot: bfloat16 [8, 512, 4096], P('section', 'tensor'), may hold values from -6 to 6
Outputs:
- weight_grad: bfloat16 [8, 4096, 4096], P('section', 'tensor')
- filter_grad: float32 [8, 32, 128], P('section')
- down_passed: bfloat16 [8, 512, 4096], P('section', 'tensor')
- up_passed: bfloat16 [8, 512, 4096], P('section', 'tensor')
The draws below stay inside these ranges and needn't reach their ends.
All inputs are finite; a program needn't handle non-finite values.
Results may differ from the reference program's by a relative error of at most 0.014.
Values may be sent and summed in bfloat16 or wider, within the bound.
No kernel may reach another device: no remote copies, remote signals or barrier semaphores. Data moves between devices by JAX's collectives and lax.ppermute only.
A program may use at most 192 MiB of HBM per device.

```python
import jax
import jax.numpy as jnp
from jax import lax

D = 4096
K = 128
GROUPS = 32
TOKENS = 512
LAYERS = 8


def levels(stream_key, extent, shards, least, high):
    gain, own = 1.0, jax.random.fold_in(stream_key, 6)
    for position, blocks in shards:
        steps = jnp.exp(jax.random.uniform(jax.random.fold_in(own, position), (blocks,), jnp.float32, least / len(shards), high / len(shards)))
        gain = gain * jnp.repeat(steps, extent[position] // blocks).reshape([-1 if axis == position else 1 for axis in range(len(extent))])
    return gain


def noise(key, extent, deviation, reach, split=(), held_as=jnp.bfloat16):
    gain = levels(key, extent, split, -0.22, 0.18) if split else 1.0
    result = jax.random.normal(key, extent, jnp.float32) * deviation * gain
    return jnp.minimum(jnp.maximum(result, -reach), reach).astype(held_as)


def setup_inputs(seed: int = 0) -> dict:
    key_of = jax.random.split(jax.random.key(seed), 7)
    weights = noise(key_of[0], (LAYERS, D, D), D ** -0.5, 0.09375, ((0, 8), (1, 4)))
    filters = noise(key_of[1], (LAYERS, GROUPS, K), K ** -0.5, 0.5, ((0, 8),), jnp.float32)
    down_input = noise(key_of[2], (LAYERS, TOKENS, D), 1.0, 6.0, ((0, 8), (1, 4)))
    down_cot = noise(key_of[3], (LAYERS, TOKENS, D), 1.0, 6.0, ((0, 8), (1, 4)))
    up_input = noise(key_of[4], (LAYERS, TOKENS, D), 1.0, 6.0, ((0, 8), (1, 4)))
    up_cot = noise(key_of[5], (LAYERS, TOKENS, D), 1.0, 6.0, ((0, 8), (1, 4)))
    return {"weights": weights, "filters": filters, "down_input": down_input, "down_cot": down_cot, "up_input": up_input, "up_cot": up_cot}


epsilon = 1e-06

def causal_mix(extended, kernel, count):
    taps_total = kernel.shape[0]

    def add_tap(tap_index, running):
        window = lax.dynamic_slice_in_dim(extended, taps_total - 1 - tap_index, count, 0)
        return running + lax.dynamic_index_in_dim(kernel, tap_index, 0, keepdims=False) * window
    return lax.fori_loop(0, taps_total, add_tap, jnp.zeros((count,) + extended.shape[1:], jnp.float32))

def ahead_mix(extended, kernel, count):
    taps_total = kernel.shape[0]

    def add_tap(tap_index, running):
        window = lax.dynamic_slice_in_dim(extended, tap_index, count, 0)
        return running + lax.dynamic_index_in_dim(kernel, tap_index, 0, keepdims=False) * window
    return lax.fori_loop(0, taps_total, add_tap, jnp.zeros((count,) + extended.shape[1:], jnp.float32))

def layer_grads(inputs, cotangent, weight, filter_taps):
    count = inputs.shape[0]
    model_width = inputs.shape[1]
    group_count = filter_taps.shape[0]
    taps_total = filter_taps.shape[1]
    input_wide = inputs.astype(jnp.float32)
    inverse_rms = lax.rsqrt(lax.optimization_barrier(jnp.mean(input_wide * input_wide, axis=1, keepdims=True)) + epsilon)
    normed = input_wide * inverse_rms
    normed_b = normed.astype(jnp.bfloat16)
    values = jnp.dot(normed_b, weight, preferred_element_type=jnp.float32)
    kernel = jnp.repeat(jnp.transpose(filter_taps), model_width // group_count, axis=1)
    extended = jnp.concatenate([jnp.zeros((taps_total - 1, model_width), jnp.float32), values], axis=0)
    convolved = causal_mix(extended, kernel, count)
    cot_wide = cotangent.astype(jnp.float32)
    grad_mix = cot_wide * normed
    grad_ext = jnp.concatenate([grad_mix, jnp.zeros((taps_total - 1, model_width), jnp.float32)], axis=0)
    grad_values = ahead_mix(grad_ext, kernel, count)

    def one_tap(tap_index):
        window = lax.dynamic_slice_in_dim(extended, taps_total - 1 - tap_index, count, 0)
        return lax.optimization_barrier(jnp.sum(grad_mix * window, axis=0))
    per_tap = lax.map(one_tap, jnp.arange(taps_total, dtype=jnp.int32))
    tap_grad = jnp.transpose(lax.optimization_barrier(jnp.sum(per_tap.reshape(taps_total, group_count, -1), axis=2)))
    grad_values_b = grad_values.astype(jnp.bfloat16)
    weight_part = jnp.dot(jnp.transpose(normed_b), grad_values_b, preferred_element_type=jnp.float32)
    grad_total = cot_wide * convolved + jnp.dot(grad_values_b, jnp.transpose(weight), preferred_element_type=jnp.float32)
    projection_mean = lax.optimization_barrier(jnp.mean(grad_total * normed, axis=1, keepdims=True))
    grad_in = (cot_wide + inverse_rms * (grad_total - normed * projection_mean)).astype(jnp.bfloat16)
    return (grad_in, weight_part, tap_grad)

def reference(weights, filters, down_input, down_cot, up_input, up_cot):

    def per_layer(operands):
        weight, filter_taps, down_in, down_ct, up_in, up_ct = operands
        down_grad, down_weight, down_taps = layer_grads(down_in, down_ct, weight, filter_taps)
        up_grad, up_weight, up_taps = layer_grads(up_in, up_ct, weight, filter_taps)
        return (down_grad, up_grad, (down_weight + up_weight).astype(jnp.bfloat16), down_taps + up_taps)
    down_grads, up_grads, weight_grad, filter_grad = lax.map(per_layer, (weights, filters, down_input, down_cot, jnp.flip(up_input, 0), jnp.flip(up_cot, 0)))
    zero_block = jnp.zeros((1,) + down_grads.shape[1:], jnp.bfloat16)
    down_passed = jnp.concatenate([down_grads[1:], zero_block], axis=0)
    up_passed = jnp.concatenate([zero_block, jnp.flip(up_grads[1:], 0)], axis=0)
    return (weight_grad, filter_grad, down_passed, up_passed)
```

```python
import functools

import jax
import jax.numpy as jnp
from jax import lax
from jax.experimental import pallas as pl
from jax.experimental.pallas import tpu as pltpu
from jax.sharding import PartitionSpec as P

epsilon = 1e-06
params = functools.partial(pltpu.CompilerParams, vmem_limit_bytes=40 * 1024 * 1024)
f32, bf16 = jnp.float32, jnp.bfloat16


def dot(a, b, dims=((1,), (0,))):
    return lax.dot_general(a, b, (dims, ((), ())), preferred_element_type=f32)


def shape(dims, dtype):
    return jax.ShapeDtypeStruct(dims, dtype)


def toeplitz_kernel(filters_ref, causal_ref, ahead_ref):
    taps = filters_ref.shape[1]
    row = lax.broadcasted_iota(jnp.int32, (taps, taps), 0)
    col = lax.broadcasted_iota(jnp.int32, (taps, taps), 1)
    for g in range(filters_ref.shape[0]):
        line = jnp.broadcast_to(filters_ref[g : g + 1, :], (taps, taps))
        turned = pltpu.roll(line, 0, 1, stride=1, stride_axis=0)
        own = jnp.where(col >= row, turned, 0.0)
        beyond = jnp.where(col < row, turned, 0.0)
        ahead_ref[g, :, :taps] = own.astype(bf16)
        ahead_ref[g, :, taps:] = beyond.astype(bf16)
        causal_ref[g, :, :taps] = beyond.T.astype(bf16)
        causal_ref[g, :, taps:] = own.T.astype(bf16)


def toeplitz(filters):
    groups, taps = filters.shape
    step = 8
    out = shape((groups, taps, 2 * taps), bf16)
    spec = pl.BlockSpec((step, taps, 2 * taps), lambda i: (i, 0, 0))
    return pl.pallas_call(
        toeplitz_kernel,
        grid=(groups // step,),
        in_specs=[pl.BlockSpec((step, taps), lambda i: (i, 0))],
        out_specs=[spec, spec],
        out_shape=[out, out],
        compiler_params=params(),
        name="toeplitz",
    )(filters)


def prepare_kernel(xin_ref, cot_ref, normed_ref, mix_ref):
    wide = xin_ref[...].astype(f32)
    inverse = lax.rsqrt(jnp.mean(wide * wide, axis=1, keepdims=True) + epsilon)
    normed = wide * inverse
    mix_ref[...] = (cot_ref[...].astype(f32) * normed).astype(bf16)
    width = normed_ref.shape[2]
    for i in range(normed_ref.shape[0]):
        normed_ref[i] = normed[:, i * width : (i + 1) * width].astype(bf16)


def prepare(xin, cot, blocks):
    rows, width = xin.shape
    step = 32
    spec = pl.BlockSpec((step, width), lambda i: (i, 0))
    return pl.pallas_call(
        prepare_kernel,
        grid=(rows // step,),
        in_specs=[spec, spec],
        out_specs=[pl.BlockSpec((blocks, step, width // blocks), lambda i: (0, i, 0)), spec],
        out_shape=[shape((blocks, rows, width // blocks), bf16), shape((rows, width), bf16)],
        compiler_params=params(),
        name="prepare",
    )(xin, cot)


def project_kernel(normed_ref, weight_ref, causal_ref, part_ref, mixed_ref):
    taps = causal_ref.shape[1]
    groups = causal_ref.shape[0]
    part = dot(normed_ref[...], weight_ref[...]).astype(bf16)
    part_ref[...] = part
    width = part.shape[1] // groups
    for g in range(groups):
        cols = slice(g * width, (g + 1) * width)
        for start in range(0, part.shape[0], taps):
            if start == 0:
                out = dot(causal_ref[g, :, taps:], part[:taps, cols])
            else:
                out = dot(causal_ref[g], part[start - taps : start + taps, cols])
            mixed_ref[start : start + taps, cols] = out.astype(bf16)


def project(normed, weight, causal):
    tokens, depth = normed.shape
    width = weight.shape[1]
    groups, taps, _ = causal.shape
    step = 4
    tile = width // groups * step
    spec = pl.BlockSpec((tokens, tile), lambda i: (0, i))
    return pl.pallas_call(
        project_kernel,
        grid=(groups // step,),
        in_specs=[
            pl.BlockSpec((tokens, depth), lambda i: (0, 0)),
            pl.BlockSpec((depth, tile), lambda i: (0, i)),
            pl.BlockSpec((step, taps, 2 * taps), lambda i: (i, 0, 0)),
        ],
        out_specs=[spec, spec],
        out_shape=[shape((tokens, width), bf16)] * 2,
        compiler_params=params(),
        name="project",
    )(normed, weight, causal)


def back_kernel(mix_ref, part_ref, weight_ref, ahead_ref, grad_ref, back_ref, taps_ref, total):
    groups, taps, _ = ahead_ref.shape
    tokens = mix_ref.shape[0]
    width = mix_ref.shape[1] // groups
    row = lax.broadcasted_iota(jnp.int32, (taps, taps), 0)
    col = lax.broadcasted_iota(jnp.int32, (taps, taps), 1)
    starts = range(0, tokens, taps)
    for g in range(groups):
        cols = slice(g * width, (g + 1) * width)
        mix = mix_ref[:, cols]
        part = part_ref[:, cols]
        for start in starts:
            if start + taps == tokens:
                out = dot(ahead_ref[g, :, :taps], mix[start:])
            else:
                out = dot(ahead_ref[g], mix[start : start + 2 * taps])
            grad_ref[start : start + taps, cols] = out.astype(bf16)
        mixes = jnp.concatenate([mix[s : s + taps] for s in starts], axis=1)
        parts = jnp.concatenate([part[s : s + taps] for s in starts], axis=1)
        same = dot(parts, mixes, ((1,), (1,)))
        later = dot(parts[:, :-width], mixes[:, width:], ((1,), (1,)))
        pairs = jnp.where(col >= row, same, later)
        folded = pairs[0:8]
        for a in range(8, taps, 8):
            folded = folded + pltpu.roll(pairs[a : a + 8], taps - a, 1)
        line = folded[0:1]
        for b in range(1, 8):
            line = line + pltpu.roll(folded[b : b + 1], taps - b, 1)
        taps_ref[0, g : g + 1, :] = line
    product = dot(grad_ref[...], weight_ref[...], ((1,), (1,)))
    step = pl.program_id(0)

    @pl.when(step == 0)
    def _():
        total[...] = product

    @pl.when(step > 0)
    def _():
        total[...] += product

    @pl.when(step == pl.num_programs(0) - 1)
    def _():
        back_ref[...] = total[...].astype(bf16)


def back(mix, part, weight, ahead):
    tokens, width = mix.shape
    depth = weight.shape[0]
    groups, taps, _ = ahead.shape
    step = 4
    tile = width // groups * step
    spec = pl.BlockSpec((tokens, tile), lambda i: (0, i))
    return pl.pallas_call(
        back_kernel,
        grid=(groups // step,),
        in_specs=[
            spec,
            spec,
            pl.BlockSpec((depth, tile), lambda i: (0, i)),
            pl.BlockSpec((step, taps, 2 * taps), lambda i: (i, 0, 0)),
        ],
        out_specs=[
            spec,
            pl.BlockSpec((tokens, depth), lambda i: (0, 0)),
            pl.BlockSpec((1, step, taps), lambda i: (i, 0, 0)),
        ],
        out_shape=[
            shape((tokens, width), bf16),
            shape((tokens, depth), bf16),
            shape((groups // step, step, taps), f32),
        ],
        scratch_shapes=[pltpu.VMEM((tokens, depth), f32)],
        compiler_params=params(),
        name="back",
    )(mix, part, weight, ahead)


def weight_kernel(down_x, up_x, down_g, up_g, out_ref, down_t, up_t):
    @pl.when(pl.program_id(0) == 0)
    def _():
        down_t[...] = down_x[...].T
        up_t[...] = up_x[...].T

    out_ref[...] = (dot(down_t[...], down_g[...]) + dot(up_t[...], up_g[...])).astype(bf16)


def weight_gradient(down_x, up_x, down_g, up_g):
    tokens, depth = down_x.shape
    width = down_g.shape[1]
    tile = width // 8
    whole = pl.BlockSpec((tokens, depth), lambda i: (0, 0))
    part = pl.BlockSpec((tokens, tile), lambda i: (0, i))
    return pl.pallas_call(
        weight_kernel,
        grid=(width // tile,),
        in_specs=[whole, whole, part, part],
        out_specs=pl.BlockSpec((depth, tile), lambda i: (0, i)),
        out_shape=shape((depth, width), bf16),
        scratch_shapes=[pltpu.VMEM((depth, tokens), bf16)] * 2,
        compiler_params=params(),
        name="weight_gradient",
    )(down_x, up_x, down_g, up_g)


def finish_kernel(xin_ref, cot_ref, mixed_ref, back_ref, out_ref):
    wide = xin_ref[...].astype(f32)
    inverse = lax.rsqrt(jnp.mean(wide * wide, axis=1, keepdims=True) + epsilon)
    normed = wide * inverse
    cot = cot_ref[...].astype(f32)
    returned = jnp.concatenate([back_ref[i] for i in range(back_ref.shape[0])], axis=1)
    total = cot * mixed_ref[...].astype(f32) + returned.astype(f32)
    mean = jnp.mean(total * normed, axis=1, keepdims=True)
    out_ref[...] = (cot + inverse * (total - normed * mean)).astype(bf16)


def finish(xin, cot, mixed, returned):
    rows, width = xin.shape
    blocks, _, depth = returned.shape
    step = 32
    spec = pl.BlockSpec((step, width), lambda i: (i, 0))
    return pl.pallas_call(
        finish_kernel,
        grid=(rows // step,),
        in_specs=[spec, spec, spec, pl.BlockSpec((blocks, step, depth), lambda i: (0, i, 0))],
        out_specs=spec,
        out_shape=shape((rows, width), bf16),
        compiler_params=params(),
        name="finish",
    )(xin, cot, mixed, returned)


def exchange(x):
    return lax.all_to_all(x, "tensor", split_axis=0, concat_axis=0, tiled=True)


def forward_half(xin, cot, weight, causal):
    blocks = lax.axis_size("tensor")
    normed, mix = prepare(xin, cot, blocks)
    features = exchange(normed)
    features = features.reshape(blocks * xin.shape[0], -1)
    mixes = lax.all_gather(mix, "tensor", axis=0, tiled=True)
    part, mixed = project(features, weight, causal)
    convolved = lax.psum_scatter(mixed, "tensor", scatter_dimension=0, tiled=True)
    return features, mixes, part, convolved


def backward_half(xin, cot, mixes, part, convolved, weight, ahead):
    grads, returned, taps = back(mixes, part, weight, ahead)
    returned = exchange(returned.reshape(-1, xin.shape[0], returned.shape[1]))
    return grads, taps, finish(xin, cot, convolved, returned)


def per_device(weights, filters, down_input, down_cot, up_input, up_cot):
    sections = lax.axis_size("section")
    mirror = [(s, sections - 1 - s) for s in range(sections)]
    down_pairs = [(s + 1, s) for s in range(sections - 1)]
    up_pairs = [(sections - s, s) for s in range(1, sections)]
    weight = weights[0]
    down = (down_input[0], down_cot[0])
    up = (lax.ppermute(up_input[0], "section", mirror), lax.ppermute(up_cot[0], "section", mirror))
    causal, ahead = toeplitz(filters[0])

    down_x, down_mixes, down_part, down_conv = forward_half(*down, weight, causal)
    up_x, up_mixes, up_part, up_conv = forward_half(*up, weight, causal)
    down_g, down_taps, down_grad = backward_half(
        *down, down_mixes, down_part, down_conv, weight, ahead
    )
    down_passed = lax.ppermute(down_grad, "section", down_pairs)
    up_g, up_taps, up_grad = backward_half(*up, up_mixes, up_part, up_conv, weight, ahead)
    up_passed = lax.ppermute(up_grad, "section", up_pairs)
    weight_grad = weight_gradient(down_x, up_x, down_g, up_g)
    taps = lax.psum((down_taps + up_taps).reshape(filters.shape[1:]), "tensor")
    return weight_grad[None], taps[None], down_passed[None], up_passed[None]


def solution(mesh):
    rows = P("section", "tensor", None)
    whole = P("section", None, None)
    return jax.shard_map(
        per_device,
        mesh=mesh,
        in_specs=(rows, whole, rows, rows, rows, rows),
        out_specs=(rows, whole, rows, rows),
        check_vma=False,
    )
```

```python
import functools

import jax
import jax.numpy as jnp
from jax import lax
from jax.experimental import pallas as pl
from jax.experimental.pallas import tpu as pltpu
from jax.sharding import PartitionSpec as P

epsilon = 1e-06
params = functools.partial(pltpu.CompilerParams, vmem_limit_bytes=40 * 1024 * 1024)
f32, bf16 = jnp.float32, jnp.bfloat16


def dot(a, b, dims=((1,), (0,))):
    return lax.dot_general(a, b, (dims, ((), ())), preferred_element_type=f32)


def shape(dims, dtype):
    return jax.ShapeDtypeStruct(dims, dtype)


def call(kernel, args, after, in_specs, **options):
    count = len(args)

    def body(*refs):
        kernel(*refs[:count], *refs[count + len(after) :])

    unread = [pl.BlockSpec(memory_space=pl.ANY)] * len(after)
    return pl.pallas_call(
        body, in_specs=list(in_specs) + unread, compiler_params=params(), **options
    )(*args, *after)


def toeplitz_kernel(filters_ref, causal_ref, ahead_ref):
    taps = filters_ref.shape[1]
    row = lax.broadcasted_iota(jnp.int32, (taps, taps), 0)
    col = lax.broadcasted_iota(jnp.int32, (taps, taps), 1)
    for g in range(filters_ref.shape[0]):
        line = jnp.broadcast_to(filters_ref[g : g + 1, :], (taps, taps))
        turned = pltpu.roll(line, 0, 1, stride=1, stride_axis=0)
        own = jnp.where(col >= row, turned, 0.0)
        beyond = jnp.where(col < row, turned, 0.0)
        ahead_ref[g, :, :taps] = own.astype(bf16)
        ahead_ref[g, :, taps:] = beyond.astype(bf16)
        causal_ref[g, :, :taps] = beyond.T.astype(bf16)
        causal_ref[g, :, taps:] = own.T.astype(bf16)


def toeplitz(filters):
    groups, taps = filters.shape
    step = 8
    out = shape((groups, taps, 2 * taps), bf16)
    spec = pl.BlockSpec((step, taps, 2 * taps), lambda i: (i, 0, 0))
    return call(
        toeplitz_kernel,
        (filters,),
        (),
        grid=(groups // step,),
        in_specs=[pl.BlockSpec((step, taps), lambda i: (i, 0))],
        out_specs=[spec, spec],
        out_shape=[out, out],
        name="toeplitz",
    )


def place(by):
    blocks = lax.axis_size("tensor")
    return lax.rem(lax.axis_index("tensor") + (by + blocks), blocks)


def window(index, size):
    return pl.ds(pl.multiple_of(index * size, size), size)


def normalise(wide):
    inverse = lax.rsqrt(jnp.mean(wide * wide, axis=1, keepdims=True) + epsilon)
    return wide * inverse, inverse


def normed_kernel(xin_ref, *rest):
    *piece_refs, normed_ref = rest
    normed_ref[...] = normalise(xin_ref[...].astype(f32))[0].astype(bf16)
    for s, piece_ref in enumerate(piece_refs):
        piece_ref[...] = normed_ref[:, window(place(s), piece_ref.shape[1])]


def normed_pieces(xin, after=()):
    rows, width = xin.shape
    blocks = lax.axis_size("tensor")
    step = 32
    piece = pl.BlockSpec((step, width // blocks), lambda i: (i, 0))
    return call(
        normed_kernel,
        (xin,),
        after,
        grid=(rows // step,),
        in_specs=[pl.BlockSpec((step, width), lambda i: (i, 0))],
        out_specs=[piece] * blocks,
        out_shape=[shape((rows, width // blocks), bf16)] * blocks,
        scratch_shapes=[pltpu.VMEM((step, width), bf16)],
        name="normed_pieces",
    )


def mix_kernel(xin_ref, cot_ref, mix_ref):
    normed, _ = normalise(xin_ref[...].astype(f32))
    mix_ref[...] = (cot_ref[...].astype(f32) * normed).astype(bf16)


def grad_mix(xin, cot, after=()):
    rows, width = xin.shape
    step = 32
    spec = pl.BlockSpec((step, width), lambda i: (i, 0))
    return call(
        mix_kernel,
        (xin, cot),
        after,
        grid=(rows // step,),
        in_specs=[spec, spec],
        out_specs=spec,
        out_shape=shape((rows, width), bf16),
        name="grad_mix",
    )


def project_kernel(blocks, *refs):
    piece_refs = refs[:blocks]
    weight_ref, causal_ref, features_ref, part_ref, mixed_ref = refs[blocks:]
    groups, taps, _ = causal_ref.shape

    @pl.when(pl.program_id(0) == 0)
    def _():
        for s, piece_ref in enumerate(piece_refs):
            features_ref[window(place(-s), piece_ref.shape[0]), :] = piece_ref[...]

    part = dot(features_ref[...], weight_ref[...]).astype(bf16)
    part_ref[...] = part
    width = part.shape[1] // groups
    for g in range(groups):
        cols = slice(g * width, (g + 1) * width)
        for start in range(0, part.shape[0], taps):
            if start == 0:
                out = dot(causal_ref[g, :, taps:], part[:taps, cols])
            else:
                out = dot(causal_ref[g], part[start - taps : start + taps, cols])
            mixed_ref[start : start + taps, cols] = out.astype(bf16)


def project(pieces, weight, causal, after=()):
    blocks = len(pieces)
    rows, depth = pieces[0].shape
    tokens = blocks * rows
    width = weight.shape[1]
    groups, taps, _ = causal.shape
    step = 4
    tile = width // groups * step
    spec = pl.BlockSpec((tokens, tile), lambda i: (0, i))
    return call(
        functools.partial(project_kernel, blocks),
        (*pieces, weight, causal),
        after,
        grid=(groups // step,),
        in_specs=[pl.BlockSpec((rows, depth), lambda i: (0, 0))] * blocks
        + [
            pl.BlockSpec((depth, tile), lambda i: (0, i)),
            pl.BlockSpec((step, taps, 2 * taps), lambda i: (i, 0, 0)),
        ],
        out_specs=[pl.BlockSpec((tokens, depth), lambda i: (0, 0)), spec, spec],
        out_shape=[shape((tokens, depth), bf16)] + [shape((tokens, width), bf16)] * 2,
        name="project",
    )


def back_kernel(blocks, *refs):
    count = 2 * blocks - 1
    mix_refs = refs[:count]
    part_ref, weight_ref, ahead_ref, grad_ref, taps_ref = refs[count : count + 5]
    back_refs = refs[count + 5 : count + 5 + blocks]
    mix_ref, total = refs[count + 5 + blocks :]
    groups, taps, _ = ahead_ref.shape
    tokens = mix_ref.shape[0]
    rows = tokens // blocks
    width = mix_ref.shape[1] // groups
    mine = lax.axis_index("tensor")
    mix_ref[window(mine, rows), :] = mix_refs[0][...]
    for s in range(1, blocks):

        @pl.when(mine >= s)
        def _():
            mix_ref[window(mine - s, rows), :] = mix_refs[s][...]

        @pl.when(mine < s)
        def _():
            mix_ref[window(mine + (blocks - s), rows), :] = mix_refs[2 * blocks - 1 - s][...]

    row = lax.broadcasted_iota(jnp.int32, (taps, taps), 0)
    col = lax.broadcasted_iota(jnp.int32, (taps, taps), 1)
    starts = range(0, tokens, taps)
    for g in range(groups):
        cols = slice(g * width, (g + 1) * width)
        mix = mix_ref[:, cols]
        part = part_ref[:, cols]
        for start in starts:
            if start + taps == tokens:
                out = dot(ahead_ref[g, :, :taps], mix[start:])
            else:
                out = dot(ahead_ref[g], mix[start : start + 2 * taps])
            grad_ref[start : start + taps, cols] = out.astype(bf16)
        mixes = jnp.concatenate([mix[s : s + taps] for s in starts], axis=1)
        parts = jnp.concatenate([part[s : s + taps] for s in starts], axis=1)
        same = dot(parts, mixes, ((1,), (1,)))
        later = dot(parts[:, :-width], mixes[:, width:], ((1,), (1,)))
        pairs = jnp.where(col >= row, same, later)
        folded = pairs[0:8]
        for a in range(8, taps, 8):
            folded = folded + pltpu.roll(pairs[a : a + 8], taps - a, 1)
        line = folded[0:1]
        for b in range(1, 8):
            line = line + pltpu.roll(folded[b : b + 1], taps - b, 1)
        taps_ref[0, g : g + 1, :] = line
    product = dot(grad_ref[...], weight_ref[...], ((1,), (1,)))
    step = pl.program_id(0)

    @pl.when(step == 0)
    def _():
        total[...] = product

    @pl.when(step > 0)
    def _():
        total[...] += product

    @pl.when(step == pl.num_programs(0) - 1)
    def _():
        for s, back_ref in enumerate(back_refs):
            back_ref[...] = total[window(place(s), rows), :].astype(bf16)


def back(mixes, part, weight, ahead, after=()):
    blocks = (len(mixes) + 1) // 2
    rows = mixes[0].shape[0]
    tokens, width = part.shape
    depth = weight.shape[0]
    groups, taps, _ = ahead.shape
    step = 4
    tile = width // groups * step
    spec = pl.BlockSpec((tokens, tile), lambda i: (0, i))
    grads, line, *returned = call(
        functools.partial(back_kernel, blocks),
        (*mixes, part, weight, ahead),
        after,
        grid=(groups // step,),
        in_specs=[pl.BlockSpec((rows, tile), lambda i: (0, i))] * len(mixes)
        + [
            spec,
            pl.BlockSpec((depth, tile), lambda i: (0, i)),
            pl.BlockSpec((step, taps, 2 * taps), lambda i: (i, 0, 0)),
        ],
        out_specs=[spec, pl.BlockSpec((1, step, taps), lambda i: (i, 0, 0))]
        + [pl.BlockSpec((rows, depth), lambda i: (0, 0))] * blocks,
        out_shape=[
            shape((tokens, width), bf16),
            shape((groups // step, step, taps), f32),
        ]
        + [shape((rows, depth), bf16)] * blocks,
        scratch_shapes=[pltpu.VMEM((tokens, tile), bf16), pltpu.VMEM((tokens, depth), f32)],
        name="back",
    )
    return grads, line, returned


def weight_kernel(down_x, up_x, down_g, up_g, out_ref, down_t, up_t):
    @pl.when(pl.program_id(0) == 0)
    def _():
        down_t[...] = down_x[...].T
        up_t[...] = up_x[...].T

    out_ref[...] = (dot(down_t[...], down_g[...]) + dot(up_t[...], up_g[...])).astype(bf16)


def weight_gradient(down_x, up_x, down_g, up_g, after=()):
    tokens, depth = down_x.shape
    width = down_g.shape[1]
    tile = width // 8
    whole = pl.BlockSpec((tokens, depth), lambda i: (0, 0))
    part = pl.BlockSpec((tokens, tile), lambda i: (0, i))
    return call(
        weight_kernel,
        (down_x, up_x, down_g, up_g),
        after,
        grid=(width // tile,),
        in_specs=[whole, whole, part, part],
        out_specs=pl.BlockSpec((depth, tile), lambda i: (0, i)),
        out_shape=shape((depth, width), bf16),
        scratch_shapes=[pltpu.VMEM((depth, tokens), bf16)] * 2,
        name="weight_gradient",
    )


def finish_kernel(xin_ref, cot_ref, mixed_ref, *rest):
    *back_refs, out_ref, returned_ref = rest
    for s, back_ref in enumerate(back_refs):
        returned_ref[:, window(place(-s), back_ref.shape[1])] = back_ref[...]
    normed, inverse = normalise(xin_ref[...].astype(f32))
    cot = cot_ref[...].astype(f32)
    total = cot * mixed_ref[...].astype(f32) + returned_ref[...].astype(f32)
    mean = jnp.mean(total * normed, axis=1, keepdims=True)
    out_ref[0] = (cot + inverse * (total - normed * mean)).astype(bf16)


def finish(xin, cot, mixed, returned, after=()):
    rows, width = xin.shape
    step = 32
    spec = pl.BlockSpec((step, width), lambda i: (i, 0))
    piece = pl.BlockSpec((step, returned[0].shape[1]), lambda i: (i, 0))
    return call(
        finish_kernel,
        (xin, cot, mixed, *returned),
        after,
        grid=(rows // step,),
        in_specs=[spec, spec, spec] + [piece] * len(returned),
        out_specs=pl.BlockSpec((1, step, width), lambda i: (0, i, 0)),
        out_shape=shape((1, rows, width), bf16),
        scratch_shapes=[pltpu.VMEM((step, width), bf16)],
        name="finish",
    )


def exchange(pieces):
    blocks = len(pieces)
    out = [pieces[0]]
    for s in range(1, blocks):
        pairs = [(i, (i + s) % blocks) for i in range(blocks)]
        out.append(lax.ppermute(pieces[s], "tensor", pairs))
    return out


def gather(x):
    blocks = lax.axis_size("tensor")
    onward, backward = [], []
    right = left = x
    for s in range(1, blocks):
        right = lax.ppermute(right, "tensor", [(i, i + 1) for i in range(s - 1, blocks - 1)])
        left = lax.ppermute(left, "tensor", [(i + 1, i) for i in range(0, blocks - s)])
        onward.append(right)
        backward.append(left)
    return [x] + onward + backward


def scatter_sum(x):
    return lax.psum_scatter(x, "tensor", scatter_dimension=0, tiled=True)


def per_device(weights, filters, down_input, down_cot, up_input, up_cot):
    sections = lax.axis_size("section")
    mirror = [(s, sections - 1 - s) for s in range(sections)]
    down_pairs = [(s + 1, s) for s in range(sections - 1)]
    up_pairs = [(sections - s, s) for s in range(1, sections)]
    weight = weights[0]
    down_xin, down_cot = down_input[0], down_cot[0]
    up_xin = lax.ppermute(up_input[0], "section", mirror)
    down_pieces = exchange(normed_pieces(down_xin))
    causal, ahead = toeplitz(filters[0])
    up_pieces = normed_pieces(up_xin)
    down_x, down_part, down_mixed = project(down_pieces, weight, causal, after=up_pieces[:1])
    down_conv = scatter_sum(down_mixed)
    up_pieces = exchange(up_pieces)
    down_mixes = gather(grad_mix(down_xin, down_cot))
    up_cot = lax.ppermute(up_cot[0], "section", mirror)
    up_mix = grad_mix(up_xin, up_cot, after=(down_part,))
    up_x, up_part, up_mixed = project(
        up_pieces, weight, causal, after=(up_mix, down_mixes[1], down_mixes[-3])
    )
    up_conv = scatter_sum(up_mixed)
    up_mixes = gather(up_mix)
    down_g, down_taps, down_back = back(
        down_mixes, down_part, weight, ahead, after=(up_part, up_mixes[1], up_mixes[-3])
    )
    down_back = exchange(down_back)
    up_g, up_taps, up_back = back(up_mixes, up_part, weight, ahead, after=(down_g,))
    up_back = exchange(up_back)
    weight_grad = weight_gradient(down_x, up_x, down_g, up_g)
    taps = (down_taps + up_taps).reshape(filters.shape)
    taps = sum(exchange([taps] * lax.axis_size("tensor")))
    down_grad = finish(down_xin, down_cot, down_conv, down_back)
    down_passed = lax.ppermute(down_grad, "section", down_pairs)
    up_grad = finish(up_xin, up_cot, up_conv, up_back, after=(weight_grad, taps))
    up_passed = lax.ppermute(up_grad, "section", up_pairs)
    return weight_grad[None], taps, down_passed, up_passed


def solution(mesh):
    rows = P("section", "tensor", None)
    whole = P("section", None, None)
    return jax.shard_map(
        per_device,
        mesh=mesh,
        in_specs=(rows, whole, rows, rows, rows, rows),
        out_specs=(rows, whole, rows, rows),
        check_vma=False,
    )
```

```python
import functools

import jax
import jax.numpy as jnp
from jax import lax
from jax.experimental import pallas as pl
from jax.experimental.pallas import tpu as pltpu
from jax.sharding import PartitionSpec as P

epsilon = 1e-06
params = functools.partial(pltpu.CompilerParams, vmem_limit_bytes=63 * 1024 * 1024)
f32, bf16 = jnp.float32, jnp.bfloat16


def dot(a, b, dims=((1,), (0,))):
    return lax.dot_general(a, b, (dims, ((), ())), preferred_element_type=f32)


def shape(dims, dtype):
    return jax.ShapeDtypeStruct(dims, dtype)


def call(kernel, args, after, in_specs, **options):
    count = len(args)

    def body(*refs):
        kernel(*refs[:count], *refs[count + len(after) :])

    unread = [pl.BlockSpec(memory_space=pl.ANY)] * len(after)
    return pl.pallas_call(
        body, in_specs=list(in_specs) + unread, compiler_params=params(), **options
    )(*args, *after)


def toeplitz_kernel(filters_ref, causal_ref, ahead_ref):
    taps = filters_ref.shape[1]
    row = lax.broadcasted_iota(jnp.int32, (taps, taps), 0)
    col = lax.broadcasted_iota(jnp.int32, (taps, taps), 1)
    for g in range(filters_ref.shape[0]):
        line = jnp.broadcast_to(filters_ref[g : g + 1, :], (taps, taps))
        turned = pltpu.roll(line, 0, 1, stride=1, stride_axis=0)
        own = jnp.where(col >= row, turned, 0.0)
        beyond = jnp.where(col < row, turned, 0.0)
        ahead_ref[g, :, :taps] = own.astype(bf16)
        ahead_ref[g, :, taps:] = beyond.astype(bf16)
        causal_ref[g, :, :taps] = beyond.T.astype(bf16)
        causal_ref[g, :, taps:] = own.T.astype(bf16)


def toeplitz(filters):
    groups, taps = filters.shape
    step = 8
    out = shape((groups, taps, 2 * taps), bf16)
    spec = pl.BlockSpec((step, taps, 2 * taps), lambda i: (i, 0, 0))
    return call(
        toeplitz_kernel,
        (filters,),
        (),
        grid=(groups // step,),
        in_specs=[pl.BlockSpec((step, taps), lambda i: (i, 0))],
        out_specs=[spec, spec],
        out_shape=[out, out],
        name="toeplitz",
    )


def place(by):
    blocks = lax.axis_size("tensor")
    return lax.rem(lax.axis_index("tensor") + (by + blocks), blocks)


def window(index, size):
    return pl.ds(pl.multiple_of(index * size, size), size)


def normalise(wide):
    inverse = lax.rsqrt(jnp.mean(wide * wide, axis=1, keepdims=True) + epsilon)
    return wide * inverse, inverse


def normed_kernel(xin_ref, normed_ref):
    normed = normalise(xin_ref[...].astype(f32))[0].astype(bf16)
    width = normed_ref.shape[2]
    for i in range(normed_ref.shape[0]):
        normed_ref[i] = normed[:, i * width : (i + 1) * width]


def normed_blocks(xin, after=()):
    rows, width = xin.shape
    blocks = lax.axis_size("tensor")
    step = 32
    return call(
        normed_kernel,
        (xin,),
        after,
        grid=(rows // step,),
        in_specs=[pl.BlockSpec((step, width), lambda i: (i, 0))],
        out_specs=pl.BlockSpec((blocks, step, width // blocks), lambda i: (0, i, 0)),
        out_shape=shape((blocks, rows, width // blocks), bf16),
        name="normed_blocks",
    )


def mix_kernel(xin_ref, cot_ref, mix_ref):
    normed, _ = normalise(xin_ref[...].astype(f32))
    mix_ref[...] = (cot_ref[...].astype(f32) * normed).astype(bf16)


def grad_mix(xin, cot, after=()):
    rows, width = xin.shape
    step = 32
    spec = pl.BlockSpec((step, width), lambda i: (i, 0))
    return call(
        mix_kernel,
        (xin, cot),
        after,
        grid=(rows // step,),
        in_specs=[spec, spec],
        out_specs=spec,
        out_shape=shape((rows, width), bf16),
        name="grad_mix",
    )


def project_kernel(features_ref, weight_ref, causal_ref, part_ref, *rest):
    *mixed_refs, mixed_ref = rest
    groups, taps, _ = causal_ref.shape
    part = dot(features_ref[...], weight_ref[...]).astype(bf16)
    part_ref[...] = part
    width = part.shape[1] // groups
    for g in range(groups):
        cols = slice(g * width, (g + 1) * width)
        for start in range(0, part.shape[0], taps):
            if start == 0:
                out = dot(causal_ref[g, :, taps:], part[:taps, cols])
            else:
                out = dot(causal_ref[g], part[start - taps : start + taps, cols])
            mixed_ref[start : start + taps, cols] = out.astype(bf16)
    for s, out_ref in enumerate(mixed_refs):
        out_ref[...] = mixed_ref[window(place(s), out_ref.shape[0]), :]


def project(features, weight, causal, after=()):
    blocks = lax.axis_size("tensor")
    tokens, depth = features.shape
    rows = tokens // blocks
    width = weight.shape[1]
    groups, taps, _ = causal.shape
    step = 4
    tile = width // groups * step
    part, *mixed = call(
        project_kernel,
        (features, weight, causal),
        after,
        grid=(groups // step,),
        in_specs=[
            pl.BlockSpec((tokens, depth), lambda i: (0, 0)),
            pl.BlockSpec((depth, tile), lambda i: (0, i)),
            pl.BlockSpec((step, taps, 2 * taps), lambda i: (i, 0, 0)),
        ],
        out_specs=[pl.BlockSpec((tokens, tile), lambda i: (0, i))]
        + [pl.BlockSpec((rows, tile), lambda i: (0, i))] * blocks,
        out_shape=[shape((tokens, width), bf16)] + [shape((rows, width), bf16)] * blocks,
        scratch_shapes=[pltpu.VMEM((tokens, tile), bf16)],
        name="project",
    )
    return part, mixed


def back_kernel(blocks, *refs):
    count = 2 * blocks - 1
    mix_refs = refs[:count]
    part_ref, weight_ref, ahead_ref, grad_ref, taps_ref, back_ref, mix_ref, total = refs[count:]
    groups, taps, _ = ahead_ref.shape
    tokens = mix_ref.shape[0]
    rows = tokens // blocks
    width = mix_ref.shape[1] // groups
    mine = lax.axis_index("tensor")
    mix_ref[window(mine, rows), :] = mix_refs[0][...]
    for s in range(1, blocks):

        @pl.when(mine >= s)
        def _():
            mix_ref[window(mine - s, rows), :] = mix_refs[s][...]

        @pl.when(mine < s)
        def _():
            mix_ref[window(mine + (blocks - s), rows), :] = mix_refs[2 * blocks - 1 - s][...]

    row = lax.broadcasted_iota(jnp.int32, (taps, taps), 0)
    col = lax.broadcasted_iota(jnp.int32, (taps, taps), 1)
    starts = range(0, tokens, taps)
    for g in range(groups):
        cols = slice(g * width, (g + 1) * width)
        mix = mix_ref[:, cols]
        part = part_ref[:, cols]
        for start in starts:
            if start + taps == tokens:
                out = dot(ahead_ref[g, :, :taps], mix[start:])
            else:
                out = dot(ahead_ref[g], mix[start : start + 2 * taps])
            grad_ref[start : start + taps, cols] = out.astype(bf16)
        mixes = jnp.concatenate([mix[s : s + taps] for s in starts], axis=1)
        parts = jnp.concatenate([part[s : s + taps] for s in starts], axis=1)
        same = dot(parts, mixes, ((1,), (1,)))
        later = dot(parts[:, :-width], mixes[:, width:], ((1,), (1,)))
        pairs = jnp.where(col >= row, same, later)
        folded = pairs[0:8]
        for a in range(8, taps, 8):
            folded = folded + pltpu.roll(pairs[a : a + 8], taps - a, 1)
        line = folded[0:1]
        for b in range(1, 8):
            line = line + pltpu.roll(folded[b : b + 1], taps - b, 1)
        taps_ref[0, g : g + 1, :] = line
    product = dot(grad_ref[...], weight_ref[...], ((1,), (1,)))
    step = pl.program_id(0)

    @pl.when(step == 0)
    def _():
        total[...] = product

    @pl.when(step > 0)
    def _():
        total[...] += product

    @pl.when(step == pl.num_programs(0) - 1)
    def _():
        back_ref[...] = total[...].astype(bf16)


def back(mixes, part, weight, ahead, after=()):
    blocks = (len(mixes) + 1) // 2
    rows = mixes[0].shape[0]
    tokens, width = part.shape
    depth = weight.shape[0]
    groups, taps, _ = ahead.shape
    step = 4
    tile = width // groups * step
    spec = pl.BlockSpec((tokens, tile), lambda i: (0, i))
    return call(
        functools.partial(back_kernel, blocks),
        (*mixes, part, weight, ahead),
        after,
        grid=(groups // step,),
        in_specs=[pl.BlockSpec((rows, tile), lambda i: (0, i))] * len(mixes)
        + [
            spec,
            pl.BlockSpec((depth, tile), lambda i: (0, i)),
            pl.BlockSpec((step, taps, 2 * taps), lambda i: (i, 0, 0)),
        ],
        out_specs=[
            spec,
            pl.BlockSpec((1, step, taps), lambda i: (i, 0, 0)),
            pl.BlockSpec((tokens, depth), lambda i: (0, 0)),
        ],
        out_shape=[
            shape((tokens, width), bf16),
            shape((groups // step, step, taps), f32),
            shape((tokens, depth), bf16),
        ],
        scratch_shapes=[pltpu.VMEM((tokens, tile), bf16), pltpu.VMEM((tokens, depth), f32)],
        name="back",
    )


def weight_kernel(down_x, up_x, down_g, up_g, out_ref, down_t, up_t):
    @pl.when(pl.program_id(0) == 0)
    def _():
        down_t[...] = down_x[...].T
        up_t[...] = up_x[...].T

    out_ref[...] = (dot(down_t[...], down_g[...]) + dot(up_t[...], up_g[...])).astype(bf16)


def weight_gradient(down_x, up_x, down_g, up_g, after=()):
    tokens, depth = down_x.shape
    width = down_g.shape[1]
    tile = width // 8
    whole = pl.BlockSpec((tokens, depth), lambda i: (0, 0))
    part = pl.BlockSpec((tokens, tile), lambda i: (0, i))
    return call(
        weight_kernel,
        (down_x, up_x, down_g, up_g),
        after,
        grid=(width // tile,),
        in_specs=[whole, whole, part, part],
        out_specs=pl.BlockSpec((depth, tile), lambda i: (0, i)),
        out_shape=shape((depth, width), bf16),
        scratch_shapes=[pltpu.VMEM((depth, tokens), bf16)] * 2,
        name="weight_gradient",
    )


def finish_kernel(xin_ref, cot_ref, back_ref, *rest):
    *mixed_refs, out_ref = rest
    normed, inverse = normalise(xin_ref[...].astype(f32))
    cot = cot_ref[...].astype(f32)
    returned = jnp.concatenate([back_ref[i] for i in range(back_ref.shape[0])], axis=1)
    mixed = sum(ref[...].astype(f32) for ref in mixed_refs)
    total = cot * mixed + returned.astype(f32)
    mean = jnp.mean(total * normed, axis=1, keepdims=True)
    out_ref[0] = (cot + inverse * (total - normed * mean)).astype(bf16)


def finish(xin, cot, mixed, returned, after=()):
    rows, width = xin.shape
    blocks, _, depth = returned.shape
    step = 32
    spec = pl.BlockSpec((step, width), lambda i: (i, 0))
    return call(
        finish_kernel,
        (xin, cot, returned, *mixed),
        after,
        grid=(rows // step,),
        in_specs=[spec, spec, pl.BlockSpec((blocks, step, depth), lambda i: (0, i, 0))]
        + [spec] * len(mixed),
        out_specs=pl.BlockSpec((1, step, width), lambda i: (0, i, 0)),
        out_shape=shape((1, rows, width), bf16),
        name="finish",
    )


def exchange(x):
    blocks = lax.axis_size("tensor")
    x = x.reshape(blocks, -1, x.shape[-1])
    return lax.all_to_all(x, "tensor", split_axis=0, concat_axis=0, tiled=True)


def both_ways(right, left):
    blocks = lax.axis_size("tensor")
    onward = [(i, i + 1) for i in range(blocks - 1)]
    return (
        lax.ppermute(right, "tensor", onward),
        lax.ppermute(left, "tensor", [(j, i) for i, j in onward]),
    )


def payload_kernel(s, right_ref, left_ref, right_piece, left_piece, right_out, left_out):
    mine = lax.axis_index("tensor")
    blocks = lax.axis_size("tensor")

    def put(came, piece, out, adds):
        @pl.when(adds)
        def _():
            out[...] = (came[...].astype(f32) + piece[...].astype(f32)).astype(bf16)

        @pl.when(jnp.logical_not(adds))
        def _():
            out[...] = came[...]

    put(right_ref, right_piece, right_out, mine < s - 1)
    put(left_ref, left_piece, left_out, mine > blocks - s)


def payload(s, arrived, pieces, after=()):
    blocks = len(pieces)
    rows, width = pieces[0].shape
    step = 32
    spec = pl.BlockSpec((step, width), lambda i: (i, 0))
    return call(
        functools.partial(payload_kernel, s),
        (*arrived, pieces[blocks + 1 - s], pieces[s - 1]),
        after,
        grid=(rows // step,),
        in_specs=[spec] * 4,
        out_specs=[spec] * 2,
        out_shape=[shape((rows, width), bf16)] * 2,
        name="payload",
    )


def sort_arrivals(mix, pieces, arrivals):
    rights, lefts = zip(*arrivals)
    return [mix, *rights[:-1], *lefts[:-1]], [pieces[0], rights[-1], lefts[-1]]


def per_device(weights, filters, down_input, down_cot, up_input, up_cot):
    sections = lax.axis_size("section")
    mirror = [(s, sections - 1 - s) for s in range(sections)]
    down_pairs = [(s + 1, s) for s in range(sections - 1)]
    up_pairs = [(sections - s, s) for s in range(1, sections)]
    weight = weights[0]
    down_xin, down_cot = down_input[0], down_cot[0]
    up_xin = lax.ppermute(up_input[0], "section", mirror)
    up_cot = lax.ppermute(up_cot[0], "section", mirror)
    blocks = lax.axis_size("tensor")
    depth = weight.shape[0]
    down_x = exchange(normed_blocks(down_xin)).reshape(-1, depth)
    down_mix = grad_mix(down_xin, down_cot)
    down_arrivals = [both_ways(down_mix, down_mix)]
    causal, ahead = toeplitz(filters[0])
    up_normed = normed_blocks(up_xin)
    up_x = exchange(up_normed).reshape(-1, depth)
    up_mix = grad_mix(up_xin, up_cot, after=down_arrivals[0])
    up_arrivals = [both_ways(up_mix, up_mix)]
    down_part, down_pieces = project(down_x, weight, causal, after=(up_normed, up_mix))
    last = down_part
    for s in range(2, blocks + 1):
        sent = payload(s, down_arrivals[-1], down_pieces, after=(last,))
        down_arrivals.append(both_ways(*sent))
        if s == 2:
            up_part, up_pieces = project(up_x, weight, causal, after=sent)
        if s == blocks:
            down_mixes, down_conv = sort_arrivals(down_mix, down_pieces, down_arrivals)
            down_g, down_taps, down_back = back(down_mixes, down_part, weight, ahead, after=sent)
            sent = (down_g,)
            down_back = exchange(down_back)
        sent = payload(s, up_arrivals[-1], up_pieces, after=sent[:1])
        up_arrivals.append(both_ways(*sent))
        last = sent[0]
    up_mixes, up_conv = sort_arrivals(up_mix, up_pieces, up_arrivals)
    up_g, up_taps, up_back = back(up_mixes, up_part, weight, ahead, after=(last,))
    up_back = exchange(up_back)
    weight_grad = weight_gradient(down_x, up_x, down_g, up_g)
    taps = (down_taps + up_taps).reshape(filters.shape)
    taps = jnp.sum(lax.all_gather(taps, "tensor", axis=0, tiled=True), axis=0, keepdims=True)
    down_grad = finish(down_xin, down_cot, down_conv, down_back, after=(up_g,))
    down_passed = lax.ppermute(down_grad, "section", down_pairs)
    up_grad = finish(up_xin, up_cot, up_conv, up_back, after=(weight_grad, taps))
    up_passed = lax.ppermute(up_grad, "section", up_pairs)
    return weight_grad[None], taps, down_passed, up_passed


def solution(mesh):
    rows = P("section", "tensor", None)
    whole = P("section", None, None)
    return jax.shard_map(
        per_device,
        mesh=mesh,
        in_specs=(rows, whole, rows, rows, rows, rows),
        out_specs=(rows, whole, rows, rows),
        check_vma=False,
    )
```

```python
import functools

import jax
import jax.numpy as jnp
from jax import lax
from jax.experimental import pallas as pl
from jax.experimental.pallas import tpu as pltpu
from jax.sharding import PartitionSpec as P

epsilon = 1e-06
params = functools.partial(pltpu.CompilerParams, vmem_limit_bytes=63 * 1024 * 1024)
f32, bf16 = jnp.float32, jnp.bfloat16


def dot(a, b, dims=((1,), (0,))):
    return lax.dot_general(a, b, (dims, ((), ())), preferred_element_type=f32)


def shape(dims, dtype):
    return jax.ShapeDtypeStruct(dims, dtype)


def call(kernel, args, after, in_specs, out_shape, flops=0, **options):
    count = len(args)
    arrays = [*args, *(out_shape if isinstance(out_shape, list) else [out_shape])]
    cost = pl.CostEstimate(
        flops=flops,
        transcendentals=0,
        bytes_accessed=sum(x.size * x.dtype.itemsize for x in arrays),
    )

    def body(*refs):
        kernel(*refs[:count], *refs[count + len(after) :])

    unread = [pl.BlockSpec(memory_space=pl.ANY)] * len(after)
    return pl.pallas_call(
        body,
        in_specs=list(in_specs) + unread,
        out_shape=out_shape,
        cost_estimate=cost,
        compiler_params=params(),
        **options,
    )(*args, *after)


def toeplitz_kernel(filters_ref, causal_ref, ahead_ref):
    taps = filters_ref.shape[1]
    row = lax.broadcasted_iota(jnp.int32, (taps, taps), 0)
    col = lax.broadcasted_iota(jnp.int32, (taps, taps), 1)
    for g in range(filters_ref.shape[0]):
        line = jnp.broadcast_to(filters_ref[g : g + 1, :], (taps, taps))
        turned = pltpu.roll(line, 0, 1, stride=1, stride_axis=0)
        own = jnp.where(col >= row, turned, 0.0)
        beyond = jnp.where(col < row, turned, 0.0)
        ahead_ref[g, :, :taps] = own.astype(bf16)
        ahead_ref[g, :, taps:] = beyond.astype(bf16)
        causal_ref[g, :, :taps] = beyond.T.astype(bf16)
        causal_ref[g, :, taps:] = own.T.astype(bf16)


def toeplitz(filters):
    groups, taps = filters.shape
    step = 8
    out = shape((groups, taps, 2 * taps), bf16)
    spec = pl.BlockSpec((step, taps, 2 * taps), lambda i: (i, 0, 0))
    return call(
        toeplitz_kernel,
        (filters,),
        (),
        grid=(groups // step,),
        in_specs=[pl.BlockSpec((step, taps), lambda i: (i, 0))],
        out_specs=[spec, spec],
        out_shape=[out, out],
        name="toeplitz",
    )


def place(by):
    blocks = lax.axis_size("tensor")
    return lax.rem(lax.axis_index("tensor") + (by + blocks), blocks)


def window(index, size):
    return pl.ds(pl.multiple_of(index * size, size), size)


def normalise(wide):
    inverse = lax.rsqrt(jnp.mean(wide * wide, axis=1, keepdims=True) + epsilon)
    return wide * inverse, inverse


def prepare_kernel(xin_ref, *refs):
    *cot_ref, normed_ref = refs[: len(refs) // 2 + 1]
    normed, _ = normalise(xin_ref[...].astype(f32))
    width = normed_ref.shape[2]
    for i in range(normed_ref.shape[0]):
        normed_ref[i] = normed[:, i * width : (i + 1) * width].astype(bf16)
    if cot_ref:
        refs[-1][...] = (cot_ref[0][...].astype(f32) * normed).astype(bf16)


def prepare(*args):
    rows, width = args[0].shape
    blocks = lax.axis_size("tensor")
    step = 32
    spec = pl.BlockSpec((step, width), lambda i: (i, 0))
    normed_spec = pl.BlockSpec((blocks, step, width // blocks), lambda i: (0, i, 0))
    extra = len(args) - 1
    return call(
        prepare_kernel,
        args,
        (),
        grid=(rows // step,),
        in_specs=[spec] * len(args),
        out_specs=[normed_spec] + [spec] * extra,
        out_shape=[shape((blocks, rows, width // blocks), bf16)] + [shape((rows, width), bf16)] * extra,
        name="prepare",
    )


def mix_kernel(xin_ref, cot_ref, mix_ref):
    normed, _ = normalise(xin_ref[...].astype(f32))
    mix_ref[...] = (cot_ref[...].astype(f32) * normed).astype(bf16)


def grad_mix(xin, cot, after=()):
    rows, width = xin.shape
    step = 32
    spec = pl.BlockSpec((step, width), lambda i: (i, 0))
    return call(
        mix_kernel,
        (xin, cot),
        after,
        grid=(rows // step,),
        in_specs=[spec, spec],
        out_specs=spec,
        out_shape=shape((rows, width), bf16),
        name="grad_mix",
    )


def project_kernel(features_ref, weight_ref, causal_ref, part_ref, *rest):
    *mixed_refs, mixed_ref = rest
    groups, taps, _ = causal_ref.shape
    part = dot(features_ref[...], weight_ref[...]).astype(bf16)
    part_ref[...] = part
    width = part.shape[1] // groups
    for g in range(groups):
        cols = slice(g * width, (g + 1) * width)
        for start in range(0, part.shape[0], taps):
            if start == 0:
                out = dot(causal_ref[g, :, taps:], part[:taps, cols])
            else:
                out = dot(causal_ref[g], part[start - taps : start + taps, cols])
            mixed_ref[start : start + taps, cols] = out.astype(bf16)
    for s, out_ref in enumerate(mixed_refs):
        out_ref[...] = mixed_ref[window(place(s), out_ref.shape[0]), :]


def project(features, weight, causal, after=()):
    blocks = lax.axis_size("tensor")
    tokens, depth = features.shape
    rows = tokens // blocks
    width = weight.shape[1]
    groups, taps, _ = causal.shape
    step = 4
    tile = width // groups * step
    part, *mixed = call(
        project_kernel,
        (features, weight, causal),
        after,
        grid=(groups // step,),
        in_specs=[
            pl.BlockSpec((tokens, depth), lambda i: (0, 0)),
            pl.BlockSpec((depth, tile), lambda i: (0, i)),
            pl.BlockSpec((step, taps, 2 * taps), lambda i: (i, 0, 0)),
        ],
        out_specs=[pl.BlockSpec((tokens, tile), lambda i: (0, i))]
        + [pl.BlockSpec((rows, tile), lambda i: (0, i))] * blocks,
        out_shape=[shape((tokens, width), bf16)] + [shape((rows, width), bf16)] * blocks,
        scratch_shapes=[pltpu.VMEM((tokens, tile), bf16)],
        flops=2 * tokens * width * (depth + 2 * taps),
        name="project",
    )
    return part, mixed


def back_kernel(blocks, *refs):
    count = 2 * blocks - 1
    mix_refs = refs[:count]
    part_ref, weight_ref, ahead_ref, grad_ref, taps_ref, back_ref, mix_ref, total = refs[count:]
    groups, taps, _ = ahead_ref.shape
    tokens = mix_ref.shape[0]
    rows = tokens // blocks
    width = mix_ref.shape[1] // groups
    mine = lax.axis_index("tensor")
    mix_ref[window(mine, rows), :] = mix_refs[0][...]
    for s in range(1, blocks):

        @pl.when(mine >= s)
        def _():
            mix_ref[window(mine - s, rows), :] = mix_refs[s][...]

        @pl.when(mine < s)
        def _():
            mix_ref[window(mine + (blocks - s), rows), :] = mix_refs[2 * blocks - 1 - s][...]

    row = lax.broadcasted_iota(jnp.int32, (taps, taps), 0)
    col = lax.broadcasted_iota(jnp.int32, (taps, taps), 1)
    starts = range(0, tokens, taps)
    for g in range(groups):
        cols = slice(g * width, (g + 1) * width)
        mix = mix_ref[:, cols]
        part = part_ref[:, cols]
        for start in starts:
            if start + taps == tokens:
                out = dot(ahead_ref[g, :, :taps], mix[start:])
            else:
                out = dot(ahead_ref[g], mix[start : start + 2 * taps])
            grad_ref[start : start + taps, cols] = out.astype(bf16)
        mixes = jnp.concatenate([mix[s : s + taps] for s in starts], axis=1)
        parts = jnp.concatenate([part[s : s + taps] for s in starts], axis=1)
        same = dot(parts, mixes, ((1,), (1,)))
        later = dot(parts[:, :-width], mixes[:, width:], ((1,), (1,)))
        pairs = jnp.where(col >= row, same, later)
        folded = pairs[0:8]
        for a in range(8, taps, 8):
            folded = folded + pltpu.roll(pairs[a : a + 8], taps - a, 1)
        line = folded[0:1]
        for b in range(1, 8):
            line = line + pltpu.roll(folded[b : b + 1], taps - b, 1)
        taps_ref[0, g : g + 1, :] = line
    product = dot(grad_ref[...], weight_ref[...], ((1,), (1,)))
    step = pl.program_id(0)

    @pl.when(step == 0)
    def _():
        total[...] = product

    @pl.when(step > 0)
    def _():
        total[...] += product

    @pl.when(step == pl.num_programs(0) - 1)
    def _():
        back_ref[...] = total[...].astype(bf16)


def back(mixes, part, weight, ahead, after=()):
    blocks = (len(mixes) + 1) // 2
    rows = mixes[0].shape[0]
    tokens, width = part.shape
    depth = weight.shape[0]
    groups, taps, _ = ahead.shape
    step = 4
    tile = width // groups * step
    spec = pl.BlockSpec((tokens, tile), lambda i: (0, i))
    return call(
        functools.partial(back_kernel, blocks),
        (*mixes, part, weight, ahead),
        after,
        grid=(groups // step,),
        in_specs=[pl.BlockSpec((rows, tile), lambda i: (0, i))] * len(mixes)
        + [
            spec,
            pl.BlockSpec((depth, tile), lambda i: (0, i)),
            pl.BlockSpec((step, taps, 2 * taps), lambda i: (i, 0, 0)),
        ],
        out_specs=[
            spec,
            pl.BlockSpec((1, step, taps), lambda i: (i, 0, 0)),
            pl.BlockSpec((tokens, depth), lambda i: (0, 0)),
        ],
        out_shape=[
            shape((tokens, width), bf16),
            shape((groups // step, step, taps), f32),
            shape((tokens, depth), bf16),
        ],
        scratch_shapes=[pltpu.VMEM((tokens, tile), bf16), pltpu.VMEM((tokens, depth), f32)],
        flops=2 * tokens * width * (depth + 4 * taps),
        name="back",
    )


def weight_kernel(down_x, up_x, down_g, up_g, out_ref, down_t, up_t):
    @pl.when(pl.program_id(0) == 0)
    def _():
        down_t[...] = down_x[...].T
        up_t[...] = up_x[...].T

    out_ref[...] = (dot(down_t[...], down_g[...]) + dot(up_t[...], up_g[...])).astype(bf16)


def weight_gradient(down_x, up_x, down_g, up_g, after=()):
    tokens, depth = down_x.shape
    width = down_g.shape[1]
    tile = width // 8
    whole = pl.BlockSpec((tokens, depth), lambda i: (0, 0))
    part = pl.BlockSpec((tokens, tile), lambda i: (0, i))
    return call(
        weight_kernel,
        (down_x, up_x, down_g, up_g),
        after,
        grid=(width // tile,),
        in_specs=[whole, whole, part, part],
        out_specs=pl.BlockSpec((depth, tile), lambda i: (0, i)),
        out_shape=shape((depth, width), bf16),
        scratch_shapes=[pltpu.VMEM((depth, tokens), bf16)] * 2,
        flops=4 * tokens * depth * width,
        name="weight_gradient",
    )


def finish_kernel(xin_ref, cot_ref, back_ref, *rest):
    *mixed_refs, out_ref = rest
    normed, inverse = normalise(xin_ref[...].astype(f32))
    cot = cot_ref[...].astype(f32)
    returned = jnp.concatenate([back_ref[i] for i in range(back_ref.shape[0])], axis=1)
    mixed = sum(ref[...].astype(f32) for ref in mixed_refs)
    total = cot * mixed + returned.astype(f32)
    mean = jnp.mean(total * normed, axis=1, keepdims=True)
    out_ref[0] = (cot + inverse * (total - normed * mean)).astype(bf16)


def finish(xin, cot, mixed, returned, after=()):
    rows, width = xin.shape
    blocks, _, depth = returned.shape
    step = 32
    spec = pl.BlockSpec((step, width), lambda i: (i, 0))
    return call(
        finish_kernel,
        (xin, cot, returned, *mixed),
        after,
        grid=(rows // step,),
        in_specs=[spec, spec, pl.BlockSpec((blocks, step, depth), lambda i: (0, i, 0))]
        + [spec] * len(mixed),
        out_specs=pl.BlockSpec((1, step, width), lambda i: (0, i, 0)),
        out_shape=shape((1, rows, width), bf16),
        name="finish",
    )


def exchange(x):
    blocks = lax.axis_size("tensor")
    x = x.reshape(blocks, -1, x.shape[-1])
    return lax.all_to_all(x, "tensor", split_axis=0, concat_axis=0, tiled=True)


def both_ways(right, left):
    blocks = lax.axis_size("tensor")
    onward = [(i, i + 1) for i in range(blocks - 1)]
    return (
        lax.ppermute(right, "tensor", onward),
        lax.ppermute(left, "tensor", [(j, i) for i, j in onward]),
    )


def payload_kernel(s, right_ref, left_ref, right_piece, left_piece, right_out, left_out):
    mine = lax.axis_index("tensor")
    blocks = lax.axis_size("tensor")

    def put(came, piece, out, adds):
        @pl.when(adds)
        def _():
            out[...] = (came[...].astype(f32) + piece[...].astype(f32)).astype(bf16)

        @pl.when(jnp.logical_not(adds))
        def _():
            out[...] = came[...]

    put(right_ref, right_piece, right_out, mine < s - 1)
    put(left_ref, left_piece, left_out, mine > blocks - s)


def payload(s, arrived, pieces, after=()):
    blocks = len(pieces)
    rows, width = pieces[0].shape
    step = 32
    spec = pl.BlockSpec((step, width), lambda i: (i, 0))
    return call(
        functools.partial(payload_kernel, s),
        (*arrived, pieces[blocks + 1 - s], pieces[s - 1]),
        after,
        grid=(rows // step,),
        in_specs=[spec] * 4,
        out_specs=[spec] * 2,
        out_shape=[shape((rows, width), bf16)] * 2,
        name="payload",
    )


def sort_arrivals(mix, pieces, arrivals):
    rights, lefts = zip(*arrivals)
    return [mix, *rights[:-1], *lefts[:-1]], [pieces[0], rights[-1], lefts[-1]]


def sum_all(x):
    blocks = lax.axis_size("tensor")
    apart = 1
    while apart < blocks:
        x = x + lax.ppermute(x, "tensor", [(i, i ^ apart) for i in range(blocks)])
        apart *= 2
    return x


def per_device(weights, filters, down_input, down_cot, up_input, up_cot):
    sections = lax.axis_size("section")
    mirror = [(s, sections - 1 - s) for s in range(sections)]
    down_pairs = [(s + 1, s) for s in range(sections - 1)]
    up_pairs = [(sections - s, s) for s in range(1, sections)]
    weight = weights[0]
    down_xin, down_cot = down_input[0], down_cot[0]
    up_xin = lax.ppermute(up_input[0], "section", mirror)
    up_cot = lax.ppermute(up_cot[0], "section", mirror)
    blocks = lax.axis_size("tensor")
    depth = weight.shape[0]
    down_normed, down_mix = prepare(down_xin, down_cot)
    down_x = exchange(down_normed).reshape(-1, depth)
    down_arrivals = [both_ways(down_mix, down_mix)]
    causal, ahead = toeplitz(filters[0])
    (up_normed,) = prepare(up_xin)
    up_x = exchange(up_normed).reshape(-1, depth)
    up_mix = grad_mix(up_xin, up_cot, after=down_arrivals[0])
    up_arrivals = [both_ways(up_mix, up_mix)]
    down_part, down_pieces = project(down_x, weight, causal, after=(up_normed, up_mix))
    last = down_part
    for s in range(2, blocks + 1):
        sent = payload(s, down_arrivals[-1], down_pieces, after=(last,))
        down_arrivals.append(both_ways(*sent))
        if s == 2:
            up_part, up_pieces = project(up_x, weight, causal, after=sent)
        sent = payload(s, up_arrivals[-1], up_pieces, after=sent)
        up_arrivals.append(both_ways(*sent))
        last = sent[0]
    down_mixes, down_conv = sort_arrivals(down_mix, down_pieces, down_arrivals)
    up_mixes, up_conv = sort_arrivals(up_mix, up_pieces, up_arrivals)
    up_g, up_taps, up_back = back(up_mixes, up_part, weight, ahead, after=(last,))
    up_back = exchange(up_back)
    down_g, down_taps, down_back = back(
        down_mixes, down_part, weight, ahead, after=(up_g, *down_arrivals[-1])
    )
    down_back = exchange(down_back)
    up_grad = finish(up_xin, up_cot, up_conv, up_back, after=(down_g,))
    up_passed = lax.ppermute(up_grad, "section", up_pairs)
    weight_grad = weight_gradient(down_x, up_x, down_g, up_g)
    taps = sum_all((down_taps + up_taps).reshape(filters.shape))
    down_grad = finish(
        down_xin, down_cot, down_conv, down_back, after=(up_grad, weight_grad, taps)
    )
    down_passed = lax.ppermute(down_grad, "section", down_pairs)
    return weight_grad[None], taps, down_passed, up_passed


def solution(mesh):
    rows = P("section", "tensor", None)
    whole = P("section", None, None)
    return jax.shard_map(
        per_device,
        mesh=mesh,
        in_specs=(rows, whole, rows, rows, rows, rows),
        out_specs=(rows, whole, rows, rows),
        check_vma=False,
    )
```

```python
import functools

import jax
import jax.numpy as jnp
from jax import lax
from jax.experimental import pallas as pl
from jax.experimental.pallas import tpu as pltpu
from jax.sharding import PartitionSpec as P

epsilon = 1e-06
params = functools.partial(pltpu.CompilerParams, vmem_limit_bytes=63 * 1024 * 1024)
f32, bf16 = jnp.float32, jnp.bfloat16


def dot(a, b, dims=((1,), (0,))):
    return lax.dot_general(a, b, (dims, ((), ())), preferred_element_type=f32)


def shape(dims, dtype):
    return jax.ShapeDtypeStruct(dims, dtype)


def call(kernel, args, after, in_specs, out_shape, flops=0, **options):
    count = len(args)
    arrays = [*args, *(out_shape if isinstance(out_shape, list) else [out_shape])]
    cost = pl.CostEstimate(
        flops=flops,
        transcendentals=0,
        bytes_accessed=sum(x.size * x.dtype.itemsize for x in arrays),
    )

    def body(*refs):
        kernel(*refs[:count], *refs[count + len(after) :])

    unread = [pl.BlockSpec(memory_space=pl.ANY)] * len(after)
    return pl.pallas_call(
        body,
        in_specs=list(in_specs) + unread,
        out_shape=out_shape,
        cost_estimate=cost,
        compiler_params=params(),
        **options,
    )(*args, *after)


def toeplitz_kernel(filters_ref, causal_ref, ahead_ref):
    taps = filters_ref.shape[1]
    row = lax.broadcasted_iota(jnp.int32, (taps, taps), 0)
    col = lax.broadcasted_iota(jnp.int32, (taps, taps), 1)
    for g in range(filters_ref.shape[0]):
        line = jnp.broadcast_to(filters_ref[g : g + 1, :], (taps, taps))
        turned = pltpu.roll(line, 0, 1, stride=1, stride_axis=0)
        own = jnp.where(col >= row, turned, 0.0)
        beyond = jnp.where(col < row, turned, 0.0)
        ahead_ref[g, :, :taps] = own.astype(bf16)
        ahead_ref[g, :, taps:] = beyond.astype(bf16)
        causal_ref[g, :, :taps] = beyond.T.astype(bf16)
        causal_ref[g, :, taps:] = own.T.astype(bf16)


def toeplitz(filters):
    groups, taps = filters.shape
    step = 8
    out = shape((groups, taps, 2 * taps), bf16)
    spec = pl.BlockSpec((step, taps, 2 * taps), lambda i: (i, 0, 0))
    return call(
        toeplitz_kernel,
        (filters,),
        (),
        grid=(groups // step,),
        in_specs=[pl.BlockSpec((step, taps), lambda i: (i, 0))],
        out_specs=[spec, spec],
        out_shape=[out, out],
        name="toeplitz",
    )


def place(by):
    blocks = lax.axis_size("tensor")
    return lax.rem(lax.axis_index("tensor") + (by + blocks), blocks)


def window(index, size):
    return pl.ds(pl.multiple_of(index * size, size), size)


def normalise(wide):
    inverse = lax.rsqrt(jnp.mean(wide * wide, axis=1, keepdims=True) + epsilon)
    return wide * inverse, inverse


def prepare_kernel(xin_ref, *refs):
    *cot_ref, normed_ref = refs[: len(refs) // 2 + 1]
    normed, _ = normalise(xin_ref[...].astype(f32))
    width = normed_ref.shape[2]
    for i in range(normed_ref.shape[0]):
        normed_ref[i] = normed[:, i * width : (i + 1) * width].astype(bf16)
    if cot_ref:
        refs[-1][...] = (cot_ref[0][...].astype(f32) * normed).astype(bf16)


def prepare(*args):
    rows, width = args[0].shape
    blocks = lax.axis_size("tensor")
    step = 32
    spec = pl.BlockSpec((step, width), lambda i: (i, 0))
    normed_spec = pl.BlockSpec((blocks, step, width // blocks), lambda i: (0, i, 0))
    extra = len(args) - 1
    return call(
        prepare_kernel,
        args,
        (),
        grid=(rows // step,),
        in_specs=[spec] * len(args),
        out_specs=[normed_spec] + [spec] * extra,
        out_shape=[shape((blocks, rows, width // blocks), bf16)] + [shape((rows, width), bf16)] * extra,
        name="prepare",
    )


def mix_kernel(xin_ref, cot_ref, mix_ref):
    normed, _ = normalise(xin_ref[...].astype(f32))
    mix_ref[...] = (cot_ref[...].astype(f32) * normed).astype(bf16)


def grad_mix(xin, cot, after=()):
    rows, width = xin.shape
    step = 32
    spec = pl.BlockSpec((step, width), lambda i: (i, 0))
    return call(
        mix_kernel,
        (xin, cot),
        after,
        grid=(rows // step,),
        in_specs=[spec, spec],
        out_specs=spec,
        out_shape=shape((rows, width), bf16),
        name="grad_mix",
    )


def project_kernel(features_ref, weight_ref, causal_ref, part_ref, *rest):
    *mixed_refs, mixed_ref = rest
    groups, taps, _ = causal_ref.shape
    part = dot(features_ref[...], weight_ref[...]).astype(bf16)
    part_ref[...] = part
    width = part.shape[1] // groups
    for g in range(groups):
        cols = slice(g * width, (g + 1) * width)
        for start in range(0, part.shape[0], taps):
            if start == 0:
                out = dot(causal_ref[g, :, taps:], part[:taps, cols])
            else:
                out = dot(causal_ref[g], part[start - taps : start + taps, cols])
            mixed_ref[start : start + taps, cols] = out.astype(bf16)
    for s, out_ref in enumerate(mixed_refs):
        out_ref[...] = mixed_ref[window(place(s), out_ref.shape[0]), :]


def project(features, weight, causal, after=()):
    blocks = lax.axis_size("tensor")
    tokens, depth = features.shape
    rows = tokens // blocks
    width = weight.shape[1]
    groups, taps, _ = causal.shape
    step = 4
    tile = width // groups * step
    part, *mixed = call(
        project_kernel,
        (features, weight, causal),
        after,
        grid=(groups // step,),
        in_specs=[
            pl.BlockSpec((tokens, depth), lambda i: (0, 0)),
            pl.BlockSpec((depth, tile), lambda i: (0, i)),
            pl.BlockSpec((step, taps, 2 * taps), lambda i: (i, 0, 0)),
        ],
        out_specs=[pl.BlockSpec((tokens, tile), lambda i: (0, i))]
        + [pl.BlockSpec((rows, tile), lambda i: (0, i))] * blocks,
        out_shape=[shape((tokens, width), bf16)] + [shape((rows, width), bf16)] * blocks,
        scratch_shapes=[pltpu.VMEM((tokens, tile), bf16)],
        flops=2 * tokens * width * (depth + 2 * taps),
        name="project",
    )
    return part, mixed


def back_kernel(blocks, *refs):
    count = 2 * blocks - 1
    mix_refs = refs[:count]
    part_ref, weight_ref, ahead_ref, grad_ref, taps_ref, back_ref, mix_ref, total = refs[count:]
    groups, taps, _ = ahead_ref.shape
    tokens = mix_ref.shape[0]
    rows = tokens // blocks
    width = mix_ref.shape[1] // groups
    mine = lax.axis_index("tensor")
    mix_ref[window(mine, rows), :] = mix_refs[0][...]
    for s in range(1, blocks):

        @pl.when(mine >= s)
        def _():
            mix_ref[window(mine - s, rows), :] = mix_refs[s][...]

        @pl.when(mine < s)
        def _():
            mix_ref[window(mine + (blocks - s), rows), :] = mix_refs[2 * blocks - 1 - s][...]

    row = lax.broadcasted_iota(jnp.int32, (taps, taps), 0)
    col = lax.broadcasted_iota(jnp.int32, (taps, taps), 1)
    starts = range(0, tokens, taps)
    for g in range(groups):
        cols = slice(g * width, (g + 1) * width)
        mix = mix_ref[:, cols]
        part = part_ref[:, cols]
        for start in starts:
            if start + taps == tokens:
                out = dot(ahead_ref[g, :, :taps], mix[start:])
            else:
                out = dot(ahead_ref[g], mix[start : start + 2 * taps])
            grad_ref[start : start + taps, cols] = out.astype(bf16)
        mixes = jnp.concatenate([mix[s : s + taps] for s in starts], axis=1)
        parts = jnp.concatenate([part[s : s + taps] for s in starts], axis=1)
        same = dot(parts, mixes, ((1,), (1,)))
        later = dot(parts[:, :-width], mixes[:, width:], ((1,), (1,)))
        pairs = jnp.where(col >= row, same, later)
        folded = pairs[0:8]
        for a in range(8, taps, 8):
            folded = folded + pltpu.roll(pairs[a : a + 8], taps - a, 1)
        line = folded[0:1]
        for b in range(1, 8):
            line = line + pltpu.roll(folded[b : b + 1], taps - b, 1)
        taps_ref[0, g : g + 1, :] = line
    product = dot(grad_ref[...], weight_ref[...], ((1,), (1,)))
    step = pl.program_id(0)

    @pl.when(step == 0)
    def _():
        total[...] = product

    @pl.when(step > 0)
    def _():
        total[...] += product

    @pl.when(step == pl.num_programs(0) - 1)
    def _():
        back_ref[...] = total[...].astype(bf16)


def back(mixes, part, weight, ahead, after=()):
    blocks = (len(mixes) + 1) // 2
    rows = mixes[0].shape[0]
    tokens, width = part.shape
    depth = weight.shape[0]
    groups, taps, _ = ahead.shape
    step = 4
    tile = width // groups * step
    spec = pl.BlockSpec((tokens, tile), lambda i: (0, i))
    return call(
        functools.partial(back_kernel, blocks),
        (*mixes, part, weight, ahead),
        after,
        grid=(groups // step,),
        in_specs=[pl.BlockSpec((rows, tile), lambda i: (0, i))] * len(mixes)
        + [
            spec,
            pl.BlockSpec((depth, tile), lambda i: (0, i)),
            pl.BlockSpec((step, taps, 2 * taps), lambda i: (i, 0, 0)),
        ],
        out_specs=[
            spec,
            pl.BlockSpec((1, step, taps), lambda i: (i, 0, 0)),
            pl.BlockSpec((tokens, depth), lambda i: (0, 0)),
        ],
        out_shape=[
            shape((tokens, width), bf16),
            shape((groups // step, step, taps), f32),
            shape((tokens, depth), bf16),
        ],
        scratch_shapes=[pltpu.VMEM((tokens, tile), bf16), pltpu.VMEM((tokens, depth), f32)],
        flops=2 * tokens * width * (depth + 4 * taps),
        name="back",
    )


def weight_kernel(down_x, up_x, down_g, up_g, out_ref, down_t, up_t):
    @pl.when(pl.program_id(0) == 0)
    def _():
        down_t[...] = down_x[...].T
        up_t[...] = up_x[...].T

    out_ref[...] = (dot(down_t[...], down_g[...]) + dot(up_t[...], up_g[...])).astype(bf16)


def weight_gradient(down_x, up_x, down_g, up_g, after=()):
    tokens, depth = down_x.shape
    width = down_g.shape[1]
    tile = width // 8
    whole = pl.BlockSpec((tokens, depth), lambda i: (0, 0))
    part = pl.BlockSpec((tokens, tile), lambda i: (0, i))
    return call(
        weight_kernel,
        (down_x, up_x, down_g, up_g),
        after,
        grid=(width // tile,),
        in_specs=[whole, whole, part, part],
        out_specs=pl.BlockSpec((depth, tile), lambda i: (0, i)),
        out_shape=shape((depth, width), bf16),
        scratch_shapes=[pltpu.VMEM((depth, tokens), bf16)] * 2,
        flops=4 * tokens * depth * width,
        name="weight_gradient",
    )


def finish_kernel(xin_ref, cot_ref, back_ref, *rest):
    *mixed_refs, out_ref = rest
    normed, inverse = normalise(xin_ref[...].astype(f32))
    cot = cot_ref[...].astype(f32)
    returned = jnp.concatenate([back_ref[i] for i in range(back_ref.shape[0])], axis=1)
    mixed = sum(ref[...].astype(f32) for ref in mixed_refs)
    total = cot * mixed + returned.astype(f32)
    mean = jnp.mean(total * normed, axis=1, keepdims=True)
    out_ref[0] = (cot + inverse * (total - normed * mean)).astype(bf16)


def finish(xin, cot, mixed, returned, after=()):
    rows, width = xin.shape
    blocks, _, depth = returned.shape
    step = 32
    spec = pl.BlockSpec((step, width), lambda i: (i, 0))
    return call(
        finish_kernel,
        (xin, cot, returned, *mixed),
        after,
        grid=(rows // step,),
        in_specs=[spec, spec, pl.BlockSpec((blocks, step, depth), lambda i: (0, i, 0))]
        + [spec] * len(mixed),
        out_specs=pl.BlockSpec((1, step, width), lambda i: (0, i, 0)),
        out_shape=shape((1, rows, width), bf16),
        name="finish",
    )


def exchange(x):
    blocks = lax.axis_size("tensor")
    x = x.reshape(blocks, -1, x.shape[-1])
    return lax.all_to_all(x, "tensor", split_axis=0, concat_axis=0, tiled=True)


def both_ways(right, left):
    blocks = lax.axis_size("tensor")
    onward = [(i, i + 1) for i in range(blocks - 1)]
    return (
        lax.ppermute(right, "tensor", onward),
        lax.ppermute(left, "tensor", [(j, i) for i, j in onward]),
    )


def payload_kernel(s, right_ref, left_ref, right_piece, left_piece, right_out, left_out):
    mine = lax.axis_index("tensor")
    blocks = lax.axis_size("tensor")

    def put(came, piece, out, adds):
        @pl.when(adds)
        def _():
            out[...] = (came[...].astype(f32) + piece[...].astype(f32)).astype(bf16)

        @pl.when(jnp.logical_not(adds))
        def _():
            out[...] = came[...]

    put(right_ref, right_piece, right_out, mine < s - 1)
    put(left_ref, left_piece, left_out, mine > blocks - s)


def payload(s, arrived, pieces, after=()):
    blocks = len(pieces)
    rows, width = pieces[0].shape
    step = 32
    spec = pl.BlockSpec((step, width), lambda i: (i, 0))
    return call(
        functools.partial(payload_kernel, s),
        (*arrived, pieces[blocks + 1 - s], pieces[s - 1]),
        after,
        grid=(rows // step,),
        in_specs=[spec] * 4,
        out_specs=[spec] * 2,
        out_shape=[shape((rows, width), bf16)] * 2,
        name="payload",
    )


def sort_arrivals(mix, pieces, arrivals):
    rights, lefts = zip(*arrivals)
    return [mix, *rights[:-1], *lefts[:-1]], [pieces[0], rights[-1], lefts[-1]]


def add_kernel(a_ref, b_ref, out_ref):
    out_ref[...] = a_ref[...] + b_ref[...]


def add(a, b, after=()):
    spec = pl.BlockSpec(a.shape, lambda i: (0,) * a.ndim)
    return call(
        add_kernel,
        (a, b),
        after,
        grid=(1,),
        in_specs=[spec, spec],
        out_specs=spec,
        out_shape=shape(a.shape, a.dtype),
        name="add",
    )


def sum_all(x, after=()):
    blocks = lax.axis_size("tensor")
    apart = 1
    while apart < blocks:
        other = lax.ppermute(x, "tensor", [(i, i ^ apart) for i in range(blocks)])
        x = add(x, other, after)
        apart *= 2
    return x


def per_device(weights, filters, down_input, down_cot, up_input, up_cot):
    sections = lax.axis_size("section")
    mirror = [(s, sections - 1 - s) for s in range(sections)]
    down_pairs = [(s + 1, s) for s in range(sections - 1)]
    up_pairs = [(sections - s, s) for s in range(1, sections)]
    weight = weights[0]
    down_xin, down_cot = down_input[0], down_cot[0]
    up_xin = lax.ppermute(up_input[0], "section", mirror)
    up_cot = lax.ppermute(up_cot[0], "section", mirror)
    blocks = lax.axis_size("tensor")
    depth = weight.shape[0]
    down_normed, down_mix = prepare(down_xin, down_cot)
    down_x = exchange(down_normed).reshape(-1, depth)
    down_arrivals = [both_ways(down_mix, down_mix)]
    causal, ahead = toeplitz(filters[0])
    (up_normed,) = prepare(up_xin)
    up_x = exchange(up_normed).reshape(-1, depth)
    up_mix = grad_mix(up_xin, up_cot, after=down_arrivals[0])
    up_arrivals = [both_ways(up_mix, up_mix)]
    down_part, down_pieces = project(down_x, weight, causal, after=(up_normed, up_mix))
    last = down_part
    for s in range(2, blocks + 1):
        sent = payload(s, down_arrivals[-1], down_pieces, after=(last,))
        down_arrivals.append(both_ways(*sent))
        if s == 2:
            up_part, up_pieces = project(up_x, weight, causal, after=sent)
        sent = payload(s, up_arrivals[-1], up_pieces, after=sent)
        up_arrivals.append(both_ways(*sent))
        last = sent[0]
    down_mixes, down_conv = sort_arrivals(down_mix, down_pieces, down_arrivals)
    up_mixes, up_conv = sort_arrivals(up_mix, up_pieces, up_arrivals)
    up_g, up_taps, up_back = back(up_mixes, up_part, weight, ahead, after=(last,))
    up_back = exchange(up_back)
    down_g, down_taps, down_back = back(
        down_mixes, down_part, weight, ahead, after=(up_g, *down_arrivals[-1], *up_arrivals[-1])
    )
    down_back = exchange(down_back)
    up_grad = finish(up_xin, up_cot, up_conv, up_back, after=(down_g,))
    up_passed = lax.ppermute(up_grad, "section", up_pairs)
    weight_grad = weight_gradient(down_x, up_x, down_g, up_g, after=(up_grad,))
    taps = add(down_taps, up_taps).reshape(filters.shape)
    taps = sum_all(taps, after=(weight_grad,))
    down_grad = finish(
        down_xin, down_cot, down_conv, down_back, after=(taps,)
    )
    down_passed = lax.ppermute(down_grad, "section", down_pairs)
    return weight_grad[None], taps, down_passed, up_passed


def solution(mesh):
    rows = P("section", "tensor", None)
    whole = P("section", None, None)
    return jax.shard_map(
        per_device,
        mesh=mesh,
        in_specs=(rows, whole, rows, rows, rows, rows),
        out_specs=(rows, whole, rows, rows),
        check_vma=False,
    )
```

```python
import functools

import jax
import jax.numpy as jnp
from jax import lax
from jax.experimental import pallas as pl
from jax.experimental.pallas import tpu as pltpu
from jax.sharding import PartitionSpec as P

epsilon = 1e-06
params = functools.partial(pltpu.CompilerParams, vmem_limit_bytes=63 * 1024 * 1024)
f32, bf16 = jnp.float32, jnp.bfloat16


def dot(a, b, dims=((1,), (0,))):
    return lax.dot_general(a, b, (dims, ((), ())), preferred_element_type=f32)


def shape(dims, dtype):
    return jax.ShapeDtypeStruct(dims, dtype)


def call(kernel, args, after, in_specs, **options):
    count = len(args)

    def body(*refs):
        kernel(*refs[:count], *refs[count + len(after) :])

    unread = [pl.BlockSpec(memory_space=pl.ANY)] * len(after)
    return pl.pallas_call(
        body,
        in_specs=list(in_specs) + unread,
        cost_estimate=pl.CostEstimate(flops=0, transcendentals=0, bytes_accessed=0),
        compiler_params=params(),
        **options,
    )(*args, *after)


def toeplitz_kernel(filters_ref, causal_ref, ahead_ref):
    taps = filters_ref.shape[1]
    row = lax.broadcasted_iota(jnp.int32, (taps, taps), 0)
    col = lax.broadcasted_iota(jnp.int32, (taps, taps), 1)
    for g in range(filters_ref.shape[0]):
        line = jnp.broadcast_to(filters_ref[g : g + 1, :], (taps, taps))
        turned = pltpu.roll(line, 0, 1, stride=1, stride_axis=0)
        own = jnp.where(col >= row, turned, 0.0)
        beyond = jnp.where(col < row, turned, 0.0)
        ahead_ref[g, :, :taps] = own.astype(bf16)
        ahead_ref[g, :, taps:] = beyond.astype(bf16)
        causal_ref[g, :, :taps] = beyond.T.astype(bf16)
        causal_ref[g, :, taps:] = own.T.astype(bf16)


def toeplitz(filters):
    groups, taps = filters.shape
    step = 8
    out = shape((groups, taps, 2 * taps), bf16)
    spec = pl.BlockSpec((step, taps, 2 * taps), lambda i: (i, 0, 0))
    return call(
        toeplitz_kernel,
        (filters,),
        (),
        grid=(groups // step,),
        in_specs=[pl.BlockSpec((step, taps), lambda i: (i, 0))],
        out_specs=[spec, spec],
        out_shape=[out, out],
        name="toeplitz",
    )


def place(by):
    blocks = lax.axis_size("tensor")
    return lax.rem(lax.axis_index("tensor") + (by + blocks), blocks)


def window(index, size):
    return pl.ds(pl.multiple_of(index * size, size), size)


def normalise(wide):
    inverse = lax.rsqrt(jnp.mean(wide * wide, axis=1, keepdims=True) + epsilon)
    return wide * inverse, inverse


def prepare_kernel(xin_ref, *refs):
    *cot_ref, normed_ref = refs[: len(refs) // 2 + 1]
    normed, _ = normalise(xin_ref[...].astype(f32))
    width = normed_ref.shape[2]
    for i in range(normed_ref.shape[0]):
        normed_ref[i] = normed[:, i * width : (i + 1) * width].astype(bf16)
    if cot_ref:
        refs[-1][...] = (cot_ref[0][...].astype(f32) * normed).astype(bf16)


def prepare(*args):
    rows, width = args[0].shape
    blocks = lax.axis_size("tensor")
    step = 32
    spec = pl.BlockSpec((step, width), lambda i: (i, 0))
    normed_spec = pl.BlockSpec((blocks, step, width // blocks), lambda i: (0, i, 0))
    extra = len(args) - 1
    return call(
        prepare_kernel,
        args,
        (),
        grid=(rows // step,),
        in_specs=[spec] * len(args),
        out_specs=[normed_spec] + [spec] * extra,
        out_shape=[shape((blocks, rows, width // blocks), bf16)] + [shape((rows, width), bf16)] * extra,
        name="prepare",
    )


def mix_kernel(xin_ref, cot_ref, mix_ref):
    normed, _ = normalise(xin_ref[...].astype(f32))
    mix_ref[...] = (cot_ref[...].astype(f32) * normed).astype(bf16)


def grad_mix(xin, cot, after=()):
    rows, width = xin.shape
    step = 32
    spec = pl.BlockSpec((step, width), lambda i: (i, 0))
    return call(
        mix_kernel,
        (xin, cot),
        after,
        grid=(rows // step,),
        in_specs=[spec, spec],
        out_specs=spec,
        out_shape=shape((rows, width), bf16),
        name="grad_mix",
    )


def project_kernel(features_ref, weight_ref, causal_ref, part_ref, *rest):
    *mixed_refs, mixed_ref = rest
    groups, taps, _ = causal_ref.shape
    part = dot(features_ref[...], weight_ref[...]).astype(bf16)
    part_ref[...] = part
    width = part.shape[1] // groups
    for g in range(groups):
        cols = slice(g * width, (g + 1) * width)
        for start in range(0, part.shape[0], taps):
            if start == 0:
                out = dot(causal_ref[g, :, taps:], part[:taps, cols])
            else:
                out = dot(causal_ref[g], part[start - taps : start + taps, cols])
            mixed_ref[start : start + taps, cols] = out.astype(bf16)
    for s, out_ref in enumerate(mixed_refs):
        out_ref[...] = mixed_ref[window(place(s), out_ref.shape[0]), :]


def project(features, weight, causal, after=()):
    blocks = lax.axis_size("tensor")
    tokens, depth = features.shape
    rows = tokens // blocks
    width = weight.shape[1]
    groups, taps, _ = causal.shape
    step = 4
    tile = width // groups * step
    part, *mixed = call(
        project_kernel,
        (features, weight, causal),
        after,
        grid=(groups // step,),
        in_specs=[
            pl.BlockSpec((tokens, depth), lambda i: (0, 0)),
            pl.BlockSpec((depth, tile), lambda i: (0, i)),
            pl.BlockSpec((step, taps, 2 * taps), lambda i: (i, 0, 0)),
        ],
        out_specs=[pl.BlockSpec((tokens, tile), lambda i: (0, i))]
        + [pl.BlockSpec((rows, tile), lambda i: (0, i))] * blocks,
        out_shape=[shape((tokens, width), bf16)] + [shape((rows, width), bf16)] * blocks,
        scratch_shapes=[pltpu.VMEM((tokens, tile), bf16)],
        name="project",
    )
    return part, mixed


def back_kernel(blocks, *refs):
    count = 2 * blocks - 1
    mix_refs = refs[:count]
    part_ref, weight_ref, ahead_ref, grad_ref, taps_ref, back_ref, mix_ref, total = refs[count:]
    groups, taps, _ = ahead_ref.shape
    tokens = mix_ref.shape[0]
    rows = tokens // blocks
    width = mix_ref.shape[1] // groups
    mine = lax.axis_index("tensor")
    mix_ref[window(mine, rows), :] = mix_refs[0][...]
    for s in range(1, blocks):

        @pl.when(mine >= s)
        def _():
            mix_ref[window(mine - s, rows), :] = mix_refs[s][...]

        @pl.when(mine < s)
        def _():
            mix_ref[window(mine + (blocks - s), rows), :] = mix_refs[2 * blocks - 1 - s][...]

    row = lax.broadcasted_iota(jnp.int32, (taps, taps), 0)
    col = lax.broadcasted_iota(jnp.int32, (taps, taps), 1)
    starts = range(0, tokens, taps)
    for g in range(groups):
        cols = slice(g * width, (g + 1) * width)
        mix = mix_ref[:, cols]
        part = part_ref[:, cols]
        for start in starts:
            if start + taps == tokens:
                out = dot(ahead_ref[g, :, :taps], mix[start:])
            else:
                out = dot(ahead_ref[g], mix[start : start + 2 * taps])
            grad_ref[start : start + taps, cols] = out.astype(bf16)
        mixes = jnp.concatenate([mix[s : s + taps] for s in starts], axis=1)
        parts = jnp.concatenate([part[s : s + taps] for s in starts], axis=1)
        same = dot(parts, mixes, ((1,), (1,)))
        later = dot(parts[:, :-width], mixes[:, width:], ((1,), (1,)))
        pairs = jnp.where(col >= row, same, later)
        folded = pairs[0:8]
        for a in range(8, taps, 8):
            folded = folded + pltpu.roll(pairs[a : a + 8], taps - a, 1)
        line = folded[0:1]
        for b in range(1, 8):
            line = line + pltpu.roll(folded[b : b + 1], taps - b, 1)
        taps_ref[0, g : g + 1, :] = line
    product = dot(grad_ref[...], weight_ref[...], ((1,), (1,)))
    step = pl.program_id(0)

    @pl.when(step == 0)
    def _():
        total[...] = product

    @pl.when(step > 0)
    def _():
        total[...] += product

    @pl.when(step == pl.num_programs(0) - 1)
    def _():
        back_ref[...] = total[...].astype(bf16)


def back(mixes, part, weight, ahead, after=()):
    blocks = (len(mixes) + 1) // 2
    rows = mixes[0].shape[0]
    tokens, width = part.shape
    depth = weight.shape[0]
    groups, taps, _ = ahead.shape
    step = 4
    tile = width // groups * step
    spec = pl.BlockSpec((tokens, tile), lambda i: (0, i))
    return call(
        functools.partial(back_kernel, blocks),
        (*mixes, part, weight, ahead),
        after,
        grid=(groups // step,),
        in_specs=[pl.BlockSpec((rows, tile), lambda i: (0, i))] * len(mixes)
        + [
            spec,
            pl.BlockSpec((depth, tile), lambda i: (0, i)),
            pl.BlockSpec((step, taps, 2 * taps), lambda i: (i, 0, 0)),
        ],
        out_specs=[
            spec,
            pl.BlockSpec((1, step, taps), lambda i: (i, 0, 0)),
            pl.BlockSpec((tokens, depth), lambda i: (0, 0)),
        ],
        out_shape=[
            shape((tokens, width), bf16),
            shape((groups // step, step, taps), f32),
            shape((tokens, depth), bf16),
        ],
        scratch_shapes=[pltpu.VMEM((tokens, tile), bf16), pltpu.VMEM((tokens, depth), f32)],
        name="back",
    )


def weight_kernel(down_x, up_x, down_g, up_g, out_ref, down_t, up_t):
    @pl.when(pl.program_id(0) == 0)
    def _():
        down_t[...] = down_x[...].T
        up_t[...] = up_x[...].T

    out_ref[...] = (dot(down_t[...], down_g[...]) + dot(up_t[...], up_g[...])).astype(bf16)


def weight_gradient(down_x, up_x, down_g, up_g, after=()):
    tokens, depth = down_x.shape
    width = down_g.shape[1]
    tile = width // 8
    whole = pl.BlockSpec((tokens, depth), lambda i: (0, 0))
    part = pl.BlockSpec((tokens, tile), lambda i: (0, i))
    return call(
        weight_kernel,
        (down_x, up_x, down_g, up_g),
        after,
        grid=(width // tile,),
        in_specs=[whole, whole, part, part],
        out_specs=pl.BlockSpec((depth, tile), lambda i: (0, i)),
        out_shape=shape((depth, width), bf16),
        scratch_shapes=[pltpu.VMEM((depth, tokens), bf16)] * 2,
        name="weight_gradient",
    )


def finish_kernel(xin_ref, cot_ref, back_ref, *rest):
    *mixed_refs, out_ref = rest
    normed, inverse = normalise(xin_ref[...].astype(f32))
    cot = cot_ref[...].astype(f32)
    returned = jnp.concatenate([back_ref[i] for i in range(back_ref.shape[0])], axis=1)
    mixed = sum(ref[...].astype(f32) for ref in mixed_refs)
    total = cot * mixed + returned.astype(f32)
    mean = jnp.mean(total * normed, axis=1, keepdims=True)
    out_ref[0] = (cot + inverse * (total - normed * mean)).astype(bf16)


def finish(xin, cot, mixed, returned, after=()):
    rows, width = xin.shape
    blocks, _, depth = returned.shape
    step = 32
    spec = pl.BlockSpec((step, width), lambda i: (i, 0))
    return call(
        finish_kernel,
        (xin, cot, returned, *mixed),
        after,
        grid=(rows // step,),
        in_specs=[spec, spec, pl.BlockSpec((blocks, step, depth), lambda i: (0, i, 0))]
        + [spec] * len(mixed),
        out_specs=pl.BlockSpec((1, step, width), lambda i: (0, i, 0)),
        out_shape=shape((1, rows, width), bf16),
        name="finish",
    )


def exchange(x):
    blocks = lax.axis_size("tensor")
    x = x.reshape(blocks, -1, x.shape[-1])
    return lax.all_to_all(x, "tensor", split_axis=0, concat_axis=0, tiled=True)


def both_ways(right, left):
    blocks = lax.axis_size("tensor")
    onward = [(i, i + 1) for i in range(blocks - 1)]
    return (
        lax.ppermute(right, "tensor", onward),
        lax.ppermute(left, "tensor", [(j, i) for i, j in onward]),
    )


def payload_kernel(s, right_ref, left_ref, right_piece, left_piece, right_out, left_out):
    mine = lax.axis_index("tensor")
    blocks = lax.axis_size("tensor")

    def put(came, piece, out, adds):
        @pl.when(adds)
        def _():
            out[...] = (came[...].astype(f32) + piece[...].astype(f32)).astype(bf16)

        @pl.when(jnp.logical_not(adds))
        def _():
            out[...] = came[...]

    put(right_ref, right_piece, right_out, mine < s - 1)
    put(left_ref, left_piece, left_out, mine > blocks - s)


def payload(s, arrived, pieces, after=()):
    blocks = len(pieces)
    rows, width = pieces[0].shape
    step = 32
    spec = pl.BlockSpec((step, width), lambda i: (i, 0))
    return call(
        functools.partial(payload_kernel, s),
        (*arrived, pieces[blocks + 1 - s], pieces[s - 1]),
        after,
        grid=(rows // step,),
        in_specs=[spec] * 4,
        out_specs=[spec] * 2,
        out_shape=[shape((rows, width), bf16)] * 2,
        name="payload",
    )


def sort_arrivals(mix, pieces, arrivals):
    rights, lefts = zip(*arrivals)
    return [mix, *rights[:-1], *lefts[:-1]], [pieces[0], rights[-1], lefts[-1]]


def add_kernel(a_ref, b_ref, out_ref):
    out_ref[...] = a_ref[...] + b_ref[...]


def add(a, b, after=()):
    spec = pl.BlockSpec(a.shape, lambda i: (0,) * a.ndim)
    return call(
        add_kernel,
        (a, b),
        after,
        grid=(1,),
        in_specs=[spec, spec],
        out_specs=spec,
        out_shape=shape(a.shape, a.dtype),
        name="add",
    )


def sum_all(x, after=()):
    blocks = lax.axis_size("tensor")
    apart = 1
    while apart < blocks:
        other = lax.ppermute(x, "tensor", [(i, i ^ apart) for i in range(blocks)])
        x = add(x, other, after)
        apart *= 2
    return x


def per_device(weights, filters, down_input, down_cot, up_input, up_cot):
    sections = lax.axis_size("section")
    mirror = [(s, sections - 1 - s) for s in range(sections)]
    down_pairs = [(s + 1, s) for s in range(sections - 1)]
    up_pairs = [(sections - s, s) for s in range(1, sections)]
    weight = weights[0]
    down_xin, down_cot = down_input[0], down_cot[0]
    up_xin = lax.ppermute(up_input[0], "section", mirror)
    up_cot = lax.ppermute(up_cot[0], "section", mirror)
    blocks = lax.axis_size("tensor")
    depth = weight.shape[0]
    down_normed, down_mix = prepare(down_xin, down_cot)
    down_x = exchange(down_normed).reshape(-1, depth)
    down_arrivals = [both_ways(down_mix, down_mix)]
    causal, ahead = toeplitz(filters[0])
    (up_normed,) = prepare(up_xin)
    up_x = exchange(up_normed).reshape(-1, depth)
    up_mix = grad_mix(up_xin, up_cot, after=down_arrivals[0])
    up_arrivals = [both_ways(up_mix, up_mix)]
    down_part, down_pieces = project(down_x, weight, causal, after=(up_normed, up_mix))
    last = down_part
    for s in range(2, blocks + 1):
        sent = payload(s, down_arrivals[-1], down_pieces, after=(last,))
        down_arrivals.append(both_ways(*sent))
        if s == 2:
            up_part, up_pieces = project(up_x, weight, causal, after=sent)
        sent = payload(s, up_arrivals[-1], up_pieces, after=sent)
        up_arrivals.append(both_ways(*sent))
        last = sent[0]
    down_mixes, down_conv = sort_arrivals(down_mix, down_pieces, down_arrivals)
    up_mixes, up_conv = sort_arrivals(up_mix, up_pieces, up_arrivals)
    up_g, up_taps, up_back = back(up_mixes, up_part, weight, ahead, after=(last,))
    up_back = exchange(up_back)
    down_g, down_taps, down_back = back(
        down_mixes, down_part, weight, ahead, after=(up_g,)
    )
    down_back = exchange(down_back)
    up_grad = finish(up_xin, up_cot, up_conv, up_back, after=(down_g,))
    up_passed = lax.ppermute(up_grad, "section", up_pairs)
    weight_grad = weight_gradient(down_x, up_x, down_g, up_g, after=(up_grad,))
    taps = add(down_taps, up_taps).reshape(filters.shape)
    taps = sum_all(taps, after=(weight_grad,))
    down_grad = finish(
        down_xin, down_cot, down_conv, down_back, after=(taps,)
    )
    down_passed = lax.ppermute(down_grad, "section", down_pairs)
    return weight_grad[None], taps, down_passed, up_passed


def solution(mesh):
    rows = P("section", "tensor", None)
    whole = P("section", None, None)
    return jax.shard_map(
        per_device,
        mesh=mesh,
        in_specs=(rows, whole, rows, rows, rows, rows),
        out_specs=(rows, whole, rows, rows),
        check_vma=False,
    )
```

```python
import functools

import jax
import jax.numpy as jnp
from jax import lax
from jax.experimental import pallas as pl
from jax.experimental.pallas import tpu as pltpu
from jax.sharding import PartitionSpec as P

epsilon = 1e-06
params = functools.partial(pltpu.CompilerParams, vmem_limit_bytes=63 * 1024 * 1024)
f32, bf16 = jnp.float32, jnp.bfloat16


def dot(a, b, dims=((1,), (0,))):
    return lax.dot_general(a, b, (dims, ((), ())), preferred_element_type=f32)


def shape(dims, dtype):
    return jax.ShapeDtypeStruct(dims, dtype)


def call(kernel, args, after, in_specs, **options):
    count = len(args)

    def body(*refs):
        kernel(*refs[:count], *refs[count + len(after) :])

    unread = [pl.BlockSpec(memory_space=pl.ANY)] * len(after)
    return pl.pallas_call(
        body,
        in_specs=list(in_specs) + unread,
        compiler_params=params(),
        **options,
    )(*args, *after)


def toeplitz_kernel(filters_ref, causal_ref, ahead_ref):
    taps = filters_ref.shape[1]
    row = lax.broadcasted_iota(jnp.int32, (taps, taps), 0)
    col = lax.broadcasted_iota(jnp.int32, (taps, taps), 1)
    for g in range(filters_ref.shape[0]):
        line = jnp.broadcast_to(filters_ref[g : g + 1, :], (taps, taps))
        turned = pltpu.roll(line, 0, 1, stride=1, stride_axis=0)
        own = jnp.where(col >= row, turned, 0.0)
        beyond = jnp.where(col < row, turned, 0.0)
        ahead_ref[g, :, :taps] = own.astype(bf16)
        ahead_ref[g, :, taps:] = beyond.astype(bf16)
        causal_ref[g, :, :taps] = beyond.T.astype(bf16)
        causal_ref[g, :, taps:] = own.T.astype(bf16)


def toeplitz(filters):
    groups, taps = filters.shape
    step = 8
    out = shape((groups, taps, 2 * taps), bf16)
    spec = pl.BlockSpec((step, taps, 2 * taps), lambda i: (i, 0, 0))
    return call(
        toeplitz_kernel,
        (filters,),
        (),
        grid=(groups // step,),
        in_specs=[pl.BlockSpec((step, taps), lambda i: (i, 0))],
        out_specs=[spec, spec],
        out_shape=[out, out],
        name="toeplitz",
    )


def place(by):
    blocks = lax.axis_size("tensor")
    return lax.rem(lax.axis_index("tensor") + (by + blocks), blocks)


def window(index, size):
    return pl.ds(pl.multiple_of(index * size, size), size)


def normalise(wide):
    inverse = lax.rsqrt(jnp.mean(wide * wide, axis=1, keepdims=True) + epsilon)
    return wide * inverse, inverse


def prepare_kernel(xin_ref, *refs):
    *cot_ref, normed_ref = refs[: len(refs) // 2 + 1]
    normed, _ = normalise(xin_ref[...].astype(f32))
    width = normed_ref.shape[2]
    for i in range(normed_ref.shape[0]):
        normed_ref[i] = normed[:, i * width : (i + 1) * width].astype(bf16)
    if cot_ref:
        refs[-1][...] = (cot_ref[0][...].astype(f32) * normed).astype(bf16)


def prepare(*args):
    rows, width = args[0].shape
    blocks = lax.axis_size("tensor")
    step = 32
    spec = pl.BlockSpec((step, width), lambda i: (i, 0))
    normed_spec = pl.BlockSpec((blocks, step, width // blocks), lambda i: (0, i, 0))
    extra = len(args) - 1
    return call(
        prepare_kernel,
        args,
        (),
        grid=(rows // step,),
        in_specs=[spec] * len(args),
        out_specs=[normed_spec] + [spec] * extra,
        out_shape=[shape((blocks, rows, width // blocks), bf16)] + [shape((rows, width), bf16)] * extra,
        name="prepare",
    )


def mix_kernel(xin_ref, cot_ref, mix_ref):
    normed, _ = normalise(xin_ref[...].astype(f32))
    mix_ref[...] = (cot_ref[...].astype(f32) * normed).astype(bf16)


def grad_mix(xin, cot, after=()):
    rows, width = xin.shape
    step = 32
    spec = pl.BlockSpec((step, width), lambda i: (i, 0))
    return call(
        mix_kernel,
        (xin, cot),
        after,
        grid=(rows // step,),
        in_specs=[spec, spec],
        out_specs=spec,
        out_shape=shape((rows, width), bf16),
        name="grad_mix",
    )


def project_kernel(features_ref, weight_ref, causal_ref, part_ref, *rest):
    *mixed_refs, mixed_ref = rest
    groups, taps, _ = causal_ref.shape
    part = dot(features_ref[...], weight_ref[...]).astype(bf16)
    part_ref[...] = part
    width = part.shape[1] // groups
    for g in range(groups):
        cols = slice(g * width, (g + 1) * width)
        for start in range(0, part.shape[0], taps):
            if start == 0:
                out = dot(causal_ref[g, :, taps:], part[:taps, cols])
            else:
                out = dot(causal_ref[g], part[start - taps : start + taps, cols])
            mixed_ref[start : start + taps, cols] = out.astype(bf16)
    for s, out_ref in enumerate(mixed_refs):
        out_ref[...] = mixed_ref[window(place(s), out_ref.shape[0]), :]


def project(features, weight, causal, after=()):
    blocks = lax.axis_size("tensor")
    tokens, depth = features.shape
    rows = tokens // blocks
    width = weight.shape[1]
    groups, taps, _ = causal.shape
    step = 4
    tile = width // groups * step
    part, *mixed = call(
        project_kernel,
        (features, weight, causal),
        after,
        grid=(groups // step,),
        in_specs=[
            pl.BlockSpec((tokens, depth), lambda i: (0, 0)),
            pl.BlockSpec((depth, tile), lambda i: (0, i)),
            pl.BlockSpec((step, taps, 2 * taps), lambda i: (i, 0, 0)),
        ],
        out_specs=[pl.BlockSpec((tokens, tile), lambda i: (0, i))]
        + [pl.BlockSpec((rows, tile), lambda i: (0, i))] * blocks,
        out_shape=[shape((tokens, width), bf16)] + [shape((rows, width), bf16)] * blocks,
        scratch_shapes=[pltpu.VMEM((tokens, tile), bf16)],
        name="project",
    )
    return part, mixed


def back_kernel(blocks, *refs):
    count = 2 * blocks - 1
    mix_refs = refs[:count]
    part_ref, weight_ref, ahead_ref, grad_ref, taps_ref, back_ref, mix_ref, total = refs[count:]
    groups, taps, _ = ahead_ref.shape
    tokens = mix_ref.shape[0]
    rows = tokens // blocks
    width = mix_ref.shape[1] // groups
    mine = lax.axis_index("tensor")
    mix_ref[window(mine, rows), :] = mix_refs[0][...]
    for s in range(1, blocks):

        @pl.when(mine >= s)
        def _():
            mix_ref[window(mine - s, rows), :] = mix_refs[s][...]

        @pl.when(mine < s)
        def _():
            mix_ref[window(mine + (blocks - s), rows), :] = mix_refs[2 * blocks - 1 - s][...]

    row = lax.broadcasted_iota(jnp.int32, (taps, taps), 0)
    col = lax.broadcasted_iota(jnp.int32, (taps, taps), 1)
    starts = range(0, tokens, taps)
    for g in range(groups):
        cols = slice(g * width, (g + 1) * width)
        mix = mix_ref[:, cols]
        part = part_ref[:, cols]
        for start in starts:
            if start + taps == tokens:
                out = dot(ahead_ref[g, :, :taps], mix[start:])
            else:
                out = dot(ahead_ref[g], mix[start : start + 2 * taps])
            grad_ref[start : start + taps, cols] = out.astype(bf16)
        mixes = jnp.concatenate([mix[s : s + taps] for s in starts], axis=1)
        parts = jnp.concatenate([part[s : s + taps] for s in starts], axis=1)
        same = dot(parts, mixes, ((1,), (1,)))
        later = dot(parts[:, :-width], mixes[:, width:], ((1,), (1,)))
        pairs = jnp.where(col >= row, same, later)
        folded = pairs[0:8]
        for a in range(8, taps, 8):
            folded = folded + pltpu.roll(pairs[a : a + 8], taps - a, 1)
        line = folded[0:1]
        for b in range(1, 8):
            line = line + pltpu.roll(folded[b : b + 1], taps - b, 1)
        taps_ref[0, g : g + 1, :] = line
    product = dot(grad_ref[...], weight_ref[...], ((1,), (1,)))
    step = pl.program_id(0)

    @pl.when(step == 0)
    def _():
        total[...] = product

    @pl.when(step > 0)
    def _():
        total[...] += product

    @pl.when(step == pl.num_programs(0) - 1)
    def _():
        back_ref[...] = total[...].astype(bf16)


def back(mixes, part, weight, ahead, after=()):
    blocks = (len(mixes) + 1) // 2
    rows = mixes[0].shape[0]
    tokens, width = part.shape
    depth = weight.shape[0]
    groups, taps, _ = ahead.shape
    step = 4
    tile = width // groups * step
    spec = pl.BlockSpec((tokens, tile), lambda i: (0, i))
    return call(
        functools.partial(back_kernel, blocks),
        (*mixes, part, weight, ahead),
        after,
        grid=(groups // step,),
        in_specs=[pl.BlockSpec((rows, tile), lambda i: (0, i))] * len(mixes)
        + [
            spec,
            pl.BlockSpec((depth, tile), lambda i: (0, i)),
            pl.BlockSpec((step, taps, 2 * taps), lambda i: (i, 0, 0)),
        ],
        out_specs=[
            spec,
            pl.BlockSpec((1, step, taps), lambda i: (i, 0, 0)),
            pl.BlockSpec((tokens, depth), lambda i: (0, 0)),
        ],
        out_shape=[
            shape((tokens, width), bf16),
            shape((groups // step, step, taps), f32),
            shape((tokens, depth), bf16),
        ],
        scratch_shapes=[pltpu.VMEM((tokens, tile), bf16), pltpu.VMEM((tokens, depth), f32)],
        name="back",
    )


def weight_kernel(down_x, up_x, down_g, up_g, out_ref, down_t, up_t):
    @pl.when(pl.program_id(0) == 0)
    def _():
        down_t[...] = down_x[...].T
        up_t[...] = up_x[...].T

    out_ref[...] = (dot(down_t[...], down_g[...]) + dot(up_t[...], up_g[...])).astype(bf16)


def weight_gradient(down_x, up_x, down_g, up_g, after=()):
    tokens, depth = down_x.shape
    width = down_g.shape[1]
    tile = width // 8
    whole = pl.BlockSpec((tokens, depth), lambda i: (0, 0))
    part = pl.BlockSpec((tokens, tile), lambda i: (0, i))
    return call(
        weight_kernel,
        (down_x, up_x, down_g, up_g),
        after,
        grid=(width // tile,),
        in_specs=[whole, whole, part, part],
        out_specs=pl.BlockSpec((depth, tile), lambda i: (0, i)),
        out_shape=shape((depth, width), bf16),
        scratch_shapes=[pltpu.VMEM((depth, tokens), bf16)] * 2,
        name="weight_gradient",
    )


def finish_kernel(xin_ref, cot_ref, back_ref, *rest):
    *mixed_refs, out_ref = rest
    normed, inverse = normalise(xin_ref[...].astype(f32))
    cot = cot_ref[...].astype(f32)
    returned = jnp.concatenate([back_ref[i] for i in range(back_ref.shape[0])], axis=1)
    mixed = sum(ref[...].astype(f32) for ref in mixed_refs)
    total = cot * mixed + returned.astype(f32)
    mean = jnp.mean(total * normed, axis=1, keepdims=True)
    out_ref[0] = (cot + inverse * (total - normed * mean)).astype(bf16)


def finish(xin, cot, mixed, returned, after=()):
    rows, width = xin.shape
    blocks, _, depth = returned.shape
    step = 32
    spec = pl.BlockSpec((step, width), lambda i: (i, 0))
    return call(
        finish_kernel,
        (xin, cot, returned, *mixed),
        after,
        grid=(rows // step,),
        in_specs=[spec, spec, pl.BlockSpec((blocks, step, depth), lambda i: (0, i, 0))]
        + [spec] * len(mixed),
        out_specs=pl.BlockSpec((1, step, width), lambda i: (0, i, 0)),
        out_shape=shape((1, rows, width), bf16),
        name="finish",
    )


def exchange(x):
    blocks = lax.axis_size("tensor")
    x = x.reshape(blocks, -1, x.shape[-1])
    return lax.all_to_all(x, "tensor", split_axis=0, concat_axis=0, tiled=True)


def both_ways(right, left):
    blocks = lax.axis_size("tensor")
    onward = [(i, i + 1) for i in range(blocks - 1)]
    return (
        lax.ppermute(right, "tensor", onward),
        lax.ppermute(left, "tensor", [(j, i) for i, j in onward]),
    )


def payload_kernel(s, right_ref, left_ref, right_piece, left_piece, right_out, left_out):
    mine = lax.axis_index("tensor")
    blocks = lax.axis_size("tensor")

    def put(came, piece, out, adds):
        @pl.when(adds)
        def _():
            out[...] = (came[...].astype(f32) + piece[...].astype(f32)).astype(bf16)

        @pl.when(jnp.logical_not(adds))
        def _():
            out[...] = came[...]

    put(right_ref, right_piece, right_out, mine < s - 1)
    put(left_ref, left_piece, left_out, mine > blocks - s)


def payload(s, arrived, pieces, after=()):
    blocks = len(pieces)
    rows, width = pieces[0].shape
    step = 32
    spec = pl.BlockSpec((step, width), lambda i: (i, 0))
    return call(
        functools.partial(payload_kernel, s),
        (*arrived, pieces[blocks + 1 - s], pieces[s - 1]),
        after,
        grid=(rows // step,),
        in_specs=[spec] * 4,
        out_specs=[spec] * 2,
        out_shape=[shape((rows, width), bf16)] * 2,
        name="payload",
    )


def sort_arrivals(mix, pieces, arrivals):
    rights, lefts = zip(*arrivals)
    return [mix, *rights[:-1], *lefts[:-1]], [pieces[0], rights[-1], lefts[-1]]


def add_kernel(a_ref, b_ref, out_ref):
    out_ref[...] = a_ref[...] + b_ref[...]


def add(a, b, after=()):
    spec = pl.BlockSpec(a.shape, lambda i: (0,) * a.ndim)
    return call(
        add_kernel,
        (a, b),
        after,
        grid=(1,),
        in_specs=[spec, spec],
        out_specs=spec,
        out_shape=shape(a.shape, a.dtype),
        name="add",
    )


def sum_all(x, after=()):
    blocks = lax.axis_size("tensor")
    apart = 1
    while apart < blocks:
        other = lax.ppermute(x, "tensor", [(i, i ^ apart) for i in range(blocks)])
        x = add(x, other, after)
        apart *= 2
    return x


def per_device(weights, filters, down_input, down_cot, up_input, up_cot):
    sections = lax.axis_size("section")
    mirror = [(s, sections - 1 - s) for s in range(sections)]
    down_pairs = [(s + 1, s) for s in range(sections - 1)]
    up_pairs = [(sections - s, s) for s in range(1, sections)]
    weight = weights[0]
    down_xin, down_cot = down_input[0], down_cot[0]
    up_xin = lax.ppermute(up_input[0], "section", mirror)
    up_cot = lax.ppermute(up_cot[0], "section", mirror)
    blocks = lax.axis_size("tensor")
    depth = weight.shape[0]
    down_normed, down_mix = prepare(down_xin, down_cot)
    down_x = exchange(down_normed).reshape(-1, depth)
    down_arrivals = [both_ways(down_mix, down_mix)]
    causal, ahead = toeplitz(filters[0])
    (up_normed,) = prepare(up_xin)
    up_x = exchange(up_normed).reshape(-1, depth)
    up_mix = grad_mix(up_xin, up_cot, after=down_arrivals[0])
    up_arrivals = [both_ways(up_mix, up_mix)]
    down_part, down_pieces = project(down_x, weight, causal, after=(up_normed, up_mix))
    last = down_part
    for s in range(2, blocks + 1):
        sent = payload(s, down_arrivals[-1], down_pieces, after=(last,))
        down_arrivals.append(both_ways(*sent))
        if s == 2:
            up_part, up_pieces = project(up_x, weight, causal, after=sent)
        if s == blocks:
            down_mixes, down_conv = sort_arrivals(down_mix, down_pieces, down_arrivals)
            down_g, down_taps, down_back = back(down_mixes, down_part, weight, ahead, after=sent)
            down_back = exchange(down_back)
            sent = (down_g,)
        sent = payload(s, up_arrivals[-1], up_pieces, after=sent)
        up_arrivals.append(both_ways(*sent))
        last = sent[0]
    up_mixes, up_conv = sort_arrivals(up_mix, up_pieces, up_arrivals)
    up_g, up_taps, up_back = back(
        up_mixes, up_part, weight, ahead, after=(last, *down_arrivals[-1])
    )
    up_back = exchange(up_back)
    weight_grad = weight_gradient(down_x, up_x, down_g, up_g)
    down_grad = finish(down_xin, down_cot, down_conv, down_back, after=(weight_grad,))
    down_passed = lax.ppermute(down_grad, "section", down_pairs)
    taps = add(down_taps, up_taps).reshape(filters.shape)
    taps = sum_all(taps, after=(down_grad,))
    up_grad = finish(up_xin, up_cot, up_conv, up_back, after=(taps,))
    up_passed = lax.ppermute(up_grad, "section", up_pairs)
    return weight_grad[None], taps, down_passed, up_passed


def solution(mesh):
    rows = P("section", "tensor", None)
    whole = P("section", None, None)
    return jax.shard_map(
        per_device,
        mesh=mesh,
        in_specs=(rows, whole, rows, rows, rows, rows),
        out_specs=(rows, whole, rows, rows),
        check_vma=False,
    )
```

```python
import functools

import jax
import jax.numpy as jnp
from jax import lax
from jax.experimental import pallas as pl
from jax.experimental.pallas import tpu as pltpu
from jax.sharding import PartitionSpec as P

epsilon = 1e-06
params = functools.partial(pltpu.CompilerParams, vmem_limit_bytes=63 * 1024 * 1024)
f32, bf16 = jnp.float32, jnp.bfloat16


def dot(a, b, dims=((1,), (0,))):
    return lax.dot_general(a, b, (dims, ((), ())), preferred_element_type=f32)


def shape(dims, dtype):
    return jax.ShapeDtypeStruct(dims, dtype)


def call(kernel, args, after, in_specs, out_shape, flops=0, **options):
    count = len(args)
    arrays = [*args, *(out_shape if isinstance(out_shape, list) else [out_shape])]
    cost = pl.CostEstimate(
        flops=flops,
        transcendentals=0,
        bytes_accessed=sum(x.size * x.dtype.itemsize for x in arrays),
    )

    def body(*refs):
        kernel(*refs[:count], *refs[count + len(after) :])

    unread = [pl.BlockSpec(memory_space=pl.ANY)] * len(after)
    return pl.pallas_call(
        body,
        in_specs=list(in_specs) + unread,
        out_shape=out_shape,
        cost_estimate=cost,
        compiler_params=params(),
        **options,
    )(*args, *after)


def toeplitz_kernel(filters_ref, causal_ref, ahead_ref):
    taps = filters_ref.shape[1]
    row = lax.broadcasted_iota(jnp.int32, (taps, taps), 0)
    col = lax.broadcasted_iota(jnp.int32, (taps, taps), 1)
    for g in range(filters_ref.shape[0]):
        line = jnp.broadcast_to(filters_ref[g : g + 1, :], (taps, taps))
        turned = pltpu.roll(line, 0, 1, stride=1, stride_axis=0)
        own = jnp.where(col >= row, turned, 0.0)
        beyond = jnp.where(col < row, turned, 0.0)
        ahead_ref[g, :, :taps] = own.astype(bf16)
        ahead_ref[g, :, taps:] = beyond.astype(bf16)
        causal_ref[g, :, :taps] = beyond.T.astype(bf16)
        causal_ref[g, :, taps:] = own.T.astype(bf16)


def toeplitz(filters):
    groups, taps = filters.shape
    step = 8
    out = shape((groups, taps, 2 * taps), bf16)
    spec = pl.BlockSpec((step, taps, 2 * taps), lambda i: (i, 0, 0))
    return call(
        toeplitz_kernel,
        (filters,),
        (),
        grid=(groups // step,),
        in_specs=[pl.BlockSpec((step, taps), lambda i: (i, 0))],
        out_specs=[spec, spec],
        out_shape=[out, out],
        name="toeplitz",
    )


def place(by):
    blocks = lax.axis_size("tensor")
    return lax.rem(lax.axis_index("tensor") + (by + blocks), blocks)


def window(index, size):
    return pl.ds(pl.multiple_of(index * size, size), size)


def normalise(wide):
    inverse = lax.rsqrt(jnp.mean(wide * wide, axis=1, keepdims=True) + epsilon)
    return wide * inverse, inverse


def prepare_kernel(xin_ref, *refs):
    *cot_ref, normed_ref = refs[: len(refs) // 2 + 1]
    normed, _ = normalise(xin_ref[...].astype(f32))
    width = normed_ref.shape[2]
    for i in range(normed_ref.shape[0]):
        normed_ref[i] = normed[:, i * width : (i + 1) * width].astype(bf16)
    if cot_ref:
        refs[-1][...] = (cot_ref[0][...].astype(f32) * normed).astype(bf16)


def prepare(*args):
    rows, width = args[0].shape
    blocks = lax.axis_size("tensor")
    step = 32
    spec = pl.BlockSpec((step, width), lambda i: (i, 0))
    normed_spec = pl.BlockSpec((blocks, step, width // blocks), lambda i: (0, i, 0))
    extra = len(args) - 1
    return call(
        prepare_kernel,
        args,
        (),
        grid=(rows // step,),
        in_specs=[spec] * len(args),
        out_specs=[normed_spec] + [spec] * extra,
        out_shape=[shape((blocks, rows, width // blocks), bf16)] + [shape((rows, width), bf16)] * extra,
        name="prepare",
    )


def mix_kernel(xin_ref, cot_ref, mix_ref):
    normed, _ = normalise(xin_ref[...].astype(f32))
    mix_ref[...] = (cot_ref[...].astype(f32) * normed).astype(bf16)


def grad_mix(xin, cot, after=()):
    rows, width = xin.shape
    step = 32
    spec = pl.BlockSpec((step, width), lambda i: (i, 0))
    return call(
        mix_kernel,
        (xin, cot),
        after,
        grid=(rows // step,),
        in_specs=[spec, spec],
        out_specs=spec,
        out_shape=shape((rows, width), bf16),
        name="grad_mix",
    )


def side_by_side(x, rows):
    return jnp.concatenate([x[s : s + rows] for s in range(0, x.shape[0], rows)], axis=1)


def project_kernel(features_ref, weight_ref, causal_ref, part_ref, *rest):
    *mixed_refs, mixed_ref = rest
    groups, taps, _ = causal_ref.shape
    part = dot(features_ref[...], weight_ref[...]).astype(bf16)
    part_ref[...] = part
    width = part.shape[1] // groups
    for g in range(groups):
        cols = slice(g * width, (g + 1) * width)
        own = side_by_side(part[:, cols], taps)
        before = jnp.concatenate([jnp.zeros((taps, width), bf16), own[:, :-width]], axis=1)
        out = dot(causal_ref[g], jnp.concatenate([before, own], axis=0)).astype(bf16)
        for i in range(out.shape[1] // width):
            mixed_ref[i * taps : (i + 1) * taps, cols] = out[:, i * width : (i + 1) * width]
    for s, out_ref in enumerate(mixed_refs):
        out_ref[...] = mixed_ref[window(place(s), out_ref.shape[0]), :]


def project(features, weight, causal, after=()):
    blocks = lax.axis_size("tensor")
    tokens, depth = features.shape
    rows = tokens // blocks
    width = weight.shape[1]
    groups, taps, _ = causal.shape
    step = 4
    tile = width // groups * step
    part, *mixed = call(
        project_kernel,
        (features, weight, causal),
        after,
        grid=(groups // step,),
        in_specs=[
            pl.BlockSpec((tokens, depth), lambda i: (0, 0)),
            pl.BlockSpec((depth, tile), lambda i: (0, i)),
            pl.BlockSpec((step, taps, 2 * taps), lambda i: (i, 0, 0)),
        ],
        out_specs=[pl.BlockSpec((tokens, tile), lambda i: (0, i))]
        + [pl.BlockSpec((rows, tile), lambda i: (0, i))] * blocks,
        out_shape=[shape((tokens, width), bf16)] + [shape((rows, width), bf16)] * blocks,
        scratch_shapes=[pltpu.VMEM((tokens, tile), bf16)],
        flops=2 * tokens * width * (depth + 2 * taps),
        name="project",
    )
    return part, mixed


def assemble(block_refs, mix_ref):
    blocks = (len(block_refs) + 1) // 2
    rows = block_refs[0].shape[0]
    mine = lax.axis_index("tensor")
    mix_ref[window(mine, rows), :] = block_refs[0][...]
    for s in range(1, blocks):

        @pl.when(mine >= s)
        def _():
            mix_ref[window(mine - s, rows), :] = block_refs[s][...]

        @pl.when(mine < s)
        def _():
            mix_ref[window(mine + (blocks - s), rows), :] = block_refs[2 * blocks - 1 - s][...]


def with_following(mix, taps):
    own = side_by_side(mix, taps)
    width = mix.shape[1]
    following = jnp.concatenate([own[:, width:], jnp.zeros((taps, width), bf16)], axis=1)
    return jnp.concatenate([own, following], axis=0)


def back_kernel(count, *refs):
    weight_ref, ahead_ref, grad_ref, back_ref, mix_ref, total = refs[count:]
    groups, taps, _ = ahead_ref.shape
    width = mix_ref.shape[1] // groups
    assemble(refs[:count], mix_ref)
    for g in range(groups):
        cols = slice(g * width, (g + 1) * width)
        out = dot(ahead_ref[g], with_following(mix_ref[:, cols], taps)).astype(bf16)
        for i in range(out.shape[1] // width):
            grad_ref[i * taps : (i + 1) * taps, cols] = out[:, i * width : (i + 1) * width]
    product = dot(grad_ref[...], weight_ref[...], ((1,), (1,)))
    step = pl.program_id(0)

    @pl.when(step == 0)
    def _():
        total[...] = product

    @pl.when(step > 0)
    def _():
        total[...] += product

    @pl.when(step == pl.num_programs(0) - 1)
    def _():
        back_ref[...] = total[...].astype(bf16)


def back(mixes, weight, ahead, after=()):
    rows, width = mixes[0].shape
    tokens = (len(mixes) + 1) // 2 * rows
    depth = weight.shape[0]
    groups, taps, _ = ahead.shape
    step = 4
    tile = width // groups * step
    return call(
        functools.partial(back_kernel, len(mixes)),
        (*mixes, weight, ahead),
        after,
        grid=(groups // step,),
        in_specs=[pl.BlockSpec((rows, tile), lambda i: (0, i))] * len(mixes)
        + [
            pl.BlockSpec((depth, tile), lambda i: (0, i)),
            pl.BlockSpec((step, taps, 2 * taps), lambda i: (i, 0, 0)),
        ],
        out_specs=[
            pl.BlockSpec((tokens, tile), lambda i: (0, i)),
            pl.BlockSpec((tokens, depth), lambda i: (0, 0)),
        ],
        out_shape=[shape((tokens, width), bf16), shape((tokens, depth), bf16)],
        scratch_shapes=[pltpu.VMEM((tokens, tile), bf16), pltpu.VMEM((tokens, depth), f32)],
        flops=2 * tokens * width * (depth + 2 * taps),
        name="back",
    )


def taps_kernel(count, groups, *refs):
    taps_ref, *mix_refs = refs[-3:]
    taps = taps_ref.shape[2]
    width = mix_refs[0].shape[1] // groups
    row = lax.broadcasted_iota(jnp.int32, (taps, taps), 0)
    col = lax.broadcasted_iota(jnp.int32, (taps, taps), 1)
    total = [0] * groups
    for first, mix_ref in zip((0, count + 1), mix_refs):
        assemble(refs[first : first + count], mix_ref)
        part_ref = refs[first + count]
        for g in range(groups):
            cols = slice(g * width, (g + 1) * width)
            both = with_following(mix_ref[:, cols], taps)
            total[g] += dot(side_by_side(part_ref[:, cols], taps), both, ((1,), (1,)))
    for g in range(groups):
        pairs = jnp.where(col >= row, total[g][:, :taps], total[g][:, taps:])
        folded = pairs[0:8]
        for a in range(8, taps, 8):
            folded = folded + pltpu.roll(pairs[a : a + 8], taps - a, 1)
        line = folded[0:1]
        for b in range(1, 8):
            line = line + pltpu.roll(folded[b : b + 1], taps - b, 1)
        taps_ref[0, g : g + 1, :] = line


def filter_gradient(down_mixes, down_part, up_mixes, up_part, groups, taps, after=()):
    rows, width = down_mixes[0].shape
    tokens = down_part.shape[0]
    step = 4
    tile = width // groups * step
    count = len(down_mixes)
    block = [pl.BlockSpec((rows, tile), lambda i: (0, i))] * count
    part = [pl.BlockSpec((tokens, tile), lambda i: (0, i))]
    return call(
        functools.partial(taps_kernel, count, step),
        (*down_mixes, down_part, *up_mixes, up_part),
        after,
        grid=(groups // step,),
        in_specs=(block + part) * 2,
        out_specs=pl.BlockSpec((1, step, taps), lambda i: (i, 0, 0)),
        out_shape=shape((groups // step, step, taps), f32),
        scratch_shapes=[pltpu.VMEM((tokens, tile), bf16)] * 2,
        flops=8 * tokens * width * taps,
        name="filter_gradient",
    ).reshape(1, groups, taps)


def weight_kernel(down_x, up_x, down_g, up_g, out_ref, down_t, up_t):
    @pl.when(pl.program_id(0) == 0)
    def _():
        down_t[...] = down_x[...].T
        up_t[...] = up_x[...].T

    out_ref[...] = (dot(down_t[...], down_g[...]) + dot(up_t[...], up_g[...])).astype(bf16)


def weight_gradient(down_x, up_x, down_g, up_g, after=()):
    tokens, depth = down_x.shape
    width = down_g.shape[1]
    tile = width // 8
    whole = pl.BlockSpec((tokens, depth), lambda i: (0, 0))
    part = pl.BlockSpec((tokens, tile), lambda i: (0, i))
    return call(
        weight_kernel,
        (down_x, up_x, down_g, up_g),
        after,
        grid=(width // tile,),
        in_specs=[whole, whole, part, part],
        out_specs=pl.BlockSpec((depth, tile), lambda i: (0, i)),
        out_shape=shape((depth, width), bf16),
        scratch_shapes=[pltpu.VMEM((depth, tokens), bf16)] * 2,
        flops=4 * tokens * depth * width,
        name="weight_gradient",
    )


def finish_kernel(xin_ref, cot_ref, back_ref, *rest):
    *mixed_refs, out_ref = rest
    normed, inverse = normalise(xin_ref[...].astype(f32))
    cot = cot_ref[...].astype(f32)
    returned = jnp.concatenate([back_ref[i] for i in range(back_ref.shape[0])], axis=1)
    mixed = sum(ref[...].astype(f32) for ref in mixed_refs)
    total = cot * mixed + returned.astype(f32)
    mean = jnp.mean(total * normed, axis=1, keepdims=True)
    out_ref[0] = (cot + inverse * (total - normed * mean)).astype(bf16)


def finish(xin, cot, mixed, returned, after=()):
    rows, width = xin.shape
    blocks, _, depth = returned.shape
    step = 32
    spec = pl.BlockSpec((step, width), lambda i: (i, 0))
    return call(
        finish_kernel,
        (xin, cot, returned, *mixed),
        after,
        grid=(rows // step,),
        in_specs=[spec, spec, pl.BlockSpec((blocks, step, depth), lambda i: (0, i, 0))]
        + [spec] * len(mixed),
        out_specs=pl.BlockSpec((1, step, width), lambda i: (0, i, 0)),
        out_shape=shape((1, rows, width), bf16),
        name="finish",
    )


def exchange(x):
    blocks = lax.axis_size("tensor")
    x = x.reshape(blocks, -1, x.shape[-1])
    return lax.all_to_all(x, "tensor", split_axis=0, concat_axis=0, tiled=True)


def both_ways(right, left):
    blocks = lax.axis_size("tensor")
    onward = [(i, i + 1) for i in range(blocks - 1)]
    return (
        lax.ppermute(right, "tensor", onward),
        lax.ppermute(left, "tensor", [(j, i) for i, j in onward]),
    )


def payload_kernel(s, right_ref, left_ref, right_piece, left_piece, right_out, left_out):
    mine = lax.axis_index("tensor")
    blocks = lax.axis_size("tensor")

    def put(came, piece, out, adds):
        @pl.when(adds)
        def _():
            out[...] = (came[...].astype(f32) + piece[...].astype(f32)).astype(bf16)

        @pl.when(jnp.logical_not(adds))
        def _():
            out[...] = came[...]

    put(right_ref, right_piece, right_out, mine < s - 1)
    put(left_ref, left_piece, left_out, mine > blocks - s)


def payload(s, arrived, pieces, after=()):
    blocks = len(pieces)
    rows, width = pieces[0].shape
    step = 32
    spec = pl.BlockSpec((step, width), lambda i: (i, 0))
    return call(
        functools.partial(payload_kernel, s),
        (*arrived, pieces[blocks + 1 - s], pieces[s - 1]),
        after,
        grid=(rows // step,),
        in_specs=[spec] * 4,
        out_specs=[spec] * 2,
        out_shape=[shape((rows, width), bf16)] * 2,
        name="payload",
    )


def sort_arrivals(mix, pieces, arrivals):
    rights, lefts = zip(*arrivals)
    return [mix, *rights[:-1], *lefts[:-1]], [pieces[0], rights[-1], lefts[-1]]


def sum_kernel(*refs):
    *in_refs, out_ref, sorted_ref = refs
    for s, ref in enumerate(in_refs):
        sorted_ref[pl.ds(place(-s), 1)] = ref[...]
    out_ref[...] = sum(sorted_ref[i : i + 1] for i in range(len(in_refs)))


def sum_all(x, after=()):
    blocks = lax.axis_size("tensor")
    terms = [x]
    for s in range(1, blocks):
        terms.append(lax.ppermute(x, "tensor", [(i, (i + s) % blocks) for i in range(blocks)]))
    spec = pl.BlockSpec(x.shape, lambda i: (0,) * x.ndim)
    return call(
        sum_kernel,
        terms,
        after,
        grid=(1,),
        in_specs=[spec] * blocks,
        out_specs=spec,
        out_shape=shape(x.shape, x.dtype),
        scratch_shapes=[pltpu.VMEM((blocks, *x.shape[1:]), x.dtype)],
        name="sum_all",
    )


def per_device(weights, filters, down_input, down_cot, up_input, up_cot):
    sections = lax.axis_size("section")
    mirror = [(s, sections - 1 - s) for s in range(sections)]
    down_pairs = [(s + 1, s) for s in range(sections - 1)]
    up_pairs = [(sections - s, s) for s in range(1, sections)]
    weight = weights[0]
    down_xin, down_cot = down_input[0], down_cot[0]
    up_xin = lax.ppermute(up_input[0], "section", mirror)
    up_cot = lax.ppermute(up_cot[0], "section", mirror)
    blocks = lax.axis_size("tensor")
    depth = weight.shape[0]
    down_normed, down_mix = prepare(down_xin, down_cot)
    down_x = exchange(down_normed).reshape(-1, depth)
    down_arrivals = [both_ways(down_mix, down_mix)]
    causal, ahead = toeplitz(filters[0])
    (up_normed,) = prepare(up_xin)
    up_x = exchange(up_normed).reshape(-1, depth)
    up_mix = grad_mix(up_xin, up_cot, after=down_arrivals[0])
    up_arrivals = [both_ways(up_mix, up_mix)]
    down_part, down_pieces = project(down_x, weight, causal, after=(up_normed, up_mix))
    last = down_part
    for s in range(2, blocks + 1):
        sent = payload(s, down_arrivals[-1], down_pieces, after=(last,))
        down_arrivals.append(both_ways(*sent))
        if s == 2:
            up_part, up_pieces = project(up_x, weight, causal, after=sent)
        sent = payload(s, up_arrivals[-1], up_pieces, after=sent)
        up_arrivals.append(both_ways(*sent))
        last = sent[0]
    down_mixes, down_conv = sort_arrivals(down_mix, down_pieces, down_arrivals)
    up_mixes, up_conv = sort_arrivals(up_mix, up_pieces, up_arrivals)
    up_g, up_back = back(up_mixes, weight, ahead, after=(last,))
    up_back = exchange(up_back)
    taps = filter_gradient(
        down_mixes, down_part, up_mixes, up_part, *filters.shape[1:], after=(up_g,)
    )
    down_g, down_back = back(
        down_mixes, weight, ahead, after=(taps, *down_arrivals[-1], *up_arrivals[-1])
    )
    down_back = exchange(down_back)
    up_grad = finish(up_xin, up_cot, up_conv, up_back, after=(down_g,))
    up_passed = lax.ppermute(up_grad, "section", up_pairs)
    weight_grad = weight_gradient(down_x, up_x, down_g, up_g, after=(up_grad,))
    taps = sum_all(taps, after=(weight_grad,))
    down_grad = finish(down_xin, down_cot, down_conv, down_back, after=(taps, up_passed))
    down_passed = lax.ppermute(down_grad, "section", down_pairs)
    return weight_grad[None], taps, down_passed, up_passed


def solution(mesh):
    rows = P("section", "tensor", None)
    whole = P("section", None, None)
    return jax.shard_map(
        per_device,
        mesh=mesh,
        in_specs=(rows, whole, rows, rows, rows, rows),
        out_specs=(rows, whole, rows, rows),
        check_vma=False,
    )
```

```python
import functools

import jax
import jax.numpy as jnp
from jax import lax
from jax.experimental import pallas as pl
from jax.experimental.pallas import tpu as pltpu
from jax.sharding import PartitionSpec as P

epsilon = 1e-06
params = functools.partial(pltpu.CompilerParams, vmem_limit_bytes=63 * 1024 * 1024)
f32, bf16 = jnp.float32, jnp.bfloat16


def dot(a, b, dims=((1,), (0,))):
    return lax.dot_general(a, b, (dims, ((), ())), preferred_element_type=f32)


def shape(dims, dtype):
    return jax.ShapeDtypeStruct(dims, dtype)


def call(kernel, args, after, in_specs, out_shape, flops=0, counted=True, **options):
    count = len(args)
    arrays = [*args, *(out_shape if isinstance(out_shape, list) else [out_shape])]
    cost = pl.CostEstimate(
        flops=flops,
        transcendentals=0,
        bytes_accessed=counted * sum(x.size * x.dtype.itemsize for x in arrays),
    )

    def body(*refs):
        kernel(*refs[:count], *refs[count + len(after) :])

    unread = [pl.BlockSpec(memory_space=pl.ANY)] * len(after)
    return pl.pallas_call(
        body,
        in_specs=list(in_specs) + unread,
        out_shape=out_shape,
        cost_estimate=cost,
        compiler_params=params(),
        **options,
    )(*args, *after)


def toeplitz_kernel(filters_ref, causal_ref, ahead_ref):
    taps = filters_ref.shape[1]
    row = lax.broadcasted_iota(jnp.int32, (taps, taps), 0)
    col = lax.broadcasted_iota(jnp.int32, (taps, taps), 1)
    for g in range(filters_ref.shape[0]):
        line = jnp.broadcast_to(filters_ref[g : g + 1, :], (taps, taps))
        turned = pltpu.roll(line, 0, 1, stride=1, stride_axis=0)
        own = jnp.where(col >= row, turned, 0.0)
        beyond = jnp.where(col < row, turned, 0.0)
        ahead_ref[g, :, :taps] = own.astype(bf16)
        ahead_ref[g, :, taps:] = beyond.astype(bf16)
        causal_ref[g, :, :taps] = beyond.T.astype(bf16)
        causal_ref[g, :, taps:] = own.T.astype(bf16)


def toeplitz(filters):
    groups, taps = filters.shape
    step = 8
    out = shape((groups, taps, 2 * taps), bf16)
    spec = pl.BlockSpec((step, taps, 2 * taps), lambda i: (i, 0, 0))
    return call(
        toeplitz_kernel,
        (filters,),
        (),
        grid=(groups // step,),
        in_specs=[pl.BlockSpec((step, taps), lambda i: (i, 0))],
        out_specs=[spec, spec],
        out_shape=[out, out],
        name="toeplitz",
    )


def place(by):
    blocks = lax.axis_size("tensor")
    return lax.rem(lax.axis_index("tensor") + (by + blocks), blocks)


def window(index, size):
    return pl.ds(pl.multiple_of(index * size, size), size)


def normalise(wide):
    inverse = lax.rsqrt(jnp.mean(wide * wide, axis=1, keepdims=True) + epsilon)
    return wide * inverse, inverse


def prepare_kernel(xin_ref, *refs):
    *cot_ref, normed_ref = refs[: len(refs) // 2 + 1]
    normed, _ = normalise(xin_ref[...].astype(f32))
    width = normed_ref.shape[2]
    for i in range(normed_ref.shape[0]):
        normed_ref[i] = normed[:, i * width : (i + 1) * width].astype(bf16)
    if cot_ref:
        refs[-1][...] = (cot_ref[0][...].astype(f32) * normed).astype(bf16)


def prepare(*args):
    rows, width = args[0].shape
    blocks = lax.axis_size("tensor")
    step = 16
    spec = pl.BlockSpec((step, width), lambda i: (i, 0))
    normed_spec = pl.BlockSpec((blocks, step, width // blocks), lambda i: (0, i, 0))
    extra = len(args) - 1
    return call(
        prepare_kernel,
        args,
        (),
        grid=(rows // step,),
        in_specs=[spec] * len(args),
        out_specs=[normed_spec] + [spec] * extra,
        out_shape=[shape((blocks, rows, width // blocks), bf16)] + [shape((rows, width), bf16)] * extra,
        name="prepare",
    )


def mix_kernel(xin_ref, cot_ref, mix_ref):
    normed, _ = normalise(xin_ref[...].astype(f32))
    mix_ref[...] = (cot_ref[...].astype(f32) * normed).astype(bf16)


def grad_mix(xin, cot, after=()):
    rows, width = xin.shape
    step = 32
    spec = pl.BlockSpec((step, width), lambda i: (i, 0))
    return call(
        mix_kernel,
        (xin, cot),
        after,
        grid=(rows // step,),
        in_specs=[spec, spec],
        out_specs=spec,
        out_shape=shape((rows, width), bf16),
        name="grad_mix",
    )


def side_by_side(x, rows):
    return jnp.concatenate([x[s : s + rows] for s in range(0, x.shape[0], rows)], axis=1)


def project_kernel(features_ref, weight_ref, causal_ref, part_ref, *rest):
    *mixed_refs, mixed_ref = rest
    groups, taps, _ = causal_ref.shape
    part = dot(features_ref[...], weight_ref[...]).astype(bf16)
    part_ref[...] = part
    width = part.shape[1] // groups
    for g in range(groups):
        cols = slice(g * width, (g + 1) * width)
        own = side_by_side(part[:, cols], taps)
        before = jnp.concatenate([jnp.zeros((taps, width), bf16), own[:, :-width]], axis=1)
        out = dot(causal_ref[g], jnp.concatenate([before, own], axis=0)).astype(bf16)
        for i in range(out.shape[1] // width):
            mixed_ref[i * taps : (i + 1) * taps, cols] = out[:, i * width : (i + 1) * width]
    for s, out_ref in enumerate(mixed_refs):
        out_ref[...] = mixed_ref[window(place(s), out_ref.shape[0]), :]


def project(features, weight, causal, after=()):
    blocks = lax.axis_size("tensor")
    tokens, depth = features.shape
    rows = tokens // blocks
    width = weight.shape[1]
    groups, taps, _ = causal.shape
    step = 4
    tile = width // groups * step
    part, *mixed = call(
        project_kernel,
        (features, weight, causal),
        after,
        grid=(groups // step,),
        in_specs=[
            pl.BlockSpec((tokens, depth), lambda i: (0, 0)),
            pl.BlockSpec((depth, tile), lambda i: (0, i)),
            pl.BlockSpec((step, taps, 2 * taps), lambda i: (i, 0, 0)),
        ],
        out_specs=[pl.BlockSpec((tokens, tile), lambda i: (0, i))]
        + [pl.BlockSpec((rows, tile), lambda i: (0, i))] * blocks,
        out_shape=[shape((tokens, width), bf16)] + [shape((rows, width), bf16)] * blocks,
        scratch_shapes=[pltpu.VMEM((tokens, tile), bf16)],
        flops=2 * tokens * width * (depth + 2 * taps),
        name="project",
    )
    return part, mixed


def assemble(block_refs, mix_ref):
    blocks = (len(block_refs) + 1) // 2
    rows = block_refs[0].shape[0]
    mine = lax.axis_index("tensor")
    mix_ref[window(mine, rows), :] = block_refs[0][...]
    for s in range(1, blocks):

        @pl.when(mine >= s)
        def _():
            mix_ref[window(mine - s, rows), :] = block_refs[s][...]

        @pl.when(mine < s)
        def _():
            mix_ref[window(mine + (blocks - s), rows), :] = block_refs[2 * blocks - 1 - s][...]


def with_following(mix, taps):
    own = side_by_side(mix, taps)
    width = mix.shape[1]
    following = jnp.concatenate([own[:, width:], jnp.zeros((taps, width), bf16)], axis=1)
    return jnp.concatenate([own, following], axis=0)


def back_kernel(count, *refs):
    weight_ref, ahead_ref, grad_ref, back_ref, mix_ref, total = refs[count:]
    groups, taps, _ = ahead_ref.shape
    width = mix_ref.shape[1] // groups
    assemble(refs[:count], mix_ref)
    for g in range(groups):
        cols = slice(g * width, (g + 1) * width)
        out = dot(ahead_ref[g], with_following(mix_ref[:, cols], taps)).astype(bf16)
        for i in range(out.shape[1] // width):
            grad_ref[i * taps : (i + 1) * taps, cols] = out[:, i * width : (i + 1) * width]
    product = dot(grad_ref[...], weight_ref[...], ((1,), (1,)))
    step = pl.program_id(0)

    @pl.when(step == 0)
    def _():
        total[...] = product

    @pl.when(step > 0)
    def _():
        total[...] += product

    @pl.when(step == pl.num_programs(0) - 1)
    def _():
        back_ref[...] = total[...].astype(bf16)


def back(mixes, weight, ahead, after=()):
    rows, width = mixes[0].shape
    tokens = (len(mixes) + 1) // 2 * rows
    depth = weight.shape[0]
    groups, taps, _ = ahead.shape
    step = 4
    tile = width // groups * step
    return call(
        functools.partial(back_kernel, len(mixes)),
        (*mixes, weight, ahead),
        after,
        grid=(groups // step,),
        in_specs=[pl.BlockSpec((rows, tile), lambda i: (0, i))] * len(mixes)
        + [
            pl.BlockSpec((depth, tile), lambda i: (0, i)),
            pl.BlockSpec((step, taps, 2 * taps), lambda i: (i, 0, 0)),
        ],
        out_specs=[
            pl.BlockSpec((tokens, tile), lambda i: (0, i)),
            pl.BlockSpec((tokens, depth), lambda i: (0, 0)),
        ],
        out_shape=[shape((tokens, width), bf16), shape((tokens, depth), bf16)],
        scratch_shapes=[pltpu.VMEM((tokens, tile), bf16), pltpu.VMEM((tokens, depth), f32)],
        flops=2 * tokens * width * (depth + 2 * taps),
        name="back",
    )


def taps_kernel(count, groups, *refs):
    taps_ref, *mix_refs = refs[-3:]
    taps = taps_ref.shape[2]
    width = mix_refs[0].shape[1] // groups
    row = lax.broadcasted_iota(jnp.int32, (taps, taps), 0)
    col = lax.broadcasted_iota(jnp.int32, (taps, taps), 1)
    total = [0] * groups
    for first, mix_ref in zip((0, count + 1), mix_refs):
        assemble(refs[first : first + count], mix_ref)
        part_ref = refs[first + count]
        for g in range(groups):
            cols = slice(g * width, (g + 1) * width)
            both = with_following(mix_ref[:, cols], taps)
            total[g] += dot(side_by_side(part_ref[:, cols], taps), both, ((1,), (1,)))
    for g in range(groups):
        pairs = jnp.where(col >= row, total[g][:, :taps], total[g][:, taps:])
        folded = pairs[0:8]
        for a in range(8, taps, 8):
            folded = folded + pltpu.roll(pairs[a : a + 8], taps - a, 1)
        line = folded[0:1]
        for b in range(1, 8):
            line = line + pltpu.roll(folded[b : b + 1], taps - b, 1)
        taps_ref[0, g : g + 1, :] = line


def filter_gradient(down_mixes, down_part, up_mixes, up_part, groups, taps, after=()):
    rows, width = down_mixes[0].shape
    tokens = down_part.shape[0]
    step = 4
    tile = width // groups * step
    count = len(down_mixes)
    block = [pl.BlockSpec((rows, tile), lambda i: (0, i))] * count
    part = [pl.BlockSpec((tokens, tile), lambda i: (0, i))]
    return call(
        functools.partial(taps_kernel, count, step),
        (*down_mixes, down_part, *up_mixes, up_part),
        after,
        grid=(groups // step,),
        in_specs=(block + part) * 2,
        out_specs=pl.BlockSpec((1, step, taps), lambda i: (i, 0, 0)),
        out_shape=shape((groups // step, step, taps), f32),
        scratch_shapes=[pltpu.VMEM((tokens, tile), bf16)] * 2,
        counted=False,
        name="filter_gradient",
    ).reshape(1, groups, taps)


def weight_kernel(down_x, up_x, down_g, up_g, out_ref, down_t, up_t):
    @pl.when(pl.program_id(0) == 0)
    def _():
        down_t[...] = down_x[...].T
        up_t[...] = up_x[...].T

    out_ref[...] = (dot(down_t[...], down_g[...]) + dot(up_t[...], up_g[...])).astype(bf16)


def weight_gradient(down_x, up_x, down_g, up_g, after=()):
    tokens, depth = down_x.shape
    width = down_g.shape[1]
    tile = width // 8
    whole = pl.BlockSpec((tokens, depth), lambda i: (0, 0))
    part = pl.BlockSpec((tokens, tile), lambda i: (0, i))
    return call(
        weight_kernel,
        (down_x, up_x, down_g, up_g),
        after,
        grid=(width // tile,),
        in_specs=[whole, whole, part, part],
        out_specs=pl.BlockSpec((depth, tile), lambda i: (0, i)),
        out_shape=shape((depth, width), bf16),
        scratch_shapes=[pltpu.VMEM((depth, tokens), bf16)] * 2,
        flops=4 * tokens * depth * width,
        name="weight_gradient",
    )


def finish_kernel(xin_ref, cot_ref, back_ref, *rest):
    *mixed_refs, out_ref = rest
    normed, inverse = normalise(xin_ref[...].astype(f32))
    cot = cot_ref[...].astype(f32)
    returned = jnp.concatenate([back_ref[i] for i in range(back_ref.shape[0])], axis=1)
    mixed = sum(ref[...].astype(f32) for ref in mixed_refs)
    total = cot * mixed + returned.astype(f32)
    mean = jnp.mean(total * normed, axis=1, keepdims=True)
    out_ref[0] = (cot + inverse * (total - normed * mean)).astype(bf16)


def finish(xin, cot, mixed, returned, after=()):
    rows, width = xin.shape
    blocks, _, depth = returned.shape
    step = 16
    spec = pl.BlockSpec((step, width), lambda i: (i, 0))
    return call(
        finish_kernel,
        (xin, cot, returned, *mixed),
        after,
        grid=(rows // step,),
        in_specs=[spec, spec, pl.BlockSpec((blocks, step, depth), lambda i: (0, i, 0))]
        + [spec] * len(mixed),
        out_specs=pl.BlockSpec((1, step, width), lambda i: (0, i, 0)),
        out_shape=shape((1, rows, width), bf16),
        name="finish",
    )


def exchange(x):
    blocks = lax.axis_size("tensor")
    x = x.reshape(blocks, -1, x.shape[-1])
    return lax.all_to_all(x, "tensor", split_axis=0, concat_axis=0, tiled=True)


def both_ways(right, left):
    blocks = lax.axis_size("tensor")
    onward = [(i, i + 1) for i in range(blocks - 1)]
    return (
        lax.ppermute(right, "tensor", onward),
        lax.ppermute(left, "tensor", [(j, i) for i, j in onward]),
    )


def payload_kernel(s, right_ref, left_ref, right_piece, left_piece, right_out, left_out):
    mine = lax.axis_index("tensor")
    blocks = lax.axis_size("tensor")

    def put(came, piece, out, adds):
        @pl.when(adds)
        def _():
            out[...] = (came[...].astype(f32) + piece[...].astype(f32)).astype(bf16)

        @pl.when(jnp.logical_not(adds))
        def _():
            out[...] = came[...]

    put(right_ref, right_piece, right_out, mine < s - 1)
    put(left_ref, left_piece, left_out, mine > blocks - s)


def payload(s, arrived, pieces, after=()):
    blocks = len(pieces)
    rows, width = pieces[0].shape
    step = 32
    spec = pl.BlockSpec((step, width), lambda i: (i, 0))
    return call(
        functools.partial(payload_kernel, s),
        (*arrived, pieces[blocks + 1 - s], pieces[s - 1]),
        after,
        grid=(rows // step,),
        in_specs=[spec] * 4,
        out_specs=[spec] * 2,
        out_shape=[shape((rows, width), bf16)] * 2,
        name="payload",
    )


def sort_arrivals(mix, pieces, arrivals):
    rights, lefts = zip(*arrivals)
    return [mix, *rights[:-1], *lefts[:-1]], [pieces[0], rights[-1], lefts[-1]]


def sum_kernel(*refs):
    *in_refs, out_ref, sorted_ref = refs
    for s, ref in enumerate(in_refs):
        sorted_ref[pl.ds(place(-s), 1)] = ref[...]
    out_ref[...] = sum(sorted_ref[i : i + 1] for i in range(len(in_refs)))


def sum_all(x, after=()):
    blocks = lax.axis_size("tensor")
    terms = [x]
    for s in range(1, blocks):
        terms.append(lax.ppermute(x, "tensor", [(i, (i + s) % blocks) for i in range(blocks)]))
    spec = pl.BlockSpec(x.shape, lambda i: (0,) * x.ndim)
    return call(
        sum_kernel,
        terms,
        after,
        grid=(1,),
        in_specs=[spec] * blocks,
        out_specs=spec,
        out_shape=shape(x.shape, x.dtype),
        scratch_shapes=[pltpu.VMEM((blocks, *x.shape[1:]), x.dtype)],
        name="sum_all",
    )


def per_device(weights, filters, down_input, down_cot, up_input, up_cot):
    sections = lax.axis_size("section")
    mirror = [(s, sections - 1 - s) for s in range(sections)]
    down_pairs = [(s + 1, s) for s in range(sections - 1)]
    up_pairs = [(sections - s, s) for s in range(1, sections)]
    weight = weights[0]
    down_xin, down_cot = down_input[0], down_cot[0]
    up_xin = lax.ppermute(up_input[0], "section", mirror)
    up_cot = lax.ppermute(up_cot[0], "section", mirror)
    blocks = lax.axis_size("tensor")
    depth = weight.shape[0]
    down_normed, down_mix = prepare(down_xin, down_cot)
    down_x = exchange(down_normed).reshape(-1, depth)
    down_arrivals = [both_ways(down_mix, down_mix)]
    causal, ahead = toeplitz(filters[0])
    (up_normed,) = prepare(up_xin)
    up_x = exchange(up_normed).reshape(-1, depth)
    up_mix = grad_mix(up_xin, up_cot, after=down_arrivals[0])
    up_arrivals = [both_ways(up_mix, up_mix)]
    down_part, down_pieces = project(down_x, weight, causal, after=(up_normed, up_mix))
    last = down_part
    for s in range(2, blocks + 1):
        sent = payload(s, down_arrivals[-1], down_pieces, after=(last,))
        down_arrivals.append(both_ways(*sent))
        if s == 2:
            up_part, up_pieces = project(up_x, weight, causal, after=sent)
        sent = payload(s, up_arrivals[-1], up_pieces, after=sent)
        up_arrivals.append(both_ways(*sent))
        last = sent[0]
    down_mixes, down_conv = sort_arrivals(down_mix, down_pieces, down_arrivals)
    up_mixes, up_conv = sort_arrivals(up_mix, up_pieces, up_arrivals)
    up_g, up_back = back(up_mixes, weight, ahead, after=(last,))
    up_back = exchange(up_back)
    taps = filter_gradient(
        down_mixes, down_part, up_mixes, up_part, *filters.shape[1:], after=(up_g,)
    )
    down_g, down_back = back(
        down_mixes, weight, ahead, after=(taps, *down_arrivals[-1], *up_arrivals[-1])
    )
    down_back = exchange(down_back)
    taps = sum_all(taps, after=(down_g,))
    up_grad = finish(up_xin, up_cot, up_conv, up_back, after=(taps,))
    up_passed = lax.ppermute(up_grad, "section", up_pairs)
    down_grad = finish(down_xin, down_cot, down_conv, down_back, after=(up_passed,))
    down_passed = lax.ppermute(down_grad, "section", down_pairs)
    weight_grad = weight_gradient(down_x, up_x, down_g, up_g, after=(down_grad,))
    return weight_grad[None], taps, down_passed, up_passed


def solution(mesh):
    rows = P("section", "tensor", None)
    whole = P("section", None, None)
    return jax.shard_map(
        per_device,
        mesh=mesh,
        in_specs=(rows, whole, rows, rows, rows, rows),
        out_specs=(rows, whole, rows, rows),
        check_vma=False,
    )
```

```python
import functools

import jax
import jax.numpy as jnp
from jax import lax
from jax.experimental import pallas as pl
from jax.experimental.pallas import tpu as pltpu
from jax.sharding import PartitionSpec as P

epsilon = 1e-06
params = functools.partial(pltpu.CompilerParams, vmem_limit_bytes=63 * 1024 * 1024)
f32, bf16 = jnp.float32, jnp.bfloat16


def dot(a, b, dims=((1,), (0,))):
    return lax.dot_general(a, b, (dims, ((), ())), preferred_element_type=f32)


def shape(dims, dtype):
    return jax.ShapeDtypeStruct(dims, dtype)


def call(kernel, args, after, in_specs, out_shape, flops=0, **options):
    count = len(args)
    arrays = [*args, *(out_shape if isinstance(out_shape, list) else [out_shape])]
    cost = pl.CostEstimate(
        flops=flops,
        transcendentals=0,
        bytes_accessed=sum(x.size * x.dtype.itemsize for x in arrays),
    )

    def body(*refs):
        kernel(*refs[:count], *refs[count + len(after) :])

    unread = [pl.BlockSpec(memory_space=pl.ANY)] * len(after)
    return pl.pallas_call(
        body,
        in_specs=list(in_specs) + unread,
        out_shape=out_shape,
        cost_estimate=cost,
        compiler_params=params(),
        **options,
    )(*args, *after)


def toeplitz_kernel(filters_ref, causal_ref, ahead_ref):
    taps = filters_ref.shape[1]
    row = lax.broadcasted_iota(jnp.int32, (taps, taps), 0)
    col = lax.broadcasted_iota(jnp.int32, (taps, taps), 1)
    for g in range(filters_ref.shape[0]):
        line = jnp.broadcast_to(filters_ref[g : g + 1, :], (taps, taps))
        turned = pltpu.roll(line, 0, 1, stride=1, stride_axis=0)
        own = jnp.where(col >= row, turned, 0.0)
        beyond = jnp.where(col < row, turned, 0.0)
        ahead_ref[g, :, :taps] = own.astype(bf16)
        ahead_ref[g, :, taps:] = beyond.astype(bf16)
        causal_ref[g, :, :taps] = beyond.T.astype(bf16)
        causal_ref[g, :, taps:] = own.T.astype(bf16)


def toeplitz(filters):
    groups, taps = filters.shape
    step = 8
    out = shape((groups, taps, 2 * taps), bf16)
    spec = pl.BlockSpec((step, taps, 2 * taps), lambda i: (i, 0, 0))
    return call(
        toeplitz_kernel,
        (filters,),
        (),
        grid=(groups // step,),
        in_specs=[pl.BlockSpec((step, taps), lambda i: (i, 0))],
        out_specs=[spec, spec],
        out_shape=[out, out],
        name="toeplitz",
    )


def place(by):
    blocks = lax.axis_size("tensor")
    return lax.rem(lax.axis_index("tensor") + (by + blocks), blocks)


def window(index, size):
    return pl.ds(pl.multiple_of(index * size, size), size)


def normalise(wide):
    inverse = lax.rsqrt(jnp.mean(wide * wide, axis=1, keepdims=True) + epsilon)
    return wide * inverse, inverse


def prepare_kernel(xin_ref, *refs):
    *cot_ref, normed_ref = refs[: len(refs) // 2 + 1]
    normed, _ = normalise(xin_ref[...].astype(f32))
    width = normed_ref.shape[2]
    for i in range(normed_ref.shape[0]):
        normed_ref[i] = normed[:, i * width : (i + 1) * width].astype(bf16)
    if cot_ref:
        refs[-1][...] = (cot_ref[0][...].astype(f32) * normed).astype(bf16)


def prepare(*args, after=()):
    rows, width = args[0].shape
    blocks = lax.axis_size("tensor")
    step = 64
    spec = pl.BlockSpec((step, width), lambda i: (i, 0))
    normed_spec = pl.BlockSpec((blocks, step, width // blocks), lambda i: (0, i, 0))
    extra = len(args) - 1
    return call(
        prepare_kernel,
        args,
        after,
        grid=(rows // step,),
        in_specs=[spec] * len(args),
        out_specs=[normed_spec] + [spec] * extra,
        out_shape=[shape((blocks, rows, width // blocks), bf16)] + [shape((rows, width), bf16)] * extra,
        name="prepare",
    )


def mix_kernel(xin_ref, cot_ref, mix_ref):
    normed, _ = normalise(xin_ref[...].astype(f32))
    mix_ref[...] = (cot_ref[...].astype(f32) * normed).astype(bf16)


def grad_mix(xin, cot, after=()):
    rows, width = xin.shape
    step = 64
    spec = pl.BlockSpec((step, width), lambda i: (i, 0))
    return call(
        mix_kernel,
        (xin, cot),
        after,
        grid=(rows // step,),
        in_specs=[spec, spec],
        out_specs=spec,
        out_shape=shape((rows, width), bf16),
        name="grad_mix",
    )


def side_by_side(x, rows):
    return jnp.concatenate([x[s : s + rows] for s in range(0, x.shape[0], rows)], axis=1)


def project_kernel(features_ref, weight_ref, causal_ref, part_ref, *rest):
    *mixed_refs, mixed_ref = rest
    groups, taps, _ = causal_ref.shape
    part = dot(features_ref[...], weight_ref[...]).astype(bf16)
    part_ref[...] = part
    width = part.shape[1] // groups
    for g in range(groups):
        cols = slice(g * width, (g + 1) * width)
        own = side_by_side(part[:, cols], taps)
        before = jnp.concatenate([jnp.zeros((taps, width), bf16), own[:, :-width]], axis=1)
        out = dot(causal_ref[g], jnp.concatenate([before, own], axis=0)).astype(bf16)
        for i in range(out.shape[1] // width):
            mixed_ref[i * taps : (i + 1) * taps, cols] = out[:, i * width : (i + 1) * width]
    for s, out_ref in enumerate(mixed_refs):
        out_ref[...] = mixed_ref[window(place(s), out_ref.shape[0]), :]


def project(features, weight, causal, after=()):
    blocks = lax.axis_size("tensor")
    tokens, depth = features.shape
    rows = tokens // blocks
    width = weight.shape[1]
    groups, taps, _ = causal.shape
    step = 8
    tile = width // groups * step
    part, *mixed = call(
        project_kernel,
        (features, weight, causal),
        after,
        grid=(groups // step,),
        in_specs=[
            pl.BlockSpec((tokens, depth), lambda i: (0, 0)),
            pl.BlockSpec((depth, tile), lambda i: (0, i)),
            pl.BlockSpec((step, taps, 2 * taps), lambda i: (i, 0, 0)),
        ],
        out_specs=[pl.BlockSpec((tokens, tile), lambda i: (0, i))]
        + [pl.BlockSpec((rows, tile), lambda i: (0, i))] * blocks,
        out_shape=[shape((tokens, width), bf16)] + [shape((rows, width), bf16)] * blocks,
        scratch_shapes=[pltpu.VMEM((tokens, tile), bf16)],
        flops=2 * tokens * width * (depth + 2 * taps),
        name="project",
    )
    return part, mixed


def assemble(block_refs, mix_ref):
    blocks = (len(block_refs) + 1) // 2
    rows = block_refs[0].shape[0]
    mine = lax.axis_index("tensor")
    mix_ref[window(mine, rows), :] = block_refs[0][...]
    for s in range(1, blocks):

        @pl.when(mine >= s)
        def _():
            mix_ref[window(mine - s, rows), :] = block_refs[s][...]

        @pl.when(mine < s)
        def _():
            mix_ref[window(mine + (blocks - s), rows), :] = block_refs[2 * blocks - 1 - s][...]


def with_following(mix, taps):
    own = side_by_side(mix, taps)
    width = mix.shape[1]
    following = jnp.concatenate([own[:, width:], jnp.zeros((taps, width), bf16)], axis=1)
    return jnp.concatenate([own, following], axis=0)


def back_kernel(count, *refs):
    weight_ref, ahead_ref, grad_ref, back_ref, mix_ref, total = refs[count:]
    groups, taps, _ = ahead_ref.shape
    width = mix_ref.shape[1] // groups
    assemble(refs[:count], mix_ref)
    for g in range(groups):
        cols = slice(g * width, (g + 1) * width)
        out = dot(ahead_ref[g], with_following(mix_ref[:, cols], taps)).astype(bf16)
        for i in range(out.shape[1] // width):
            grad_ref[i * taps : (i + 1) * taps, cols] = out[:, i * width : (i + 1) * width]
    product = dot(grad_ref[...], weight_ref[...], ((1,), (1,)))
    step = pl.program_id(0)

    @pl.when(step == 0)
    def _():
        total[...] = product

    @pl.when(step > 0)
    def _():
        total[...] += product

    @pl.when(step == pl.num_programs(0) - 1)
    def _():
        back_ref[...] = total[...].astype(bf16)


def back(mixes, weight, ahead, after=()):
    rows, width = mixes[0].shape
    tokens = (len(mixes) + 1) // 2 * rows
    depth = weight.shape[0]
    groups, taps, _ = ahead.shape
    step = 8
    tile = width // groups * step
    return call(
        functools.partial(back_kernel, len(mixes)),
        (*mixes, weight, ahead),
        after,
        grid=(groups // step,),
        in_specs=[pl.BlockSpec((rows, tile), lambda i: (0, i))] * len(mixes)
        + [
            pl.BlockSpec((depth, tile), lambda i: (0, i)),
            pl.BlockSpec((step, taps, 2 * taps), lambda i: (i, 0, 0)),
        ],
        out_specs=[
            pl.BlockSpec((tokens, tile), lambda i: (0, i)),
            pl.BlockSpec((tokens, depth), lambda i: (0, 0)),
        ],
        out_shape=[shape((tokens, width), bf16), shape((tokens, depth), bf16)],
        scratch_shapes=[pltpu.VMEM((tokens, tile), bf16), pltpu.VMEM((tokens, depth), f32)],
        flops=2 * tokens * width * (depth + 2 * taps),
        name="back",
    )


def taps_kernel(count, groups, *refs):
    taps_ref, *mix_refs = refs[-3:]
    taps = taps_ref.shape[2]
    width = mix_refs[0].shape[1] // groups
    row = lax.broadcasted_iota(jnp.int32, (taps, taps), 0)
    col = lax.broadcasted_iota(jnp.int32, (taps, taps), 1)
    total = [0] * groups
    for first, mix_ref in zip((0, count + 1), mix_refs):
        assemble(refs[first : first + count], mix_ref)
        part_ref = refs[first + count]
        for g in range(groups):
            cols = slice(g * width, (g + 1) * width)
            both = with_following(mix_ref[:, cols], taps)
            total[g] += dot(side_by_side(part_ref[:, cols], taps), both, ((1,), (1,)))
    for g in range(groups):
        pairs = jnp.where(col >= row, total[g][:, :taps], total[g][:, taps:])
        folded = pairs[0:8]
        for a in range(8, taps, 8):
            folded = folded + pltpu.roll(pairs[a : a + 8], taps - a, 1)
        line = folded[0:1]
        for b in range(1, 8):
            line = line + pltpu.roll(folded[b : b + 1], taps - b, 1)
        taps_ref[0, g : g + 1, :] = line


def filter_gradient(down_mixes, down_part, up_mixes, up_part, groups, taps, after=()):
    rows, width = down_mixes[0].shape
    tokens = down_part.shape[0]
    step = 8
    tile = width // groups * step
    count = len(down_mixes)
    block = [pl.BlockSpec((rows, tile), lambda i: (0, i))] * count
    part = [pl.BlockSpec((tokens, tile), lambda i: (0, i))]
    return call(
        functools.partial(taps_kernel, count, step),
        (*down_mixes, down_part, *up_mixes, up_part),
        after,
        grid=(groups // step,),
        in_specs=(block + part) * 2,
        out_specs=pl.BlockSpec((1, step, taps), lambda i: (i, 0, 0)),
        out_shape=shape((groups // step, step, taps), f32),
        scratch_shapes=[pltpu.VMEM((tokens, tile), bf16)] * 2,
        flops=8 * tokens * width * taps,
        name="filter_gradient",
    ).reshape(1, groups, taps)


def weight_kernel(down_x, up_x, down_g, up_g, out_ref, down_t, up_t):
    @pl.when(pl.program_id(0) == 0)
    def _():
        down_t[...] = down_x[...].T
        up_t[...] = up_x[...].T

    out_ref[...] = (dot(down_t[...], down_g[...]) + dot(up_t[...], up_g[...])).astype(bf16)


def weight_gradient(down_x, up_x, down_g, up_g, after=()):
    tokens, depth = down_x.shape
    width = down_g.shape[1]
    tile = width // 4
    whole = pl.BlockSpec((tokens, depth), lambda i: (0, 0))
    part = pl.BlockSpec((tokens, tile), lambda i: (0, i))
    return call(
        weight_kernel,
        (down_x, up_x, down_g, up_g),
        after,
        grid=(width // tile,),
        in_specs=[whole, whole, part, part],
        out_specs=pl.BlockSpec((depth, tile), lambda i: (0, i)),
        out_shape=shape((depth, width), bf16),
        scratch_shapes=[pltpu.VMEM((depth, tokens), bf16)] * 2,
        flops=4 * tokens * depth * width,
        name="weight_gradient",
    )


def finish_kernel(xin_ref, cot_ref, back_ref, *rest):
    *mixed_refs, out_ref = rest
    normed, inverse = normalise(xin_ref[...].astype(f32))
    cot = cot_ref[...].astype(f32)
    returned = jnp.concatenate([back_ref[i] for i in range(back_ref.shape[0])], axis=1)
    mixed = sum(ref[...].astype(f32) for ref in mixed_refs)
    total = cot * mixed + returned.astype(f32)
    mean = jnp.mean(total * normed, axis=1, keepdims=True)
    out_ref[0] = (cot + inverse * (total - normed * mean)).astype(bf16)


def finish(xin, cot, mixed, returned, after=()):
    rows, width = xin.shape
    blocks, _, depth = returned.shape
    step = 64
    spec = pl.BlockSpec((step, width), lambda i: (i, 0))
    return call(
        finish_kernel,
        (xin, cot, returned, *mixed),
        after,
        grid=(rows // step,),
        in_specs=[spec, spec, pl.BlockSpec((blocks, step, depth), lambda i: (0, i, 0))]
        + [spec] * len(mixed),
        out_specs=pl.BlockSpec((1, step, width), lambda i: (0, i, 0)),
        out_shape=shape((1, rows, width), bf16),
        name="finish",
    )


def exchange(x):
    blocks = lax.axis_size("tensor")
    x = x.reshape(blocks, -1, x.shape[-1])
    return lax.all_to_all(x, "tensor", split_axis=0, concat_axis=0, tiled=True)


def both_ways(right, left):
    blocks = lax.axis_size("tensor")
    onward = [(i, i + 1) for i in range(blocks - 1)]
    return (
        lax.ppermute(right, "tensor", onward),
        lax.ppermute(left, "tensor", [(j, i) for i, j in onward]),
    )


def payload_kernel(s, right_ref, left_ref, right_piece, left_piece, right_out, left_out):
    mine = lax.axis_index("tensor")
    blocks = lax.axis_size("tensor")

    def put(came, piece, out, adds):
        @pl.when(adds)
        def _():
            out[...] = (came[...].astype(f32) + piece[...].astype(f32)).astype(bf16)

        @pl.when(jnp.logical_not(adds))
        def _():
            out[...] = came[...]

    put(right_ref, right_piece, right_out, mine < s - 1)
    put(left_ref, left_piece, left_out, mine > blocks - s)


def payload(s, arrived, pieces, after=()):
    blocks = len(pieces)
    rows, width = pieces[0].shape
    step = 64
    spec = pl.BlockSpec((step, width), lambda i: (i, 0))
    return call(
        functools.partial(payload_kernel, s),
        (*arrived, pieces[blocks + 1 - s], pieces[s - 1]),
        after,
        grid=(rows // step,),
        in_specs=[spec] * 4,
        out_specs=[spec] * 2,
        out_shape=[shape((rows, width), bf16)] * 2,
        name="payload",
    )


def sort_arrivals(mix, pieces, arrivals):
    rights, lefts = zip(*arrivals)
    return [mix, *rights[:-1], *lefts[:-1]], [pieces[0], rights[-1], lefts[-1]]


def sum_kernel(*refs):
    *in_refs, out_ref, sorted_ref = refs
    for s, ref in enumerate(in_refs):
        sorted_ref[pl.ds(place(-s), 1)] = ref[...]
    out_ref[...] = sum(sorted_ref[i : i + 1] for i in range(len(in_refs)))


def sum_all(x, after=()):
    blocks = lax.axis_size("tensor")
    terms = [x]
    for s in range(1, blocks):
        terms.append(lax.ppermute(x, "tensor", [(i, (i + s) % blocks) for i in range(blocks)]))
    spec = pl.BlockSpec(x.shape, lambda i: (0,) * x.ndim)
    return call(
        sum_kernel,
        terms,
        after,
        grid=(1,),
        in_specs=[spec] * blocks,
        out_specs=spec,
        out_shape=shape(x.shape, x.dtype),
        scratch_shapes=[pltpu.VMEM((blocks, *x.shape[1:]), x.dtype)],
        name="sum_all",
    )


def per_device(weights, filters, down_input, down_cot, up_input, up_cot):
    sections = lax.axis_size("section")
    mirror = [(s, sections - 1 - s) for s in range(sections)]
    down_pairs = [(s + 1, s) for s in range(sections - 1)]
    up_pairs = [(sections - s, s) for s in range(1, sections)]
    weight = weights[0]
    down_xin, down_cot = down_input[0], down_cot[0]
    up_xin = lax.ppermute(up_input[0], "section", mirror)
    up_cot = lax.ppermute(up_cot[0], "section", mirror)
    blocks = lax.axis_size("tensor")
    depth = weight.shape[0]
    down_normed, down_mix = prepare(down_xin, down_cot)
    down_x = exchange(down_normed).reshape(-1, depth)
    down_arrivals = [both_ways(down_mix, down_mix)]
    causal, ahead = toeplitz(filters[0])
    (up_normed,) = prepare(up_xin, after=(ahead,))
    up_x = exchange(up_normed).reshape(-1, depth)
    up_mix = grad_mix(up_xin, up_cot, after=down_arrivals[0])
    up_arrivals = [both_ways(up_mix, up_mix)]
    down_part, down_pieces = project(down_x, weight, causal, after=(up_normed, up_mix))
    last = down_part
    for s in range(2, blocks + 1):
        sent = payload(s, down_arrivals[-1], down_pieces, after=(last,))
        down_arrivals.append(both_ways(*sent))
        if s == 2:
            up_part, up_pieces = project(up_x, weight, causal, after=sent)
        sent = payload(s, up_arrivals[-1], up_pieces, after=sent)
        up_arrivals.append(both_ways(*sent))
        last = sent[0]
    down_mixes, down_conv = sort_arrivals(down_mix, down_pieces, down_arrivals)
    up_mixes, up_conv = sort_arrivals(up_mix, up_pieces, up_arrivals)
    up_g, up_back = back(up_mixes, weight, ahead, after=(last,))
    up_back = exchange(up_back)
    down_g, down_back = back(
        down_mixes, weight, ahead, after=(up_g, *down_arrivals[-1], *up_arrivals[-1])
    )
    down_back = exchange(down_back)
    up_grad = finish(up_xin, up_cot, up_conv, up_back, after=(down_g,))
    up_passed = lax.ppermute(up_grad, "section", up_pairs)
    taps = filter_gradient(
        down_mixes, down_part, up_mixes, up_part, *filters.shape[1:], after=(up_grad,)
    )
    down_grad = finish(down_xin, down_cot, down_conv, down_back, after=(taps, up_passed))
    down_passed = lax.ppermute(down_grad, "section", down_pairs)
    weight_grad = weight_gradient(down_x, up_x, down_g, up_g, after=(down_grad,))
    taps = sum_all(taps, after=(weight_grad,))
    return weight_grad[None], taps, down_passed, up_passed


def solution(mesh):
    rows = P("section", "tensor", None)
    whole = P("section", None, None)
    return jax.shard_map(
        per_device,
        mesh=mesh,
        in_specs=(rows, whole, rows, rows, rows, rows),
        out_specs=(rows, whole, rows, rows),
        check_vma=False,
    )
```

```python
import functools

import jax
import jax.numpy as jnp
from jax import lax
from jax.experimental import pallas as pl
from jax.experimental.pallas import tpu as pltpu
from jax.sharding import PartitionSpec as P

epsilon = 1e-06
params = functools.partial(pltpu.CompilerParams, vmem_limit_bytes=63 * 1024 * 1024)
f32, bf16 = jnp.float32, jnp.bfloat16


def dot(a, b, dims=((1,), (0,))):
    return lax.dot_general(a, b, (dims, ((), ())), preferred_element_type=f32)


def shape(dims, dtype):
    return jax.ShapeDtypeStruct(dims, dtype)


def call(kernel, args, after, in_specs, out_shape, flops=0, **options):
    count = len(args)
    arrays = [*args, *(out_shape if isinstance(out_shape, list) else [out_shape])]
    cost = pl.CostEstimate(
        flops=flops,
        transcendentals=0,
        bytes_accessed=sum(x.size * x.dtype.itemsize for x in arrays),
    )

    def body(*refs):
        kernel(*refs[:count], *refs[count + len(after) :])

    unread = [pl.BlockSpec(memory_space=pl.ANY)] * len(after)
    return pl.pallas_call(
        body,
        in_specs=list(in_specs) + unread,
        out_shape=out_shape,
        cost_estimate=cost,
        compiler_params=params(),
        **options,
    )(*args, *after)


def toeplitz_kernel(filters_ref, causal_ref, ahead_ref):
    taps = filters_ref.shape[1]
    row = lax.broadcasted_iota(jnp.int32, (taps, taps), 0)
    col = lax.broadcasted_iota(jnp.int32, (taps, taps), 1)
    for g in range(filters_ref.shape[0]):
        line = jnp.broadcast_to(filters_ref[g : g + 1, :], (taps, taps))
        turned = pltpu.roll(line, 0, 1, stride=1, stride_axis=0)
        own = jnp.where(col >= row, turned, 0.0)
        beyond = jnp.where(col < row, turned, 0.0)
        ahead_ref[g, :, :taps] = own.astype(bf16)
        ahead_ref[g, :, taps:] = beyond.astype(bf16)
        causal_ref[g, :, :taps] = beyond.T.astype(bf16)
        causal_ref[g, :, taps:] = own.T.astype(bf16)


def toeplitz(filters):
    groups, taps = filters.shape
    step = 8
    out = shape((groups, taps, 2 * taps), bf16)
    spec = pl.BlockSpec((step, taps, 2 * taps), lambda i: (i, 0, 0))
    return call(
        toeplitz_kernel,
        (filters,),
        (),
        grid=(groups // step,),
        in_specs=[pl.BlockSpec((step, taps), lambda i: (i, 0))],
        out_specs=[spec, spec],
        out_shape=[out, out],
        name="toeplitz",
    )


def place(by):
    blocks = lax.axis_size("tensor")
    return lax.rem(lax.axis_index("tensor") + (by + blocks), blocks)


def window(index, size):
    return pl.ds(pl.multiple_of(index * size, size), size)


def normalise(wide):
    inverse = lax.rsqrt(jnp.mean(wide * wide, axis=1, keepdims=True) + epsilon)
    return wide * inverse, inverse


def prepare_kernel(xin_ref, *refs):
    *cot_ref, normed_ref = refs[: len(refs) // 2 + 1]
    normed, _ = normalise(xin_ref[...].astype(f32))
    width = normed_ref.shape[2]
    for i in range(normed_ref.shape[0]):
        normed_ref[i] = normed[:, i * width : (i + 1) * width].astype(bf16)
    if cot_ref:
        refs[-1][...] = (cot_ref[0][...].astype(f32) * normed).astype(bf16)


def prepare(*args, after=()):
    rows, width = args[0].shape
    blocks = lax.axis_size("tensor")
    step = 64
    spec = pl.BlockSpec((step, width), lambda i: (i, 0))
    normed_spec = pl.BlockSpec((blocks, step, width // blocks), lambda i: (0, i, 0))
    extra = len(args) - 1
    return call(
        prepare_kernel,
        args,
        after,
        grid=(rows // step,),
        in_specs=[spec] * len(args),
        out_specs=[normed_spec] + [spec] * extra,
        out_shape=[shape((blocks, rows, width // blocks), bf16)] + [shape((rows, width), bf16)] * extra,
        name="prepare",
    )


def mix_kernel(xin_ref, cot_ref, mix_ref):
    normed, _ = normalise(xin_ref[...].astype(f32))
    mix_ref[...] = (cot_ref[...].astype(f32) * normed).astype(bf16)


def grad_mix(xin, cot, after=()):
    rows, width = xin.shape
    step = 64
    spec = pl.BlockSpec((step, width), lambda i: (i, 0))
    return call(
        mix_kernel,
        (xin, cot),
        after,
        grid=(rows // step,),
        in_specs=[spec, spec],
        out_specs=spec,
        out_shape=shape((rows, width), bf16),
        name="grad_mix",
    )


def side_by_side(x, rows):
    return jnp.concatenate([x[s : s + rows] for s in range(0, x.shape[0], rows)], axis=1)


def project_kernel(features_ref, weight_ref, causal_ref, part_ref, *rest):
    *mixed_refs, mixed_ref = rest
    groups, taps, _ = causal_ref.shape
    part = dot(features_ref[...], weight_ref[...]).astype(bf16)
    part_ref[...] = part
    width = part.shape[1] // groups
    for g in range(groups):
        cols = slice(g * width, (g + 1) * width)
        own = side_by_side(part[:, cols], taps)
        before = jnp.concatenate([jnp.zeros((taps, width), bf16), own[:, :-width]], axis=1)
        out = dot(causal_ref[g], jnp.concatenate([before, own], axis=0)).astype(bf16)
        for i in range(out.shape[1] // width):
            mixed_ref[i * taps : (i + 1) * taps, cols] = out[:, i * width : (i + 1) * width]
    for s, out_ref in enumerate(mixed_refs):
        out_ref[...] = mixed_ref[window(place(s), out_ref.shape[0]), :]


def project(features, weight, causal, after=()):
    blocks = lax.axis_size("tensor")
    tokens, depth = features.shape
    rows = tokens // blocks
    width = weight.shape[1]
    groups, taps, _ = causal.shape
    step = 8
    tile = width // groups * step
    part, *mixed = call(
        project_kernel,
        (features, weight, causal),
        after,
        grid=(groups // step,),
        in_specs=[
            pl.BlockSpec((tokens, depth), lambda i: (0, 0)),
            pl.BlockSpec((depth, tile), lambda i: (0, i)),
            pl.BlockSpec((step, taps, 2 * taps), lambda i: (i, 0, 0)),
        ],
        out_specs=[pl.BlockSpec((tokens, tile), lambda i: (0, i))]
        + [pl.BlockSpec((rows, tile), lambda i: (0, i))] * blocks,
        out_shape=[shape((tokens, width), bf16)] + [shape((rows, width), bf16)] * blocks,
        scratch_shapes=[pltpu.VMEM((tokens, tile), bf16)],
        flops=2 * tokens * width * (depth + 2 * taps),
        name="project",
    )
    return part, mixed


def assemble(block_refs, mix_ref):
    blocks = (len(block_refs) + 1) // 2
    rows = block_refs[0].shape[0]
    mine = lax.axis_index("tensor")
    mix_ref[window(mine, rows), :] = block_refs[0][...]
    for s in range(1, blocks):

        @pl.when(mine >= s)
        def _():
            mix_ref[window(mine - s, rows), :] = block_refs[s][...]

        @pl.when(mine < s)
        def _():
            mix_ref[window(mine + (blocks - s), rows), :] = block_refs[2 * blocks - 1 - s][...]


def with_following(mix, taps):
    own = side_by_side(mix, taps)
    width = mix.shape[1]
    following = jnp.concatenate([own[:, width:], jnp.zeros((taps, width), bf16)], axis=1)
    return jnp.concatenate([own, following], axis=0)


def back_kernel(count, *refs):
    weight_ref, ahead_ref, grad_ref, back_ref, mix_ref, total = refs[count:]
    groups, taps, _ = ahead_ref.shape
    width = mix_ref.shape[1] // groups
    assemble(refs[:count], mix_ref)
    for g in range(groups):
        cols = slice(g * width, (g + 1) * width)
        out = dot(ahead_ref[g], with_following(mix_ref[:, cols], taps)).astype(bf16)
        for i in range(out.shape[1] // width):
            grad_ref[i * taps : (i + 1) * taps, cols] = out[:, i * width : (i + 1) * width]
    product = dot(grad_ref[...], weight_ref[...], ((1,), (1,)))
    step = pl.program_id(0)

    @pl.when(step == 0)
    def _():
        total[...] = product

    @pl.when(step > 0)
    def _():
        total[...] += product

    @pl.when(step == pl.num_programs(0) - 1)
    def _():
        back_ref[...] = total[...].astype(bf16)


def back(mixes, weight, ahead, after=()):
    rows, width = mixes[0].shape
    tokens = (len(mixes) + 1) // 2 * rows
    depth = weight.shape[0]
    groups, taps, _ = ahead.shape
    step = 8
    tile = width // groups * step
    return call(
        functools.partial(back_kernel, len(mixes)),
        (*mixes, weight, ahead),
        after,
        grid=(groups // step,),
        in_specs=[pl.BlockSpec((rows, tile), lambda i: (0, i))] * len(mixes)
        + [
            pl.BlockSpec((depth, tile), lambda i: (0, i)),
            pl.BlockSpec((step, taps, 2 * taps), lambda i: (i, 0, 0)),
        ],
        out_specs=[
            pl.BlockSpec((tokens, tile), lambda i: (0, i)),
            pl.BlockSpec((tokens, depth), lambda i: (0, 0)),
        ],
        out_shape=[shape((tokens, width), bf16), shape((tokens, depth), bf16)],
        scratch_shapes=[pltpu.VMEM((tokens, tile), bf16), pltpu.VMEM((tokens, depth), f32)],
        flops=6 * tokens * width * (depth + 2 * taps),
        name="back",
    )


def gradients_kernel(count, *refs):
    down_x, up_x, down_g, up_g, *rest = refs[:-6]
    out_ref, taps_ref, down_t, up_t, *mix_refs = refs[-6:]

    @pl.when(pl.program_id(0) == 0)
    def _():
        down_t[...] = down_x[...].T
        up_t[...] = up_x[...].T

    out_ref[...] = (dot(down_t[...], down_g[...]) + dot(up_t[...], up_g[...])).astype(bf16)

    groups, taps = taps_ref.shape[1:]
    width = mix_refs[0].shape[1] // groups
    row = lax.broadcasted_iota(jnp.int32, (taps, taps), 0)
    col = lax.broadcasted_iota(jnp.int32, (taps, taps), 1)
    total = [0] * groups
    for first, mix_ref in zip((0, count + 1), mix_refs):
        assemble(rest[first : first + count], mix_ref)
        part_ref = rest[first + count]
        for g in range(groups):
            cols = slice(g * width, (g + 1) * width)
            both = with_following(mix_ref[:, cols], taps)
            total[g] += dot(side_by_side(part_ref[:, cols], taps), both, ((1,), (1,)))
    for g in range(groups):
        pairs = jnp.where(col >= row, total[g][:, :taps], total[g][:, taps:])
        folded = pairs[0:8]
        for a in range(8, taps, 8):
            folded = folded + pltpu.roll(pairs[a : a + 8], taps - a, 1)
        line = folded[0:1]
        for b in range(1, 8):
            line = line + pltpu.roll(folded[b : b + 1], taps - b, 1)
        taps_ref[0, g : g + 1, :] = line


def gradients(xs, grads, mixes, parts, groups, taps, after=()):
    rows, width = mixes[0][0].shape
    tokens, depth = xs[0].shape
    step = 8
    tile = width // groups * step
    count = len(mixes[0])
    whole = pl.BlockSpec((tokens, depth), lambda i: (0, 0))
    part = pl.BlockSpec((tokens, tile), lambda i: (0, i))
    block = pl.BlockSpec((rows, tile), lambda i: (0, i))
    weight_grad, line = call(
        functools.partial(gradients_kernel, count),
        (*xs, *grads, *mixes[0], parts[0], *mixes[1], parts[1]),
        after,
        grid=(groups // step,),
        in_specs=[whole] * 2 + [part] * 2 + ([block] * count + [part]) * 2,
        out_specs=[
            pl.BlockSpec((depth, tile), lambda i: (0, i)),
            pl.BlockSpec((1, step, taps), lambda i: (i, 0, 0)),
        ],
        out_shape=[shape((depth, width), bf16), shape((groups // step, step, taps), f32)],
        scratch_shapes=[pltpu.VMEM((depth, tokens), bf16)] * 2
        + [pltpu.VMEM((tokens, tile), bf16)] * 2,
        flops=4 * tokens * depth * width + 8 * tokens * width * taps,
        name="gradients",
    )
    return weight_grad, line.reshape(1, groups, taps)


def settle_kernel(in_ref, out_ref):
    out_ref[...] = in_ref[...]


def settle(x):
    step = x.shape[1] // 2
    spec = pl.BlockSpec((1, step, x.shape[2]), lambda i: (0, i, 0))
    return call(
        settle_kernel,
        (x,),
        (),
        grid=(2,),
        in_specs=[spec],
        out_specs=spec,
        out_shape=shape(x.shape, x.dtype),
        name="settle",
    )


def finish_kernel(xin_ref, cot_ref, back_ref, *rest):
    *mixed_refs, out_ref = rest
    normed, inverse = normalise(xin_ref[...].astype(f32))
    cot = cot_ref[...].astype(f32)
    returned = jnp.concatenate([back_ref[i] for i in range(back_ref.shape[0])], axis=1)
    mixed = sum(ref[...].astype(f32) for ref in mixed_refs)
    total = cot * mixed + returned.astype(f32)
    mean = jnp.mean(total * normed, axis=1, keepdims=True)
    out_ref[0] = (cot + inverse * (total - normed * mean)).astype(bf16)


def finish(xin, cot, mixed, returned, after=()):
    rows, width = xin.shape
    blocks, _, depth = returned.shape
    step = 64
    spec = pl.BlockSpec((step, width), lambda i: (i, 0))
    return call(
        finish_kernel,
        (xin, cot, returned, *mixed),
        after,
        grid=(rows // step,),
        in_specs=[spec, spec, pl.BlockSpec((blocks, step, depth), lambda i: (0, i, 0))]
        + [spec] * len(mixed),
        out_specs=pl.BlockSpec((1, step, width), lambda i: (0, i, 0)),
        out_shape=shape((1, rows, width), bf16),
        name="finish",
    )


def exchange(x):
    blocks = lax.axis_size("tensor")
    x = x.reshape(blocks, -1, x.shape[-1])
    return lax.all_to_all(x, "tensor", split_axis=0, concat_axis=0, tiled=True)


def both_ways(right, left):
    blocks = lax.axis_size("tensor")
    onward = [(i, i + 1) for i in range(blocks - 1)]
    return (
        lax.ppermute(right, "tensor", onward),
        lax.ppermute(left, "tensor", [(j, i) for i, j in onward]),
    )


def payload_kernel(s, right_ref, left_ref, right_piece, left_piece, right_out, left_out):
    mine = lax.axis_index("tensor")
    blocks = lax.axis_size("tensor")

    def put(came, piece, out, adds):
        @pl.when(adds)
        def _():
            out[...] = (came[...].astype(f32) + piece[...].astype(f32)).astype(bf16)

        @pl.when(jnp.logical_not(adds))
        def _():
            out[...] = came[...]

    put(right_ref, right_piece, right_out, mine < s - 1)
    put(left_ref, left_piece, left_out, mine > blocks - s)


def payload(s, arrived, pieces, after=()):
    blocks = len(pieces)
    rows, width = pieces[0].shape
    step = 64
    spec = pl.BlockSpec((step, width), lambda i: (i, 0))
    return call(
        functools.partial(payload_kernel, s),
        (*arrived, pieces[blocks + 1 - s], pieces[s - 1]),
        after,
        grid=(rows // step,),
        in_specs=[spec] * 4,
        out_specs=[spec] * 2,
        out_shape=[shape((rows, width), bf16)] * 2,
        name="payload",
    )


def sort_arrivals(mix, pieces, arrivals):
    rights, lefts = zip(*arrivals)
    return [mix, *rights[:-1], *lefts[:-1]], [pieces[0], rights[-1], lefts[-1]]


def sum_kernel(*refs):
    *in_refs, out_ref, sorted_ref = refs
    for s, ref in enumerate(in_refs):
        sorted_ref[pl.ds(place(-s), 1)] = ref[...]
    out_ref[...] = sum(sorted_ref[i : i + 1] for i in range(len(in_refs)))


def sum_all(x, after=()):
    blocks = lax.axis_size("tensor")
    terms = [x]
    for s in range(1, blocks):
        terms.append(lax.ppermute(x, "tensor", [(i, (i + s) % blocks) for i in range(blocks)]))
    spec = pl.BlockSpec(x.shape, lambda i: (0,) * x.ndim)
    return call(
        sum_kernel,
        terms,
        after,
        grid=(1,),
        in_specs=[spec] * blocks,
        out_specs=spec,
        out_shape=shape(x.shape, x.dtype),
        scratch_shapes=[pltpu.VMEM((blocks, *x.shape[1:]), x.dtype)],
        name="sum_all",
    )


def per_device(weights, filters, down_input, down_cot, up_input, up_cot):
    sections = lax.axis_size("section")
    mirror = [(s, sections - 1 - s) for s in range(sections)]
    down_pairs = [(s + 1, s) for s in range(sections - 1)]
    up_pairs = [(sections - s, s) for s in range(1, sections)]
    weight = weights[0]
    down_xin, down_cot = down_input[0], down_cot[0]
    up_xin = lax.ppermute(up_input[0], "section", mirror)
    up_cot = lax.ppermute(up_cot[0], "section", mirror)
    blocks = lax.axis_size("tensor")
    depth = weight.shape[0]
    down_normed, down_mix = prepare(down_xin, down_cot)
    down_x = exchange(down_normed).reshape(-1, depth)
    down_arrivals = [both_ways(down_mix, down_mix)]
    causal, ahead = toeplitz(filters[0])
    (up_normed,) = prepare(up_xin, after=(ahead,))
    up_x = exchange(up_normed).reshape(-1, depth)
    up_mix = grad_mix(up_xin, up_cot, after=down_arrivals[0])
    up_arrivals = [both_ways(up_mix, up_mix)]
    down_part, down_pieces = project(down_x, weight, causal, after=(up_normed, up_mix))
    last = down_part
    for s in range(2, blocks + 1):
        sent = payload(s, down_arrivals[-1], down_pieces, after=(last,))
        down_arrivals.append(both_ways(*sent))
        if s == 2:
            up_part, up_pieces = project(up_x, weight, causal, after=sent)
        sent = payload(s, up_arrivals[-1], up_pieces, after=sent)
        up_arrivals.append(both_ways(*sent))
        last = sent[0]
    down_mixes, down_conv = sort_arrivals(down_mix, down_pieces, down_arrivals)
    up_mixes, up_conv = sort_arrivals(up_mix, up_pieces, up_arrivals)
    up_g, up_back = back(up_mixes, weight, ahead, after=(last,))
    up_back = exchange(up_back)
    down_g, down_back = back(
        down_mixes, weight, ahead, after=(up_g, *down_arrivals[-1], *up_arrivals[-1])
    )
    down_back = exchange(down_back)
    up_grad = finish(up_xin, up_cot, up_conv, up_back, after=(down_g,))
    up_passed = lax.ppermute(up_grad, "section", up_pairs)
    weight_grad, taps = gradients(
        (down_x, up_x),
        (down_g, up_g),
        (down_mixes, up_mixes),
        (down_part, up_part),
        *filters.shape[1:],
        after=(up_grad,),
    )
    up_passed = settle(up_passed)
    down_grad = finish(
        down_xin, down_cot, down_conv, down_back, after=(weight_grad, up_passed)
    )
    down_passed = lax.ppermute(down_grad, "section", down_pairs)
    taps = sum_all(taps, after=(down_grad,))
    return weight_grad[None], taps, down_passed, up_passed


def solution(mesh):
    rows = P("section", "tensor", None)
    whole = P("section", None, None)
    return jax.shard_map(
        per_device,
        mesh=mesh,
        in_specs=(rows, whole, rows, rows, rows, rows),
        out_specs=(rows, whole, rows, rows),
        check_vma=False,
    )
```

```python
import functools

import jax
import jax.numpy as jnp
from jax import lax
from jax.experimental import pallas as pl
from jax.experimental.pallas import tpu as pltpu
from jax.sharding import PartitionSpec as P

epsilon = 1e-06
params = functools.partial(pltpu.CompilerParams, vmem_limit_bytes=63 * 1024 * 1024)
f32, bf16 = jnp.float32, jnp.bfloat16


def dot(a, b, dims=((1,), (0,))):
    return lax.dot_general(a, b, (dims, ((), ())), preferred_element_type=f32)


def shape(dims, dtype):
    return jax.ShapeDtypeStruct(dims, dtype)


def call(kernel, args, after, in_specs, out_shape, flops=0, counted=True, **options):
    count = len(args)
    arrays = [*args, *(out_shape if isinstance(out_shape, list) else [out_shape])]
    cost = pl.CostEstimate(
        flops=flops,
        transcendentals=0,
        bytes_accessed=counted * sum(x.size * x.dtype.itemsize for x in arrays),
    )

    def body(*refs):
        kernel(*refs[:count], *refs[count + len(after) :])

    unread = [pl.BlockSpec(memory_space=pl.ANY)] * len(after)
    return pl.pallas_call(
        body,
        in_specs=list(in_specs) + unread,
        out_shape=out_shape,
        cost_estimate=cost,
        compiler_params=params(),
        **options,
    )(*args, *after)


def toeplitz_kernel(filters_ref, causal_ref, ahead_ref):
    taps = filters_ref.shape[1]
    row = lax.broadcasted_iota(jnp.int32, (taps, taps), 0)
    col = lax.broadcasted_iota(jnp.int32, (taps, taps), 1)
    for g in range(filters_ref.shape[0]):
        line = jnp.broadcast_to(filters_ref[g : g + 1, :], (taps, taps))
        turned = pltpu.roll(line, 0, 1, stride=1, stride_axis=0)
        own = jnp.where(col >= row, turned, 0.0)
        beyond = jnp.where(col < row, turned, 0.0)
        ahead_ref[g, :, :taps] = own.astype(bf16)
        ahead_ref[g, :, taps:] = beyond.astype(bf16)
        causal_ref[g, :, :taps] = beyond.T.astype(bf16)
        causal_ref[g, :, taps:] = own.T.astype(bf16)


def toeplitz(filters):
    groups, taps = filters.shape
    step = 8
    out = shape((groups, taps, 2 * taps), bf16)
    spec = pl.BlockSpec((step, taps, 2 * taps), lambda i: (i, 0, 0))
    return call(
        toeplitz_kernel,
        (filters,),
        (),
        grid=(groups // step,),
        in_specs=[pl.BlockSpec((step, taps), lambda i: (i, 0))],
        out_specs=[spec, spec],
        out_shape=[out, out],
        name="toeplitz",
    )


def place(by):
    blocks = lax.axis_size("tensor")
    return lax.rem(lax.axis_index("tensor") + (by + blocks), blocks)


def window(index, size):
    return pl.ds(pl.multiple_of(index * size, size), size)


def normalise(wide):
    inverse = lax.rsqrt(jnp.mean(wide * wide, axis=1, keepdims=True) + epsilon)
    return wide * inverse, inverse


def prepare_kernel(xin_ref, *refs):
    *cot_ref, normed_ref = refs[: len(refs) // 2 + 1]
    normed, _ = normalise(xin_ref[...].astype(f32))
    width = normed_ref.shape[2]
    for i in range(normed_ref.shape[0]):
        normed_ref[i] = normed[:, i * width : (i + 1) * width].astype(bf16)
    if cot_ref:
        refs[-1][...] = (cot_ref[0][...].astype(f32) * normed).astype(bf16)


def prepare(*args, after=()):
    rows, width = args[0].shape
    blocks = lax.axis_size("tensor")
    step = 64
    spec = pl.BlockSpec((step, width), lambda i: (i, 0))
    normed_spec = pl.BlockSpec((blocks, step, width // blocks), lambda i: (0, i, 0))
    extra = len(args) - 1
    return call(
        prepare_kernel,
        args,
        after,
        grid=(rows // step,),
        in_specs=[spec] * len(args),
        out_specs=[normed_spec] + [spec] * extra,
        out_shape=[shape((blocks, rows, width // blocks), bf16)] + [shape((rows, width), bf16)] * extra,
        name="prepare",
    )


def mix_kernel(xin_ref, cot_ref, mix_ref):
    normed, _ = normalise(xin_ref[...].astype(f32))
    mix_ref[...] = (cot_ref[...].astype(f32) * normed).astype(bf16)


def grad_mix(xin, cot, after=()):
    rows, width = xin.shape
    step = 64
    spec = pl.BlockSpec((step, width), lambda i: (i, 0))
    return call(
        mix_kernel,
        (xin, cot),
        after,
        grid=(rows // step,),
        in_specs=[spec, spec],
        out_specs=spec,
        out_shape=shape((rows, width), bf16),
        name="grad_mix",
    )


def side_by_side(x, rows):
    return jnp.concatenate([x[s : s + rows] for s in range(0, x.shape[0], rows)], axis=1)


def project_kernel(features_ref, weight_ref, causal_ref, part_ref, *rest):
    *mixed_refs, mixed_ref = rest
    groups, taps, _ = causal_ref.shape
    part = dot(features_ref[...], weight_ref[...]).astype(bf16)
    part_ref[...] = part
    width = part.shape[1] // groups
    for g in range(groups):
        cols = slice(g * width, (g + 1) * width)
        own = side_by_side(part[:, cols], taps)
        before = jnp.concatenate([jnp.zeros((taps, width), bf16), own[:, :-width]], axis=1)
        out = dot(causal_ref[g], jnp.concatenate([before, own], axis=0)).astype(bf16)
        for i in range(out.shape[1] // width):
            mixed_ref[i * taps : (i + 1) * taps, cols] = out[:, i * width : (i + 1) * width]
    for s, out_ref in enumerate(mixed_refs):
        out_ref[...] = mixed_ref[window(place(s), out_ref.shape[0]), :]


def project(features, weight, causal, after=()):
    blocks = lax.axis_size("tensor")
    tokens, depth = features.shape
    rows = tokens // blocks
    width = weight.shape[1]
    groups, taps, _ = causal.shape
    step = 8
    tile = width // groups * step
    part, *mixed = call(
        project_kernel,
        (features, weight, causal),
        after,
        grid=(groups // step,),
        in_specs=[
            pl.BlockSpec((tokens, depth), lambda i: (0, 0)),
            pl.BlockSpec((depth, tile), lambda i: (0, i)),
            pl.BlockSpec((step, taps, 2 * taps), lambda i: (i, 0, 0)),
        ],
        out_specs=[pl.BlockSpec((tokens, tile), lambda i: (0, i))]
        + [pl.BlockSpec((rows, tile), lambda i: (0, i))] * blocks,
        out_shape=[shape((tokens, width), bf16)] + [shape((rows, width), bf16)] * blocks,
        scratch_shapes=[pltpu.VMEM((tokens, tile), bf16)],
        flops=2 * tokens * width * (depth + 2 * taps),
        name="project",
    )
    return part, mixed


def assemble(block_refs, mix_ref):
    blocks = (len(block_refs) + 1) // 2
    rows = block_refs[0].shape[0]
    mine = lax.axis_index("tensor")
    mix_ref[window(mine, rows), :] = block_refs[0][...]
    for s in range(1, blocks):

        @pl.when(mine >= s)
        def _():
            mix_ref[window(mine - s, rows), :] = block_refs[s][...]

        @pl.when(mine < s)
        def _():
            mix_ref[window(mine + (blocks - s), rows), :] = block_refs[2 * blocks - 1 - s][...]


def with_following(mix, taps):
    own = side_by_side(mix, taps)
    width = mix.shape[1]
    following = jnp.concatenate([own[:, width:], jnp.zeros((taps, width), bf16)], axis=1)
    return jnp.concatenate([own, following], axis=0)


def back_kernel(count, *refs):
    weight_ref, ahead_ref, grad_ref, back_ref, mix_ref, total = refs[count:]
    groups, taps, _ = ahead_ref.shape
    width = mix_ref.shape[1] // groups
    assemble(refs[:count], mix_ref)
    for g in range(groups):
        cols = slice(g * width, (g + 1) * width)
        out = dot(ahead_ref[g], with_following(mix_ref[:, cols], taps)).astype(bf16)
        for i in range(out.shape[1] // width):
            grad_ref[i * taps : (i + 1) * taps, cols] = out[:, i * width : (i + 1) * width]
    product = dot(grad_ref[...], weight_ref[...], ((1,), (1,)))
    step = pl.program_id(0)

    @pl.when(step == 0)
    def _():
        total[...] = product

    @pl.when(step > 0)
    def _():
        total[...] += product

    @pl.when(step == pl.num_programs(0) - 1)
    def _():
        back_ref[...] = total[...].astype(bf16)


def back(mixes, weight, ahead, after=()):
    rows, width = mixes[0].shape
    tokens = (len(mixes) + 1) // 2 * rows
    depth = weight.shape[0]
    groups, taps, _ = ahead.shape
    step = 8
    tile = width // groups * step
    return call(
        functools.partial(back_kernel, len(mixes)),
        (*mixes, weight, ahead),
        after,
        grid=(groups // step,),
        in_specs=[pl.BlockSpec((rows, tile), lambda i: (0, i))] * len(mixes)
        + [
            pl.BlockSpec((depth, tile), lambda i: (0, i)),
            pl.BlockSpec((step, taps, 2 * taps), lambda i: (i, 0, 0)),
        ],
        out_specs=[
            pl.BlockSpec((tokens, tile), lambda i: (0, i)),
            pl.BlockSpec((tokens, depth), lambda i: (0, 0)),
        ],
        out_shape=[shape((tokens, width), bf16), shape((tokens, depth), bf16)],
        scratch_shapes=[pltpu.VMEM((tokens, tile), bf16), pltpu.VMEM((tokens, depth), f32)],
        flops=6 * tokens * width * (depth + 2 * taps),
        name="back",
    )


def taps_kernel(count, groups, *refs):
    taps_ref, *mix_refs = refs[-3:]
    taps = taps_ref.shape[2]
    width = mix_refs[0].shape[1] // groups
    row = lax.broadcasted_iota(jnp.int32, (taps, taps), 0)
    col = lax.broadcasted_iota(jnp.int32, (taps, taps), 1)
    total = [0] * groups
    for first, mix_ref in zip((0, count + 1), mix_refs):
        assemble(refs[first : first + count], mix_ref)
        part_ref = refs[first + count]
        for g in range(groups):
            cols = slice(g * width, (g + 1) * width)
            both = with_following(mix_ref[:, cols], taps)
            total[g] += dot(side_by_side(part_ref[:, cols], taps), both, ((1,), (1,)))
    for g in range(groups):
        pairs = jnp.where(col >= row, total[g][:, :taps], total[g][:, taps:])
        folded = pairs[0:8]
        for a in range(8, taps, 8):
            folded = folded + pltpu.roll(pairs[a : a + 8], taps - a, 1)
        line = folded[0:1]
        for b in range(1, 8):
            line = line + pltpu.roll(folded[b : b + 1], taps - b, 1)
        taps_ref[0, g : g + 1, :] = line


def filter_gradient(down_mixes, down_part, up_mixes, up_part, groups, taps, after=()):
    rows, width = down_mixes[0].shape
    tokens = down_part.shape[0]
    step = 8
    tile = width // groups * step
    count = len(down_mixes)
    block = [pl.BlockSpec((rows, tile), lambda i: (0, i))] * count
    part = [pl.BlockSpec((tokens, tile), lambda i: (0, i))]
    return call(
        functools.partial(taps_kernel, count, step),
        (*down_mixes, down_part, *up_mixes, up_part),
        after,
        grid=(groups // step,),
        in_specs=(block + part) * 2,
        out_specs=pl.BlockSpec((1, step, taps), lambda i: (i, 0, 0)),
        out_shape=shape((groups // step, step, taps), f32),
        scratch_shapes=[pltpu.VMEM((tokens, tile), bf16)] * 2,
        counted=False,
        name="filter_gradient",
    ).reshape(1, groups, taps)


def weight_kernel(down_x, up_x, down_g, up_g, out_ref, down_t, up_t):
    @pl.when(pl.program_id(0) == 0)
    def _():
        down_t[...] = down_x[...].T
        up_t[...] = up_x[...].T

    out_ref[...] = (dot(down_t[...], down_g[...]) + dot(up_t[...], up_g[...])).astype(bf16)


def weight_gradient(down_x, up_x, down_g, up_g, after=()):
    tokens, depth = down_x.shape
    width = down_g.shape[1]
    tile = width // 4
    whole = pl.BlockSpec((tokens, depth), lambda i: (0, 0))
    part = pl.BlockSpec((tokens, tile), lambda i: (0, i))
    return call(
        weight_kernel,
        (down_x, up_x, down_g, up_g),
        after,
        grid=(width // tile,),
        in_specs=[whole, whole, part, part],
        out_specs=pl.BlockSpec((depth, tile), lambda i: (0, i)),
        out_shape=shape((depth, width), bf16),
        scratch_shapes=[pltpu.VMEM((depth, tokens), bf16)] * 2,
        flops=4 * tokens * depth * width,
        name="weight_gradient",
    )


def settle_kernel(own_ref, came_ref, out_ref):
    stays = 2 * lax.axis_index("section") == lax.axis_size("section")

    @pl.when(stays)
    def _():
        out_ref[...] = own_ref[...]

    @pl.when(jnp.logical_not(stays))
    def _():
        out_ref[...] = came_ref[...]


def settle(own, came):
    step = came.shape[1] // 2
    spec = pl.BlockSpec((1, step, came.shape[2]), lambda i: (0, i, 0))
    return call(
        settle_kernel,
        (own, came),
        (),
        grid=(2,),
        in_specs=[spec, spec],
        out_specs=spec,
        out_shape=shape(came.shape, came.dtype),
        name="settle",
    )


def finish_kernel(xin_ref, cot_ref, back_ref, *rest):
    *mixed_refs, out_ref = rest
    normed, inverse = normalise(xin_ref[...].astype(f32))
    cot = cot_ref[...].astype(f32)
    returned = jnp.concatenate([back_ref[i] for i in range(back_ref.shape[0])], axis=1)
    mixed = sum(ref[...].astype(f32) for ref in mixed_refs)
    total = cot * mixed + returned.astype(f32)
    mean = jnp.mean(total * normed, axis=1, keepdims=True)
    out_ref[0] = (cot + inverse * (total - normed * mean)).astype(bf16)


def finish(xin, cot, mixed, returned, after=()):
    rows, width = xin.shape
    blocks, _, depth = returned.shape
    step = 64
    spec = pl.BlockSpec((step, width), lambda i: (i, 0))
    return call(
        finish_kernel,
        (xin, cot, returned, *mixed),
        after,
        grid=(rows // step,),
        in_specs=[spec, spec, pl.BlockSpec((blocks, step, depth), lambda i: (0, i, 0))]
        + [spec] * len(mixed),
        out_specs=pl.BlockSpec((1, step, width), lambda i: (0, i, 0)),
        out_shape=shape((1, rows, width), bf16),
        name="finish",
    )


def exchange(x):
    blocks = lax.axis_size("tensor")
    x = x.reshape(blocks, -1, x.shape[-1])
    return lax.all_to_all(x, "tensor", split_axis=0, concat_axis=0, tiled=True)


def both_ways(right, left):
    blocks = lax.axis_size("tensor")
    onward = [(i, i + 1) for i in range(blocks - 1)]
    return (
        lax.ppermute(right, "tensor", onward),
        lax.ppermute(left, "tensor", [(j, i) for i, j in onward]),
    )


def payload_kernel(s, right_ref, left_ref, right_piece, left_piece, right_out, left_out):
    mine = lax.axis_index("tensor")
    blocks = lax.axis_size("tensor")

    def put(came, piece, out, adds):
        @pl.when(adds)
        def _():
            out[...] = (came[...].astype(f32) + piece[...].astype(f32)).astype(bf16)

        @pl.when(jnp.logical_not(adds))
        def _():
            out[...] = came[...]

    put(right_ref, right_piece, right_out, mine < s - 1)
    put(left_ref, left_piece, left_out, mine > blocks - s)


def payload(s, arrived, pieces, after=()):
    blocks = len(pieces)
    rows, width = pieces[0].shape
    step = 64
    spec = pl.BlockSpec((step, width), lambda i: (i, 0))
    return call(
        functools.partial(payload_kernel, s),
        (*arrived, pieces[blocks + 1 - s], pieces[s - 1]),
        after,
        grid=(rows // step,),
        in_specs=[spec] * 4,
        out_specs=[spec] * 2,
        out_shape=[shape((rows, width), bf16)] * 2,
        name="payload",
    )


def sort_arrivals(mix, pieces, arrivals):
    rights, lefts = zip(*arrivals)
    return [mix, *rights[:-1], *lefts[:-1]], [pieces[0], rights[-1], lefts[-1]]


def sum_kernel(*refs):
    *in_refs, out_ref, sorted_ref = refs
    for s, ref in enumerate(in_refs):
        sorted_ref[pl.ds(place(-s), 1)] = ref[...]
    out_ref[...] = sum(sorted_ref[i : i + 1] for i in range(len(in_refs)))


def sum_all(x, after=()):
    blocks = lax.axis_size("tensor")
    terms = [x]
    for s in range(1, blocks):
        terms.append(lax.ppermute(x, "tensor", [(i, (i + s) % blocks) for i in range(blocks)]))
    spec = pl.BlockSpec(x.shape, lambda i: (0,) * x.ndim)
    return call(
        sum_kernel,
        terms,
        after,
        grid=(1,),
        in_specs=[spec] * blocks,
        out_specs=spec,
        out_shape=shape(x.shape, x.dtype),
        scratch_shapes=[pltpu.VMEM((blocks, *x.shape[1:]), x.dtype)],
        name="sum_all",
    )


def per_device(weights, filters, down_input, down_cot, up_input, up_cot):
    sections = lax.axis_size("section")
    mirror = [(s, sections - 1 - s) for s in range(sections)]
    down_pairs = [(s + 1, s) for s in range(sections - 1)]
    up_pairs = [(sections - s, s) for s in range(1, sections) if 2 * s != sections]
    weight = weights[0]
    down_xin, down_cot = down_input[0], down_cot[0]
    up_xin = lax.ppermute(up_input[0], "section", mirror)
    up_cot = lax.ppermute(up_cot[0], "section", mirror)
    blocks = lax.axis_size("tensor")
    depth = weight.shape[0]
    down_normed, down_mix = prepare(down_xin, down_cot)
    down_x = exchange(down_normed).reshape(-1, depth)
    down_arrivals = [both_ways(down_mix, down_mix)]
    causal, ahead = toeplitz(filters[0])
    (up_normed,) = prepare(up_xin, after=(ahead,))
    up_x = exchange(up_normed).reshape(-1, depth)
    up_mix = grad_mix(up_xin, up_cot, after=down_arrivals[0])
    up_arrivals = [both_ways(up_mix, up_mix)]
    down_part, down_pieces = project(down_x, weight, causal, after=(up_normed, up_mix))
    last = down_part
    for s in range(2, blocks + 1):
        sent = payload(s, down_arrivals[-1], down_pieces, after=(last,))
        down_arrivals.append(both_ways(*sent))
        if s == 2:
            up_part, up_pieces = project(up_x, weight, causal, after=sent)
        sent = payload(s, up_arrivals[-1], up_pieces, after=sent)
        up_arrivals.append(both_ways(*sent))
        last = sent[0]
    down_mixes, down_conv = sort_arrivals(down_mix, down_pieces, down_arrivals)
    up_mixes, up_conv = sort_arrivals(up_mix, up_pieces, up_arrivals)
    up_g, up_back = back(up_mixes, weight, ahead, after=(last,))
    up_back = exchange(up_back)
    taps = filter_gradient(
        down_mixes, down_part, up_mixes, up_part, *filters.shape[1:], after=(up_g,)
    )
    down_g, down_back = back(
        down_mixes, weight, ahead, after=(taps, *down_arrivals[-1], *up_arrivals[-1])
    )
    down_back = exchange(down_back)
    up_grad = finish(up_xin, up_cot, up_conv, up_back, after=(down_g,))
    up_passed = lax.ppermute(up_grad, "section", up_pairs)
    weight_grad = weight_gradient(down_x, up_x, down_g, up_g, after=(up_grad,))
    up_passed = settle(up_grad, up_passed)
    down_grad = finish(
        down_xin, down_cot, down_conv, down_back, after=(weight_grad, up_passed)
    )
    down_passed = lax.ppermute(down_grad, "section", down_pairs)
    taps = sum_all(taps, after=(down_grad,))
    return weight_grad[None], taps, down_passed, up_passed


def solution(mesh):
    rows = P("section", "tensor", None)
    whole = P("section", None, None)
    return jax.shard_map(
        per_device,
        mesh=mesh,
        in_specs=(rows, whole, rows, rows, rows, rows),
        out_specs=(rows, whole, rows, rows),
        check_vma=False,
    )
```

```python
import functools

import jax
import jax.numpy as jnp
from jax import lax
from jax.experimental import pallas as pl
from jax.experimental.pallas import tpu as pltpu
from jax.sharding import PartitionSpec as P

epsilon = 1e-06
params = functools.partial(pltpu.CompilerParams, vmem_limit_bytes=63 * 1024 * 1024)
f32, bf16 = jnp.float32, jnp.bfloat16


def dot(a, b, dims=((1,), (0,))):
    return lax.dot_general(a, b, (dims, ((), ())), preferred_element_type=f32)


def shape(dims, dtype):
    return jax.ShapeDtypeStruct(dims, dtype)


def call(kernel, args, after, in_specs, out_shape, flops=0, counted=True, **options):
    count = len(args)
    arrays = [*args, *(out_shape if isinstance(out_shape, list) else [out_shape])]
    cost = pl.CostEstimate(
        flops=flops,
        transcendentals=0,
        bytes_accessed=counted * sum(x.size * x.dtype.itemsize for x in arrays),
    )

    def body(*refs):
        kernel(*refs[:count], *refs[count + len(after) :])

    unread = [pl.BlockSpec(memory_space=pl.ANY)] * len(after)
    return pl.pallas_call(
        body,
        in_specs=list(in_specs) + unread,
        out_shape=out_shape,
        cost_estimate=cost,
        compiler_params=params(),
        **options,
    )(*args, *after)


def toeplitz_kernel(filters_ref, causal_ref, ahead_ref):
    taps = filters_ref.shape[1]
    row = lax.broadcasted_iota(jnp.int32, (taps, taps), 0)
    col = lax.broadcasted_iota(jnp.int32, (taps, taps), 1)
    for g in range(filters_ref.shape[0]):
        line = jnp.broadcast_to(filters_ref[g : g + 1, :], (taps, taps))
        turned = pltpu.roll(line, 0, 1, stride=1, stride_axis=0)
        own = jnp.where(col >= row, turned, 0.0)
        beyond = jnp.where(col < row, turned, 0.0)
        ahead_ref[g, :, :taps] = own.astype(bf16)
        ahead_ref[g, :, taps:] = beyond.astype(bf16)
        causal_ref[g, :, :taps] = beyond.T.astype(bf16)
        causal_ref[g, :, taps:] = own.T.astype(bf16)


def toeplitz(filters):
    groups, taps = filters.shape
    step = 8
    out = shape((groups, taps, 2 * taps), bf16)
    spec = pl.BlockSpec((step, taps, 2 * taps), lambda i: (i, 0, 0))
    return call(
        toeplitz_kernel,
        (filters,),
        (),
        grid=(groups // step,),
        in_specs=[pl.BlockSpec((step, taps), lambda i: (i, 0))],
        out_specs=[spec, spec],
        out_shape=[out, out],
        name="toeplitz",
    )


def place(by):
    blocks = lax.axis_size("tensor")
    return lax.rem(lax.axis_index("tensor") + (by + blocks), blocks)


def window(index, size):
    return pl.ds(pl.multiple_of(index * size, size), size)


def normalise(wide):
    inverse = lax.rsqrt(jnp.mean(wide * wide, axis=1, keepdims=True) + epsilon)
    return wide * inverse, inverse


def prepare_kernel(xin_ref, *refs):
    *cot_ref, normed_ref = refs[: len(refs) // 2 + 1]
    normed, _ = normalise(xin_ref[...].astype(f32))
    width = normed_ref.shape[2]
    for i in range(normed_ref.shape[0]):
        normed_ref[i] = normed[:, i * width : (i + 1) * width].astype(bf16)
    if cot_ref:
        refs[-1][...] = (cot_ref[0][...].astype(f32) * normed).astype(bf16)


def prepare(*args, after=()):
    rows, width = args[0].shape
    blocks = lax.axis_size("tensor")
    step = 64
    spec = pl.BlockSpec((step, width), lambda i: (i, 0))
    normed_spec = pl.BlockSpec((blocks, step, width // blocks), lambda i: (0, i, 0))
    extra = len(args) - 1
    return call(
        prepare_kernel,
        args,
        after,
        grid=(rows // step,),
        in_specs=[spec] * len(args),
        out_specs=[normed_spec] + [spec] * extra,
        out_shape=[shape((blocks, rows, width // blocks), bf16)] + [shape((rows, width), bf16)] * extra,
        name="prepare",
    )


def mix_kernel(xin_ref, cot_ref, mix_ref):
    normed, _ = normalise(xin_ref[...].astype(f32))
    mix_ref[...] = (cot_ref[...].astype(f32) * normed).astype(bf16)


def grad_mix(xin, cot, after=()):
    rows, width = xin.shape
    step = 64
    spec = pl.BlockSpec((step, width), lambda i: (i, 0))
    return call(
        mix_kernel,
        (xin, cot),
        after,
        grid=(rows // step,),
        in_specs=[spec, spec],
        out_specs=spec,
        out_shape=shape((rows, width), bf16),
        name="grad_mix",
    )


def side_by_side(x, rows):
    return jnp.concatenate([x[s : s + rows] for s in range(0, x.shape[0], rows)], axis=1)


def project_kernel(features_ref, weight_ref, causal_ref, part_ref, *rest):
    *mixed_refs, mixed_ref = rest
    groups, taps, _ = causal_ref.shape
    part = dot(features_ref[...], weight_ref[...]).astype(bf16)
    part_ref[...] = part
    width = part.shape[1] // groups
    for g in range(groups):
        cols = slice(g * width, (g + 1) * width)
        own = side_by_side(part[:, cols], taps)
        before = jnp.concatenate([jnp.zeros((taps, width), bf16), own[:, :-width]], axis=1)
        out = dot(causal_ref[g], jnp.concatenate([before, own], axis=0)).astype(bf16)
        for i in range(out.shape[1] // width):
            mixed_ref[i * taps : (i + 1) * taps, cols] = out[:, i * width : (i + 1) * width]
    for s, out_ref in enumerate(mixed_refs):
        out_ref[...] = mixed_ref[window(place(s), out_ref.shape[0]), :]


def project(features, weight, causal, after=()):
    blocks = lax.axis_size("tensor")
    tokens, depth = features.shape
    rows = tokens // blocks
    width = weight.shape[1]
    groups, taps, _ = causal.shape
    step = 8
    tile = width // groups * step
    part, *mixed = call(
        project_kernel,
        (features, weight, causal),
        after,
        grid=(groups // step,),
        in_specs=[
            pl.BlockSpec((tokens, depth), lambda i: (0, 0)),
            pl.BlockSpec((depth, tile), lambda i: (0, i)),
            pl.BlockSpec((step, taps, 2 * taps), lambda i: (i, 0, 0)),
        ],
        out_specs=[pl.BlockSpec((tokens, tile), lambda i: (0, i))]
        + [pl.BlockSpec((rows, tile), lambda i: (0, i))] * blocks,
        out_shape=[shape((tokens, width), bf16)] + [shape((rows, width), bf16)] * blocks,
        scratch_shapes=[pltpu.VMEM((tokens, tile), bf16)],
        flops=2 * tokens * width * (depth + 2 * taps),
        name="project",
    )
    return part, mixed


def assemble(block_refs, mix_ref):
    blocks = (len(block_refs) + 1) // 2
    rows = block_refs[0].shape[0]
    mine = lax.axis_index("tensor")
    mix_ref[window(mine, rows), :] = block_refs[0][...]
    for s in range(1, blocks):

        @pl.when(mine >= s)
        def _():
            mix_ref[window(mine - s, rows), :] = block_refs[s][...]

        @pl.when(mine < s)
        def _():
            mix_ref[window(mine + (blocks - s), rows), :] = block_refs[2 * blocks - 1 - s][...]


def with_following(mix, taps):
    own = side_by_side(mix, taps)
    width = mix.shape[1]
    following = jnp.concatenate([own[:, width:], jnp.zeros((taps, width), bf16)], axis=1)
    return jnp.concatenate([own, following], axis=0)


def back_kernel(count, *refs):
    weight_ref, ahead_ref, grad_ref, back_ref, mix_ref, total = refs[count:]
    groups, taps, _ = ahead_ref.shape
    width = mix_ref.shape[1] // groups
    assemble(refs[:count], mix_ref)
    for g in range(groups):
        cols = slice(g * width, (g + 1) * width)
        out = dot(ahead_ref[g], with_following(mix_ref[:, cols], taps)).astype(bf16)
        for i in range(out.shape[1] // width):
            grad_ref[i * taps : (i + 1) * taps, cols] = out[:, i * width : (i + 1) * width]
    product = dot(grad_ref[...], weight_ref[...], ((1,), (1,)))
    step = pl.program_id(0)

    @pl.when(step == 0)
    def _():
        total[...] = product

    @pl.when(step > 0)
    def _():
        total[...] += product

    @pl.when(step == pl.num_programs(0) - 1)
    def _():
        back_ref[...] = total[...].astype(bf16)


def back(mixes, weight, ahead, after=()):
    rows, width = mixes[0].shape
    tokens = (len(mixes) + 1) // 2 * rows
    depth = weight.shape[0]
    groups, taps, _ = ahead.shape
    step = 8
    tile = width // groups * step
    return call(
        functools.partial(back_kernel, len(mixes)),
        (*mixes, weight, ahead),
        after,
        grid=(groups // step,),
        in_specs=[pl.BlockSpec((rows, tile), lambda i: (0, i))] * len(mixes)
        + [
            pl.BlockSpec((depth, tile), lambda i: (0, i)),
            pl.BlockSpec((step, taps, 2 * taps), lambda i: (i, 0, 0)),
        ],
        out_specs=[
            pl.BlockSpec((tokens, tile), lambda i: (0, i)),
            pl.BlockSpec((tokens, depth), lambda i: (0, 0)),
        ],
        out_shape=[shape((tokens, width), bf16), shape((tokens, depth), bf16)],
        scratch_shapes=[pltpu.VMEM((tokens, tile), bf16), pltpu.VMEM((tokens, depth), f32)],
        flops=6 * tokens * width * (depth + 2 * taps),
        name="back",
    )


def taps_kernel(count, groups, *refs):
    taps_ref, *mix_refs = refs[-3:]
    taps = taps_ref.shape[2]
    width = mix_refs[0].shape[1] // groups
    row = lax.broadcasted_iota(jnp.int32, (taps, taps), 0)
    col = lax.broadcasted_iota(jnp.int32, (taps, taps), 1)
    total = [0] * groups
    for first, mix_ref in zip((0, count + 1), mix_refs):
        assemble(refs[first : first + count], mix_ref)
        part_ref = refs[first + count]
        for g in range(groups):
            cols = slice(g * width, (g + 1) * width)
            both = with_following(mix_ref[:, cols], taps)
            total[g] += dot(side_by_side(part_ref[:, cols], taps), both, ((1,), (1,)))
    for g in range(groups):
        pairs = jnp.where(col >= row, total[g][:, :taps], total[g][:, taps:])
        folded = pairs[0:8]
        for a in range(8, taps, 8):
            folded = folded + pltpu.roll(pairs[a : a + 8], taps - a, 1)
        line = folded[0:1]
        for b in range(1, 8):
            line = line + pltpu.roll(folded[b : b + 1], taps - b, 1)
        taps_ref[0, g : g + 1, :] = line


def filter_gradient(down_mixes, down_part, up_mixes, up_part, groups, taps, after=()):
    rows, width = down_mixes[0].shape
    tokens = down_part.shape[0]
    step = 8
    tile = width // groups * step
    count = len(down_mixes)
    block = [pl.BlockSpec((rows, tile), lambda i: (0, i))] * count
    part = [pl.BlockSpec((tokens, tile), lambda i: (0, i))]
    return call(
        functools.partial(taps_kernel, count, step),
        (*down_mixes, down_part, *up_mixes, up_part),
        after,
        grid=(groups // step,),
        in_specs=(block + part) * 2,
        out_specs=pl.BlockSpec((1, step, taps), lambda i: (i, 0, 0)),
        out_shape=shape((groups // step, step, taps), f32),
        scratch_shapes=[pltpu.VMEM((tokens, tile), bf16)] * 2,
        counted=False,
        name="filter_gradient",
    ).reshape(1, groups, taps)


def weight_kernel(down_x, up_x, down_g, up_g, out_ref, down_t, up_t):
    @pl.when(pl.program_id(0) == 0)
    def _():
        down_t[...] = down_x[...].T
        up_t[...] = up_x[...].T

    out_ref[...] = (dot(down_t[...], down_g[...]) + dot(up_t[...], up_g[...])).astype(bf16)


def weight_gradient(down_x, up_x, down_g, up_g, after=()):
    tokens, depth = down_x.shape
    width = down_g.shape[1]
    tile = width // 4
    whole = pl.BlockSpec((tokens, depth), lambda i: (0, 0))
    part = pl.BlockSpec((tokens, tile), lambda i: (0, i))
    return call(
        weight_kernel,
        (down_x, up_x, down_g, up_g),
        after,
        grid=(width // tile,),
        in_specs=[whole, whole, part, part],
        out_specs=pl.BlockSpec((depth, tile), lambda i: (0, i)),
        out_shape=shape((depth, width), bf16),
        scratch_shapes=[pltpu.VMEM((depth, tokens), bf16)] * 2,
        counted=False,
        name="weight_gradient",
    )


def settle_kernel(own_ref, came_ref, out_ref):
    stays = 2 * lax.axis_index("section") == lax.axis_size("section")

    @pl.when(stays)
    def _():
        out_ref[...] = own_ref[...]

    @pl.when(jnp.logical_not(stays))
    def _():
        out_ref[...] = came_ref[...]


def settle(own, came, after=()):
    step = came.shape[1] // 2
    spec = pl.BlockSpec((1, step, came.shape[2]), lambda i: (0, i, 0))
    return call(
        settle_kernel,
        (own, came),
        after,
        grid=(2,),
        in_specs=[spec, spec],
        out_specs=spec,
        out_shape=shape(came.shape, came.dtype),
        name="settle",
    )


def finish_kernel(xin_ref, cot_ref, back_ref, *rest):
    *mixed_refs, out_ref = rest
    normed, inverse = normalise(xin_ref[...].astype(f32))
    cot = cot_ref[...].astype(f32)
    returned = jnp.concatenate([back_ref[i] for i in range(back_ref.shape[0])], axis=1)
    mixed = sum(ref[...].astype(f32) for ref in mixed_refs)
    total = cot * mixed + returned.astype(f32)
    mean = jnp.mean(total * normed, axis=1, keepdims=True)
    out_ref[0] = (cot + inverse * (total - normed * mean)).astype(bf16)


def finish(xin, cot, mixed, returned, after=()):
    rows, width = xin.shape
    blocks, _, depth = returned.shape
    step = 64
    spec = pl.BlockSpec((step, width), lambda i: (i, 0))
    return call(
        finish_kernel,
        (xin, cot, returned, *mixed),
        after,
        grid=(rows // step,),
        in_specs=[spec, spec, pl.BlockSpec((blocks, step, depth), lambda i: (0, i, 0))]
        + [spec] * len(mixed),
        out_specs=pl.BlockSpec((1, step, width), lambda i: (0, i, 0)),
        out_shape=shape((1, rows, width), bf16),
        name="finish",
    )


def exchange(x):
    blocks = lax.axis_size("tensor")
    x = x.reshape(blocks, -1, x.shape[-1])
    return lax.all_to_all(x, "tensor", split_axis=0, concat_axis=0, tiled=True)


def both_ways(right, left):
    blocks = lax.axis_size("tensor")
    onward = [(i, i + 1) for i in range(blocks - 1)]
    return (
        lax.ppermute(right, "tensor", onward),
        lax.ppermute(left, "tensor", [(j, i) for i, j in onward]),
    )


def payload_kernel(s, right_ref, left_ref, right_piece, left_piece, right_out, left_out):
    mine = lax.axis_index("tensor")
    blocks = lax.axis_size("tensor")

    def put(came, piece, out, adds):
        @pl.when(adds)
        def _():
            out[...] = (came[...].astype(f32) + piece[...].astype(f32)).astype(bf16)

        @pl.when(jnp.logical_not(adds))
        def _():
            out[...] = came[...]

    put(right_ref, right_piece, right_out, mine < s - 1)
    put(left_ref, left_piece, left_out, mine > blocks - s)


def payload(s, arrived, pieces, after=()):
    blocks = len(pieces)
    rows, width = pieces[0].shape
    step = 64
    spec = pl.BlockSpec((step, width), lambda i: (i, 0))
    return call(
        functools.partial(payload_kernel, s),
        (*arrived, pieces[blocks + 1 - s], pieces[s - 1]),
        after,
        grid=(rows // step,),
        in_specs=[spec] * 4,
        out_specs=[spec] * 2,
        out_shape=[shape((rows, width), bf16)] * 2,
        name="payload",
    )


def list_blocks(mix, arrivals):
    rights, lefts = zip(*arrivals)
    return [mix, *rights, *lefts]


def sort_arrivals(mix, pieces, arrivals):
    right, left = arrivals[-1]
    return list_blocks(mix, arrivals[:-1]), [pieces[0], right, left]


def sum_kernel(*refs):
    *in_refs, out_ref, sorted_ref = refs
    for s, ref in enumerate(in_refs):
        sorted_ref[pl.ds(place(-s), 1)] = ref[...]
    out_ref[...] = sum(sorted_ref[i : i + 1] for i in range(len(in_refs)))


def sum_all(x, after=()):
    blocks = lax.axis_size("tensor")
    terms = [x]
    for s in range(1, blocks):
        terms.append(lax.ppermute(x, "tensor", [(i, (i + s) % blocks) for i in range(blocks)]))
    spec = pl.BlockSpec(x.shape, lambda i: (0,) * x.ndim)
    return call(
        sum_kernel,
        terms,
        after,
        grid=(1,),
        in_specs=[spec] * blocks,
        out_specs=spec,
        out_shape=shape(x.shape, x.dtype),
        scratch_shapes=[pltpu.VMEM((blocks, *x.shape[1:]), x.dtype)],
        name="sum_all",
    )


def per_device(weights, filters, down_input, down_cot, up_input, up_cot):
    sections = lax.axis_size("section")
    mirror = [(s, sections - 1 - s) for s in range(sections)]
    down_pairs = [(s + 1, s) for s in range(sections - 1)]
    up_pairs = [(sections - s, s) for s in range(1, sections) if 2 * s != sections]
    weight = weights[0]
    down_xin, down_cot = down_input[0], down_cot[0]
    up_xin = lax.ppermute(up_input[0], "section", mirror)
    up_cot = lax.ppermute(up_cot[0], "section", mirror)
    blocks = lax.axis_size("tensor")
    depth = weight.shape[0]
    down_normed, down_mix = prepare(down_xin, down_cot)
    down_x = exchange(down_normed).reshape(-1, depth)
    down_arrivals = [both_ways(down_mix, down_mix)]
    causal, ahead = toeplitz(filters[0])
    (up_normed,) = prepare(up_xin, after=(ahead,))
    up_x = exchange(up_normed).reshape(-1, depth)
    up_mix = grad_mix(up_xin, up_cot, after=down_arrivals[0])
    up_arrivals = [both_ways(up_mix, up_mix)]
    down_part, down_pieces = project(down_x, weight, causal, after=(up_normed, up_mix))
    last = down_part
    for s in range(2, blocks):
        sent = payload(s, down_arrivals[-1], down_pieces, after=(last,))
        down_arrivals.append(both_ways(*sent))
        if s == 2:
            up_part, up_pieces = project(up_x, weight, causal, after=sent)
        sent = payload(s, up_arrivals[-1], up_pieces, after=sent)
        up_arrivals.append(both_ways(*sent))
        last = sent[0]
    sent = payload(blocks, up_arrivals[-1], up_pieces, after=(last, *down_arrivals[-1]))
    up_arrivals.append(both_ways(*sent))
    up_mixes, up_conv = sort_arrivals(up_mix, up_pieces, up_arrivals)
    up_g, up_back = back(up_mixes, weight, ahead, after=sent)
    up_back = exchange(up_back)
    down_mixes = list_blocks(down_mix, down_arrivals)
    down_g, down_back = back(down_mixes, weight, ahead, after=(up_g, *up_arrivals[-1]))
    down_back = exchange(down_back)
    sent = payload(blocks, down_arrivals[-1], down_pieces, after=(down_g,))
    down_arrivals.append(both_ways(*sent))
    _, down_conv = sort_arrivals(down_mix, down_pieces, down_arrivals)
    up_grad = finish(up_xin, up_cot, up_conv, up_back, after=(down_g, *sent))
    up_passed = lax.ppermute(up_grad, "section", up_pairs)
    taps = filter_gradient(
        down_mixes, down_part, up_mixes, up_part, *filters.shape[1:], after=(up_grad,)
    )
    weight_grad = weight_gradient(down_x, up_x, down_g, up_g, after=(taps,))
    up_passed = settle(up_grad, up_passed, after=(weight_grad, *down_arrivals[-1]))
    down_grad = finish(down_xin, down_cot, down_conv, down_back, after=(up_passed,))
    down_passed = lax.ppermute(down_grad, "section", down_pairs)
    taps = sum_all(taps, after=(down_grad,))
    return weight_grad[None], taps, down_passed, up_passed


def solution(mesh):
    rows = P("section", "tensor", None)
    whole = P("section", None, None)
    return jax.shard_map(
        per_device,
        mesh=mesh,
        in_specs=(rows, whole, rows, rows, rows, rows),
        out_specs=(rows, whole, rows, rows),
        check_vma=False,
    )
```

```python
import functools

import jax
import jax.numpy as jnp
from jax import lax
from jax.experimental import pallas as pl
from jax.experimental.pallas import tpu as pltpu
from jax.sharding import PartitionSpec as P

epsilon = 1e-06
params = functools.partial(pltpu.CompilerParams, vmem_limit_bytes=63 * 1024 * 1024)
f32, bf16 = jnp.float32, jnp.bfloat16


def dot(a, b, dims=((1,), (0,))):
    return lax.dot_general(a, b, (dims, ((), ())), preferred_element_type=f32)


def shape(dims, dtype):
    return jax.ShapeDtypeStruct(dims, dtype)


def call(kernel, args, after, in_specs, out_shape, flops=0, counted=True, **options):
    count = len(args)
    arrays = [*args, *(out_shape if isinstance(out_shape, list) else [out_shape])]
    cost = pl.CostEstimate(
        flops=flops,
        transcendentals=0,
        bytes_accessed=counted * sum(x.size * x.dtype.itemsize for x in arrays),
    )

    def body(*refs):
        kernel(*refs[:count], *refs[count + len(after) :])

    unread = [pl.BlockSpec(memory_space=pl.ANY)] * len(after)
    return pl.pallas_call(
        body,
        in_specs=list(in_specs) + unread,
        out_shape=out_shape,
        cost_estimate=cost,
        compiler_params=params(),
        **options,
    )(*args, *after)


def toeplitz_kernel(filters_ref, causal_ref, ahead_ref):
    taps = filters_ref.shape[1]
    row = lax.broadcasted_iota(jnp.int32, (taps, taps), 0)
    col = lax.broadcasted_iota(jnp.int32, (taps, taps), 1)
    for g in range(filters_ref.shape[0]):
        line = jnp.broadcast_to(filters_ref[g : g + 1, :], (taps, taps))
        turned = pltpu.roll(line, 0, 1, stride=1, stride_axis=0)
        own = jnp.where(col >= row, turned, 0.0)
        beyond = jnp.where(col < row, turned, 0.0)
        ahead_ref[g, :, :taps] = own.astype(bf16)
        ahead_ref[g, :, taps:] = beyond.astype(bf16)
        causal_ref[g, :, :taps] = beyond.T.astype(bf16)
        causal_ref[g, :, taps:] = own.T.astype(bf16)


def toeplitz(filters):
    groups, taps = filters.shape
    step = 8
    out = shape((groups, taps, 2 * taps), bf16)
    spec = pl.BlockSpec((step, taps, 2 * taps), lambda i: (i, 0, 0))
    return call(
        toeplitz_kernel,
        (filters,),
        (),
        grid=(groups // step,),
        in_specs=[pl.BlockSpec((step, taps), lambda i: (i, 0))],
        out_specs=[spec, spec],
        out_shape=[out, out],
        name="toeplitz",
    )


def place(by):
    blocks = lax.axis_size("tensor")
    return lax.rem(lax.axis_index("tensor") + (by + blocks), blocks)


def window(index, size):
    return pl.ds(pl.multiple_of(index * size, size), size)


def normalise(wide):
    inverse = lax.rsqrt(jnp.mean(wide * wide, axis=1, keepdims=True) + epsilon)
    return wide * inverse, inverse


def prepare_kernel(xin_ref, *refs):
    *cot_ref, normed_ref = refs[: len(refs) // 2 + 1]
    normed, _ = normalise(xin_ref[...].astype(f32))
    width = normed_ref.shape[2]
    for i in range(normed_ref.shape[0]):
        normed_ref[i] = normed[:, i * width : (i + 1) * width].astype(bf16)
    if cot_ref:
        refs[-1][...] = (cot_ref[0][...].astype(f32) * normed).astype(bf16)


def prepare(*args, after=()):
    rows, width = args[0].shape
    blocks = lax.axis_size("tensor")
    step = 64
    spec = pl.BlockSpec((step, width), lambda i: (i, 0))
    normed_spec = pl.BlockSpec((blocks, step, width // blocks), lambda i: (0, i, 0))
    extra = len(args) - 1
    return call(
        prepare_kernel,
        args,
        after,
        grid=(rows // step,),
        in_specs=[spec] * len(args),
        out_specs=[normed_spec] + [spec] * extra,
        out_shape=[shape((blocks, rows, width // blocks), bf16)] + [shape((rows, width), bf16)] * extra,
        name="prepare",
    )


def mix_kernel(xin_ref, cot_ref, mix_ref):
    normed, _ = normalise(xin_ref[...].astype(f32))
    mix_ref[...] = (cot_ref[...].astype(f32) * normed).astype(bf16)


def grad_mix(xin, cot, after=()):
    rows, width = xin.shape
    step = 64
    spec = pl.BlockSpec((step, width), lambda i: (i, 0))
    return call(
        mix_kernel,
        (xin, cot),
        after,
        grid=(rows // step,),
        in_specs=[spec, spec],
        out_specs=spec,
        out_shape=shape((rows, width), bf16),
        name="grad_mix",
    )


def side_by_side(x, rows):
    return jnp.concatenate([x[s : s + rows] for s in range(0, x.shape[0], rows)], axis=1)


def project_kernel(features_ref, weight_ref, causal_ref, part_ref, *rest):
    *mixed_refs, mixed_ref = rest
    groups, taps, _ = causal_ref.shape
    part = dot(features_ref[...], weight_ref[...]).astype(bf16)
    part_ref[...] = part
    width = part.shape[1] // groups
    for g in range(groups):
        cols = slice(g * width, (g + 1) * width)
        own = side_by_side(part[:, cols], taps)
        before = jnp.concatenate([jnp.zeros((taps, width), bf16), own[:, :-width]], axis=1)
        out = dot(causal_ref[g], jnp.concatenate([before, own], axis=0)).astype(bf16)
        for i in range(out.shape[1] // width):
            mixed_ref[i * taps : (i + 1) * taps, cols] = out[:, i * width : (i + 1) * width]
    for s, out_ref in enumerate(mixed_refs):
        out_ref[...] = mixed_ref[window(place(s), out_ref.shape[0]), :]


def project(features, weight, causal, after=()):
    blocks = lax.axis_size("tensor")
    tokens, depth = features.shape
    rows = tokens // blocks
    width = weight.shape[1]
    groups, taps, _ = causal.shape
    step = 8
    tile = width // groups * step
    part, *mixed = call(
        project_kernel,
        (features, weight, causal),
        after,
        grid=(groups // step,),
        in_specs=[
            pl.BlockSpec((tokens, depth), lambda i: (0, 0)),
            pl.BlockSpec((depth, tile), lambda i: (0, i)),
            pl.BlockSpec((step, taps, 2 * taps), lambda i: (i, 0, 0)),
        ],
        out_specs=[pl.BlockSpec((tokens, tile), lambda i: (0, i))]
        + [pl.BlockSpec((rows, tile), lambda i: (0, i))] * blocks,
        out_shape=[shape((tokens, width), bf16)] + [shape((rows, width), bf16)] * blocks,
        scratch_shapes=[pltpu.VMEM((tokens, tile), bf16)],
        flops=2 * tokens * width * (depth + 2 * taps),
        name="project",
    )
    return part, mixed


def assemble(block_refs, mix_ref):
    blocks = (len(block_refs) + 1) // 2
    rows = block_refs[0].shape[0]
    mine = lax.axis_index("tensor")
    mix_ref[window(mine, rows), :] = block_refs[0][...]
    for s in range(1, blocks):

        @pl.when(mine >= s)
        def _():
            mix_ref[window(mine - s, rows), :] = block_refs[s][...]

        @pl.when(mine < s)
        def _():
            mix_ref[window(mine + (blocks - s), rows), :] = block_refs[2 * blocks - 1 - s][...]


def with_following(mix, taps):
    own = side_by_side(mix, taps)
    width = mix.shape[1]
    following = jnp.concatenate([own[:, width:], jnp.zeros((taps, width), bf16)], axis=1)
    return jnp.concatenate([own, following], axis=0)


def back_kernel(count, *refs):
    weight_ref, ahead_ref, grad_ref, back_ref, mix_ref, total = refs[count:]
    groups, taps, _ = ahead_ref.shape
    width = mix_ref.shape[1] // groups
    assemble(refs[:count], mix_ref)
    for g in range(groups):
        cols = slice(g * width, (g + 1) * width)
        out = dot(ahead_ref[g], with_following(mix_ref[:, cols], taps)).astype(bf16)
        for i in range(out.shape[1] // width):
            grad_ref[i * taps : (i + 1) * taps, cols] = out[:, i * width : (i + 1) * width]
    product = dot(grad_ref[...], weight_ref[...], ((1,), (1,)))
    step = pl.program_id(0)

    @pl.when(step == 0)
    def _():
        total[...] = product

    @pl.when(step > 0)
    def _():
        total[...] += product

    @pl.when(step == pl.num_programs(0) - 1)
    def _():
        back_ref[...] = total[...].astype(bf16)


def back(mixes, weight, ahead, after=()):
    rows, width = mixes[0].shape
    tokens = (len(mixes) + 1) // 2 * rows
    depth = weight.shape[0]
    groups, taps, _ = ahead.shape
    step = 8
    tile = width // groups * step
    return call(
        functools.partial(back_kernel, len(mixes)),
        (*mixes, weight, ahead),
        after,
        grid=(groups // step,),
        in_specs=[pl.BlockSpec((rows, tile), lambda i: (0, i))] * len(mixes)
        + [
            pl.BlockSpec((depth, tile), lambda i: (0, i)),
            pl.BlockSpec((step, taps, 2 * taps), lambda i: (i, 0, 0)),
        ],
        out_specs=[
            pl.BlockSpec((tokens, tile), lambda i: (0, i)),
            pl.BlockSpec((tokens, depth), lambda i: (0, 0)),
        ],
        out_shape=[shape((tokens, width), bf16), shape((tokens, depth), bf16)],
        scratch_shapes=[pltpu.VMEM((tokens, tile), bf16), pltpu.VMEM((tokens, depth), f32)],
        flops=6 * tokens * width * (depth + 2 * taps),
        name="back",
    )


def taps_kernel(count, groups, *refs):
    taps_ref, *mix_refs = refs[-3:]
    taps = taps_ref.shape[2]
    width = mix_refs[0].shape[1] // groups
    row = lax.broadcasted_iota(jnp.int32, (taps, taps), 0)
    col = lax.broadcasted_iota(jnp.int32, (taps, taps), 1)
    total = [0] * groups
    for first, mix_ref in zip((0, count + 1), mix_refs):
        assemble(refs[first : first + count], mix_ref)
        part_ref = refs[first + count]
        for g in range(groups):
            cols = slice(g * width, (g + 1) * width)
            both = with_following(mix_ref[:, cols], taps)
            total[g] += dot(side_by_side(part_ref[:, cols], taps), both, ((1,), (1,)))
    for g in range(groups):
        pairs = jnp.where(col >= row, total[g][:, :taps], total[g][:, taps:])
        folded = pairs[0:8]
        for a in range(8, taps, 8):
            folded = folded + pltpu.roll(pairs[a : a + 8], taps - a, 1)
        line = folded[0:1]
        for b in range(1, 8):
            line = line + pltpu.roll(folded[b : b + 1], taps - b, 1)
        taps_ref[0, g : g + 1, :] = line


def filter_gradient(down_mixes, down_part, up_mixes, up_part, groups, taps, after=()):
    rows, width = down_mixes[0].shape
    tokens = down_part.shape[0]
    step = 8
    tile = width // groups * step
    count = len(down_mixes)
    block = [pl.BlockSpec((rows, tile), lambda i: (0, i))] * count
    part = [pl.BlockSpec((tokens, tile), lambda i: (0, i))]
    return call(
        functools.partial(taps_kernel, count, step),
        (*down_mixes, down_part, *up_mixes, up_part),
        after,
        grid=(groups // step,),
        in_specs=(block + part) * 2,
        out_specs=pl.BlockSpec((1, step, taps), lambda i: (i, 0, 0)),
        out_shape=shape((groups // step, step, taps), f32),
        scratch_shapes=[pltpu.VMEM((tokens, tile), bf16)] * 2,
        counted=False,
        name="filter_gradient",
    ).reshape(1, groups, taps)


def weight_kernel(down_x, up_x, down_g, up_g, out_ref, down_t, up_t):
    @pl.when(pl.program_id(0) == 0)
    def _():
        down_t[...] = down_x[...].T
        up_t[...] = up_x[...].T

    out_ref[...] = (dot(down_t[...], down_g[...]) + dot(up_t[...], up_g[...])).astype(bf16)


def weight_gradient(down_x, up_x, down_g, up_g, after=()):
    tokens, depth = down_x.shape
    width = down_g.shape[1]
    tile = width // 4
    whole = pl.BlockSpec((tokens, depth), lambda i: (0, 0))
    part = pl.BlockSpec((tokens, tile), lambda i: (0, i))
    return call(
        weight_kernel,
        (down_x, up_x, down_g, up_g),
        after,
        grid=(width // tile,),
        in_specs=[whole, whole, part, part],
        out_specs=pl.BlockSpec((depth, tile), lambda i: (0, i)),
        out_shape=shape((depth, width), bf16),
        scratch_shapes=[pltpu.VMEM((depth, tokens), bf16)] * 2,
        flops=4 * tokens * depth * width,
        name="weight_gradient",
    )


def settle_kernel(*refs):
    *in_refs, out_ref = refs
    stays = 2 * lax.axis_index("section") == lax.axis_size("section")
    rows = in_refs[0].shape[1]
    for i in range(2):
        for ref, taken in ((in_refs[i], stays), (in_refs[2 + i], jnp.logical_not(stays))):

            @pl.when(taken)
            def _():
                out_ref[:, i * rows : (i + 1) * rows] = ref[...]


def settle(own, came, after=()):
    _, rows, width = own[0].shape
    spec = pl.BlockSpec((1, rows, width // 2), lambda i: (0, 0, i))
    return call(
        settle_kernel,
        (*own, *came),
        after,
        grid=(2,),
        in_specs=[spec] * 4,
        out_specs=pl.BlockSpec((1, 2 * rows, width // 2), lambda i: (0, 0, i)),
        out_shape=shape((1, 2 * rows, width), bf16),
        name="settle",
    )


def finish_kernel(inputs, xin_ref, cot_ref, back_ref, *rest):
    mixed_refs, out_refs = rest[: inputs - 3], rest[inputs - 3 :]
    normed, inverse = normalise(xin_ref[...].astype(f32))
    cot = cot_ref[...].astype(f32)
    returned = jnp.concatenate([back_ref[i] for i in range(back_ref.shape[0])], axis=1)
    mixed = sum(ref[...].astype(f32) for ref in mixed_refs)
    total = cot * mixed + returned.astype(f32)
    mean = jnp.mean(total * normed, axis=1, keepdims=True)
    out = (cot + inverse * (total - normed * mean)).astype(bf16)
    if len(out_refs) == 1:
        out_refs[0][0] = out
    else:
        for i, out_ref in enumerate(out_refs):

            @pl.when(pl.program_id(0) == i)
            def _():
                out_ref[0] = out


def finish(xin, cot, mixed, returned, halves, after=()):
    rows, width = xin.shape
    blocks, _, depth = returned.shape
    step = rows // 2
    spec = pl.BlockSpec((step, width), lambda i: (i, 0))
    if halves:
        out_specs = [pl.BlockSpec((1, step, width), lambda i: (0, 0, 0))] * 2
        out_shape = [shape((1, step, width), bf16)] * 2
    else:
        out_specs = pl.BlockSpec((1, step, width), lambda i: (0, i, 0))
        out_shape = shape((1, rows, width), bf16)
    return call(
        functools.partial(finish_kernel, 3 + len(mixed)),
        (xin, cot, returned, *mixed),
        after,
        grid=(2,),
        in_specs=[spec, spec, pl.BlockSpec((blocks, step, depth), lambda i: (0, i, 0))]
        + [spec] * len(mixed),
        out_specs=out_specs,
        out_shape=out_shape,
        name="finish",
    )


def exchange(x):
    blocks = lax.axis_size("tensor")
    x = x.reshape(blocks, -1, x.shape[-1])
    return lax.all_to_all(x, "tensor", split_axis=0, concat_axis=0, tiled=True)


def both_ways(right, left):
    blocks = lax.axis_size("tensor")
    onward = [(i, i + 1) for i in range(blocks - 1)]
    return (
        lax.ppermute(right, "tensor", onward),
        lax.ppermute(left, "tensor", [(j, i) for i, j in onward]),
    )


def payload_kernel(s, right_ref, left_ref, right_piece, left_piece, right_out, left_out):
    mine = lax.axis_index("tensor")
    blocks = lax.axis_size("tensor")

    def put(came, piece, out, adds):
        @pl.when(adds)
        def _():
            out[...] = (came[...].astype(f32) + piece[...].astype(f32)).astype(bf16)

        @pl.when(jnp.logical_not(adds))
        def _():
            out[...] = came[...]

    put(right_ref, right_piece, right_out, mine < s - 1)
    put(left_ref, left_piece, left_out, mine > blocks - s)


def payload(s, arrived, pieces, after=()):
    blocks = len(pieces)
    rows, width = pieces[0].shape
    step = 64
    spec = pl.BlockSpec((step, width), lambda i: (i, 0))
    return call(
        functools.partial(payload_kernel, s),
        (*arrived, pieces[blocks + 1 - s], pieces[s - 1]),
        after,
        grid=(rows // step,),
        in_specs=[spec] * 4,
        out_specs=[spec] * 2,
        out_shape=[shape((rows, width), bf16)] * 2,
        name="payload",
    )


def sort_arrivals(mix, pieces, arrivals):
    rights, lefts = zip(*arrivals)
    return [mix, *rights[:-1], *lefts[:-1]], [pieces[0], rights[-1], lefts[-1]]


def sum_kernel(*refs):
    *in_refs, out_ref, sorted_ref = refs
    for s, ref in enumerate(in_refs):
        sorted_ref[pl.ds(place(-s), 1)] = ref[...]
    out_ref[...] = sum(sorted_ref[i : i + 1] for i in range(len(in_refs)))


def sum_all(x, after=()):
    blocks = lax.axis_size("tensor")
    terms = [x]
    for s in range(1, blocks):
        terms.append(lax.ppermute(x, "tensor", [(i, (i + s) % blocks) for i in range(blocks)]))
    spec = pl.BlockSpec(x.shape, lambda i: (0,) * x.ndim)
    return call(
        sum_kernel,
        terms,
        after,
        grid=(1,),
        in_specs=[spec] * blocks,
        out_specs=spec,
        out_shape=shape(x.shape, x.dtype),
        scratch_shapes=[pltpu.VMEM((blocks, *x.shape[1:]), x.dtype)],
        name="sum_all",
    )


def per_device(weights, filters, down_input, down_cot, up_input, up_cot):
    sections = lax.axis_size("section")
    mirror = [(s, sections - 1 - s) for s in range(sections)]
    down_pairs = [(s + 1, s) for s in range(sections - 1)]
    up_pairs = [(sections - s, s) for s in range(1, sections) if 2 * s != sections]
    weight = weights[0]
    down_xin, down_cot = down_input[0], down_cot[0]
    up_xin = lax.ppermute(up_input[0], "section", mirror)
    up_cot = lax.ppermute(up_cot[0], "section", mirror)
    blocks = lax.axis_size("tensor")
    depth = weight.shape[0]
    down_normed, down_mix = prepare(down_xin, down_cot)
    down_x = exchange(down_normed).reshape(-1, depth)
    down_arrivals = [both_ways(down_mix, down_mix)]
    causal, ahead = toeplitz(filters[0])
    (up_normed,) = prepare(up_xin, after=(ahead,))
    up_x = exchange(up_normed).reshape(-1, depth)
    up_mix = grad_mix(up_xin, up_cot, after=down_arrivals[0])
    up_arrivals = [both_ways(up_mix, up_mix)]
    down_part, down_pieces = project(down_x, weight, causal, after=(up_normed, up_mix))
    last = down_part
    for s in range(2, blocks + 1):
        sent = payload(s, down_arrivals[-1], down_pieces, after=(last,))
        down_arrivals.append(both_ways(*sent))
        if s == 2:
            up_part, up_pieces = project(up_x, weight, causal, after=sent)
        sent = payload(s, up_arrivals[-1], up_pieces, after=sent)
        up_arrivals.append(both_ways(*sent))
        last = sent[0]
    down_mixes, down_conv = sort_arrivals(down_mix, down_pieces, down_arrivals)
    up_mixes, up_conv = sort_arrivals(up_mix, up_pieces, up_arrivals)
    up_g, up_back = back(up_mixes, weight, ahead, after=(last,))
    up_back = exchange(up_back)
    taps = filter_gradient(
        down_mixes, down_part, up_mixes, up_part, *filters.shape[1:], after=(up_g,)
    )
    down_g, down_back = back(
        down_mixes, weight, ahead, after=(taps, *down_arrivals[-1])
    )
    down_back = exchange(down_back)
    up_grad = finish(up_xin, up_cot, up_conv, up_back, True, after=(down_g,))
    up_came = [lax.ppermute(half, "section", up_pairs) for half in up_grad]
    weight_grad = weight_gradient(down_x, up_x, down_g, up_g, after=(up_grad[0],))
    down_grad = finish(
        down_xin, down_cot, down_conv, down_back, False, after=(weight_grad, up_came[0])
    )
    down_passed = lax.ppermute(down_grad, "section", down_pairs)
    taps = sum_all(taps, after=(down_grad,))
    up_passed = settle(up_grad, up_came, after=(taps,))
    return weight_grad[None], taps, down_passed, up_passed


def solution(mesh):
    rows = P("section", "tensor", None)
    whole = P("section", None, None)
    return jax.shard_map(
        per_device,
        mesh=mesh,
        in_specs=(rows, whole, rows, rows, rows, rows),
        out_specs=(rows, whole, rows, rows),
        check_vma=False,
    )
```

```python
import functools

import jax
import jax.numpy as jnp
from jax import lax
from jax.experimental import pallas as pl
from jax.experimental.pallas import tpu as pltpu
from jax.sharding import PartitionSpec as P

epsilon = 1e-06
params = functools.partial(pltpu.CompilerParams, vmem_limit_bytes=63 * 1024 * 1024)
f32, bf16 = jnp.float32, jnp.bfloat16


def dot(a, b, dims=((1,), (0,))):
    return lax.dot_general(a, b, (dims, ((), ())), preferred_element_type=f32)


def shape(dims, dtype):
    return jax.ShapeDtypeStruct(dims, dtype)


def call(kernel, args, after, in_specs, out_shape, flops=0, counted=True, **options):
    count = len(args)
    arrays = [*args, *(out_shape if isinstance(out_shape, list) else [out_shape])]
    cost = pl.CostEstimate(
        flops=flops,
        transcendentals=0,
        bytes_accessed=counted * sum(x.size * x.dtype.itemsize for x in arrays),
    )

    def body(*refs):
        kernel(*refs[:count], *refs[count + len(after) :])

    unread = [pl.BlockSpec(memory_space=pl.ANY)] * len(after)
    return pl.pallas_call(
        body,
        in_specs=list(in_specs) + unread,
        out_shape=out_shape,
        cost_estimate=cost,
        compiler_params=params(),
        **options,
    )(*args, *after)


def toeplitz_kernel(filters_ref, causal_ref, ahead_ref):
    taps = filters_ref.shape[1]
    row = lax.broadcasted_iota(jnp.int32, (taps, taps), 0)
    col = lax.broadcasted_iota(jnp.int32, (taps, taps), 1)
    for g in range(filters_ref.shape[0]):
        line = jnp.broadcast_to(filters_ref[g : g + 1, :], (taps, taps))
        turned = pltpu.roll(line, 0, 1, stride=1, stride_axis=0)
        own = jnp.where(col >= row, turned, 0.0)
        beyond = jnp.where(col < row, turned, 0.0)
        ahead_ref[g, :, :taps] = own.astype(bf16)
        ahead_ref[g, :, taps:] = beyond.astype(bf16)
        causal_ref[g, :, :taps] = beyond.T.astype(bf16)
        causal_ref[g, :, taps:] = own.T.astype(bf16)


def toeplitz(filters):
    groups, taps = filters.shape
    step = 8
    out = shape((groups, taps, 2 * taps), bf16)
    spec = pl.BlockSpec((step, taps, 2 * taps), lambda i: (i, 0, 0))
    return call(
        toeplitz_kernel,
        (filters,),
        (),
        grid=(groups // step,),
        in_specs=[pl.BlockSpec((step, taps), lambda i: (i, 0))],
        out_specs=[spec, spec],
        out_shape=[out, out],
        name="toeplitz",
    )


def place(by):
    blocks = lax.axis_size("tensor")
    return lax.rem(lax.axis_index("tensor") + (by + blocks), blocks)


def window(index, size):
    return pl.ds(pl.multiple_of(index * size, size), size)


def normalise(wide):
    inverse = lax.rsqrt(jnp.mean(wide * wide, axis=1, keepdims=True) + epsilon)
    return wide * inverse, inverse


def prepare_kernel(xin_ref, *refs):
    *cot_ref, normed_ref = refs[: len(refs) // 2 + 1]
    normed, _ = normalise(xin_ref[...].astype(f32))
    width = normed_ref.shape[2]
    for i in range(normed_ref.shape[0]):
        normed_ref[i] = normed[:, i * width : (i + 1) * width].astype(bf16)
    if cot_ref:
        refs[-1][...] = (cot_ref[0][...].astype(f32) * normed).astype(bf16)


def prepare(*args, after=()):
    rows, width = args[0].shape
    blocks = lax.axis_size("tensor")
    step = 64
    spec = pl.BlockSpec((step, width), lambda i: (i, 0))
    normed_spec = pl.BlockSpec((blocks, step, width // blocks), lambda i: (0, i, 0))
    extra = len(args) - 1
    return call(
        prepare_kernel,
        args,
        after,
        grid=(rows // step,),
        in_specs=[spec] * len(args),
        out_specs=[normed_spec] + [spec] * extra,
        out_shape=[shape((blocks, rows, width // blocks), bf16)] + [shape((rows, width), bf16)] * extra,
        name="prepare",
    )


def mix_kernel(xin_ref, cot_ref, mix_ref):
    normed, _ = normalise(xin_ref[...].astype(f32))
    mix_ref[...] = (cot_ref[...].astype(f32) * normed).astype(bf16)


def grad_mix(xin, cot, after=()):
    rows, width = xin.shape
    step = 64
    spec = pl.BlockSpec((step, width), lambda i: (i, 0))
    return call(
        mix_kernel,
        (xin, cot),
        after,
        grid=(rows // step,),
        in_specs=[spec, spec],
        out_specs=spec,
        out_shape=shape((rows, width), bf16),
        name="grad_mix",
    )


def side_by_side(x, rows):
    return jnp.concatenate([x[s : s + rows] for s in range(0, x.shape[0], rows)], axis=1)


def project_kernel(features_ref, weight_ref, causal_ref, part_ref, *rest):
    *mixed_refs, mixed_ref = rest
    groups, taps, _ = causal_ref.shape
    part = dot(features_ref[...], weight_ref[...]).astype(bf16)
    part_ref[...] = part
    width = part.shape[1] // groups
    for g in range(groups):
        cols = slice(g * width, (g + 1) * width)
        own = side_by_side(part[:, cols], taps)
        before = jnp.concatenate([jnp.zeros((taps, width), bf16), own[:, :-width]], axis=1)
        out = dot(causal_ref[g], jnp.concatenate([before, own], axis=0)).astype(bf16)
        for i in range(out.shape[1] // width):
            mixed_ref[i * taps : (i + 1) * taps, cols] = out[:, i * width : (i + 1) * width]
    for s, out_ref in enumerate(mixed_refs):
        out_ref[...] = mixed_ref[window(place(s), out_ref.shape[0]), :]


def project(features, weight, causal, after=()):
    blocks = lax.axis_size("tensor")
    tokens, depth = features.shape
    rows = tokens // blocks
    width = weight.shape[1]
    groups, taps, _ = causal.shape
    step = 8
    tile = width // groups * step
    part, *mixed = call(
        project_kernel,
        (features, weight, causal),
        after,
        grid=(groups // step,),
        in_specs=[
            pl.BlockSpec((tokens, depth), lambda i: (0, 0)),
            pl.BlockSpec((depth, tile), lambda i: (0, i)),
            pl.BlockSpec((step, taps, 2 * taps), lambda i: (i, 0, 0)),
        ],
        out_specs=[pl.BlockSpec((tokens, tile), lambda i: (0, i))]
        + [pl.BlockSpec((rows, tile), lambda i: (0, i))] * blocks,
        out_shape=[shape((tokens, width), bf16)] + [shape((rows, width), bf16)] * blocks,
        scratch_shapes=[pltpu.VMEM((tokens, tile), bf16)],
        flops=2 * tokens * width * (depth + 2 * taps),
        name="project",
    )
    return part, mixed


def assemble(block_refs, mix_ref):
    blocks = (len(block_refs) + 1) // 2
    rows = block_refs[0].shape[0]
    mine = lax.axis_index("tensor")
    mix_ref[window(mine, rows), :] = block_refs[0][...]
    for s in range(1, blocks):

        @pl.when(mine >= s)
        def _():
            mix_ref[window(mine - s, rows), :] = block_refs[s][...]

        @pl.when(mine < s)
        def _():
            mix_ref[window(mine + (blocks - s), rows), :] = block_refs[2 * blocks - 1 - s][...]


def with_following(mix, taps):
    own = side_by_side(mix, taps)
    width = mix.shape[1]
    following = jnp.concatenate([own[:, width:], jnp.zeros((taps, width), bf16)], axis=1)
    return jnp.concatenate([own, following], axis=0)


def back_kernel(count, *refs):
    weight_ref, ahead_ref, grad_ref, back_ref, mix_ref, total = refs[count:]
    groups, taps, _ = ahead_ref.shape
    width = mix_ref.shape[1] // groups
    assemble(refs[:count], mix_ref)
    for g in range(groups):
        cols = slice(g * width, (g + 1) * width)
        out = dot(ahead_ref[g], with_following(mix_ref[:, cols], taps)).astype(bf16)
        for i in range(out.shape[1] // width):
            grad_ref[i * taps : (i + 1) * taps, cols] = out[:, i * width : (i + 1) * width]
    product = dot(grad_ref[...], weight_ref[...], ((1,), (1,)))
    step = pl.program_id(0)

    @pl.when(step == 0)
    def _():
        total[...] = product

    @pl.when(step > 0)
    def _():
        total[...] += product

    @pl.when(step == pl.num_programs(0) - 1)
    def _():
        back_ref[...] = total[...].astype(bf16)


def back(mixes, weight, ahead, after=()):
    rows, width = mixes[0].shape
    tokens = (len(mixes) + 1) // 2 * rows
    depth = weight.shape[0]
    groups, taps, _ = ahead.shape
    step = 8
    tile = width // groups * step
    return call(
        functools.partial(back_kernel, len(mixes)),
        (*mixes, weight, ahead),
        after,
        grid=(groups // step,),
        in_specs=[pl.BlockSpec((rows, tile), lambda i: (0, i))] * len(mixes)
        + [
            pl.BlockSpec((depth, tile), lambda i: (0, i)),
            pl.BlockSpec((step, taps, 2 * taps), lambda i: (i, 0, 0)),
        ],
        out_specs=[
            pl.BlockSpec((tokens, tile), lambda i: (0, i)),
            pl.BlockSpec((tokens, depth), lambda i: (0, 0)),
        ],
        out_shape=[shape((tokens, width), bf16), shape((tokens, depth), bf16)],
        scratch_shapes=[pltpu.VMEM((tokens, tile), bf16), pltpu.VMEM((tokens, depth), f32)],
        flops=6 * tokens * width * (depth + 2 * taps),
        name="back",
    )


def taps_kernel(count, groups, *refs):
    taps_ref, *mix_refs = refs[-3:]
    taps = taps_ref.shape[2]
    width = mix_refs[0].shape[1] // groups
    row = lax.broadcasted_iota(jnp.int32, (taps, taps), 0)
    col = lax.broadcasted_iota(jnp.int32, (taps, taps), 1)
    total = [0] * groups
    for first, mix_ref in zip((0, count + 1), mix_refs):
        assemble(refs[first : first + count], mix_ref)
        part_ref = refs[first + count]
        for g in range(groups):
            cols = slice(g * width, (g + 1) * width)
            both = with_following(mix_ref[:, cols], taps)
            total[g] += dot(side_by_side(part_ref[:, cols], taps), both, ((1,), (1,)))
    for g in range(groups):
        pairs = jnp.where(col >= row, total[g][:, :taps], total[g][:, taps:])
        folded = pairs[0:8]
        for a in range(8, taps, 8):
            folded = folded + pltpu.roll(pairs[a : a + 8], taps - a, 1)
        line = folded[0:1]
        for b in range(1, 8):
            line = line + pltpu.roll(folded[b : b + 1], taps - b, 1)
        taps_ref[0, g : g + 1, :] = line


def filter_gradient(down_mixes, down_part, up_mixes, up_part, groups, taps, after=()):
    rows, width = down_mixes[0].shape
    tokens = down_part.shape[0]
    step = 8
    tile = width // groups * step
    count = len(down_mixes)
    block = [pl.BlockSpec((rows, tile), lambda i: (0, i))] * count
    part = [pl.BlockSpec((tokens, tile), lambda i: (0, i))]
    return call(
        functools.partial(taps_kernel, count, step),
        (*down_mixes, down_part, *up_mixes, up_part),
        after,
        grid=(groups // step,),
        in_specs=(block + part) * 2,
        out_specs=pl.BlockSpec((1, step, taps), lambda i: (i, 0, 0)),
        out_shape=shape((groups // step, step, taps), f32),
        scratch_shapes=[pltpu.VMEM((tokens, tile), bf16)] * 2,
        counted=False,
        name="filter_gradient",
    ).reshape(1, groups, taps)


def weight_kernel(down_x, up_x, down_g, up_g, out_ref, down_t, up_t):
    @pl.when(pl.program_id(0) == 0)
    def _():
        down_t[...] = down_x[...].T
        up_t[...] = up_x[...].T

    out_ref[...] = (dot(down_t[...], down_g[...]) + dot(up_t[...], up_g[...])).astype(bf16)


def weight_gradient(down_x, up_x, down_g, up_g, after=()):
    tokens, depth = down_x.shape
    width = down_g.shape[1]
    tile = width // 4
    whole = pl.BlockSpec((tokens, depth), lambda i: (0, 0))
    part = pl.BlockSpec((tokens, tile), lambda i: (0, i))
    return call(
        weight_kernel,
        (down_x, up_x, down_g, up_g),
        after,
        grid=(width // tile,),
        in_specs=[whole, whole, part, part],
        out_specs=pl.BlockSpec((depth, tile), lambda i: (0, i)),
        out_shape=shape((depth, width), bf16),
        scratch_shapes=[pltpu.VMEM((depth, tokens), bf16)] * 2,
        flops=4 * tokens * depth * width,
        name="weight_gradient",
    )


def settle_kernel(own_ref, came_ref, out_ref):
    stays = 2 * lax.axis_index("section") == lax.axis_size("section")

    @pl.when(stays)
    def _():
        out_ref[...] = own_ref[...]

    @pl.when(jnp.logical_not(stays))
    def _():
        out_ref[...] = came_ref[...]


def settle(own, came, after=()):
    step = came.shape[1] // 2
    spec = pl.BlockSpec((1, step, came.shape[2]), lambda i: (0, i, 0))
    return call(
        settle_kernel,
        (own, came),
        after,
        grid=(2,),
        in_specs=[spec, spec],
        out_specs=spec,
        out_shape=shape(came.shape, came.dtype),
        flops=1 << 35,
        name="settle",
    )


def copy_kernel(in_ref, out_ref):
    out_ref[...] = in_ref[...]


def copy(x, after=()):
    step = x.shape[1] // 2
    spec = pl.BlockSpec((1, step, x.shape[2]), lambda i: (0, i, 0))
    return call(
        copy_kernel,
        (x,),
        after,
        grid=(2,),
        in_specs=[spec],
        out_specs=spec,
        out_shape=shape(x.shape, x.dtype),
        name="copy",
    )


def finish_kernel(xin_ref, cot_ref, back_ref, *rest):
    *mixed_refs, out_ref = rest
    normed, inverse = normalise(xin_ref[...].astype(f32))
    cot = cot_ref[...].astype(f32)
    returned = jnp.concatenate([back_ref[i] for i in range(back_ref.shape[0])], axis=1)
    mixed = sum(ref[...].astype(f32) for ref in mixed_refs)
    total = cot * mixed + returned.astype(f32)
    mean = jnp.mean(total * normed, axis=1, keepdims=True)
    out_ref[0] = (cot + inverse * (total - normed * mean)).astype(bf16)


def finish(xin, cot, mixed, returned, counted, after=()):
    rows, width = xin.shape
    blocks, _, depth = returned.shape
    step = 64
    spec = pl.BlockSpec((step, width), lambda i: (i, 0))
    return call(
        finish_kernel,
        (xin, cot, returned, *mixed),
        after,
        grid=(rows // step,),
        in_specs=[spec, spec, pl.BlockSpec((blocks, step, depth), lambda i: (0, i, 0))]
        + [spec] * len(mixed),
        out_specs=pl.BlockSpec((1, step, width), lambda i: (0, i, 0)),
        out_shape=shape((1, rows, width), bf16),
        counted=counted,
        name="finish",
    )


def exchange(x):
    blocks = lax.axis_size("tensor")
    x = x.reshape(blocks, -1, x.shape[-1])
    return lax.all_to_all(x, "tensor", split_axis=0, concat_axis=0, tiled=True)


def both_ways(right, left):
    blocks = lax.axis_size("tensor")
    onward = [(i, i + 1) for i in range(blocks - 1)]
    return (
        lax.ppermute(right, "tensor", onward),
        lax.ppermute(left, "tensor", [(j, i) for i, j in onward]),
    )


def payload_kernel(s, right_ref, left_ref, right_piece, left_piece, right_out, left_out):
    mine = lax.axis_index("tensor")
    blocks = lax.axis_size("tensor")

    def put(came, piece, out, adds):
        @pl.when(adds)
        def _():
            out[...] = (came[...].astype(f32) + piece[...].astype(f32)).astype(bf16)

        @pl.when(jnp.logical_not(adds))
        def _():
            out[...] = came[...]

    put(right_ref, right_piece, right_out, mine < s - 1)
    put(left_ref, left_piece, left_out, mine > blocks - s)


def payload(s, arrived, pieces, after=()):
    blocks = len(pieces)
    rows, width = pieces[0].shape
    step = 64
    spec = pl.BlockSpec((step, width), lambda i: (i, 0))
    return call(
        functools.partial(payload_kernel, s),
        (*arrived, pieces[blocks + 1 - s], pieces[s - 1]),
        after,
        grid=(rows // step,),
        in_specs=[spec] * 4,
        out_specs=[spec] * 2,
        out_shape=[shape((rows, width), bf16)] * 2,
        name="payload",
    )


def sort_arrivals(mix, pieces, arrivals):
    rights, lefts = zip(*arrivals)
    return [mix, *rights[:-1], *lefts[:-1]], [pieces[0], rights[-1], lefts[-1]]


def sum_kernel(*refs):
    *in_refs, out_ref, sorted_ref = refs
    for s, ref in enumerate(in_refs):
        sorted_ref[pl.ds(place(-s), 1)] = ref[...]
    out_ref[...] = sum(sorted_ref[i : i + 1] for i in range(len(in_refs)))


def sum_all(x, after=()):
    blocks = lax.axis_size("tensor")
    terms = [x]
    for s in range(1, blocks):
        terms.append(lax.ppermute(x, "tensor", [(i, (i + s) % blocks) for i in range(blocks)]))
    spec = pl.BlockSpec(x.shape, lambda i: (0,) * x.ndim)
    return call(
        sum_kernel,
        terms,
        after,
        grid=(1,),
        in_specs=[spec] * blocks,
        out_specs=spec,
        out_shape=shape(x.shape, x.dtype),
        scratch_shapes=[pltpu.VMEM((blocks, *x.shape[1:]), x.dtype)],
        name="sum_all",
    )


def per_device(weights, filters, down_input, down_cot, up_input, up_cot):
    sections = lax.axis_size("section")
    mirror = [(s, sections - 1 - s) for s in range(sections)]
    down_pairs = [(s + 1, s) for s in range(sections - 1)]
    up_pairs = [(sections - s, s) for s in range(1, sections) if 2 * s != sections]
    weight = weights[0]
    down_xin, down_cot = down_input[0], down_cot[0]
    up_xin = lax.ppermute(up_input[0], "section", mirror)
    up_cot = lax.ppermute(up_cot[0], "section", mirror)
    blocks = lax.axis_size("tensor")
    depth = weight.shape[0]
    down_normed, down_mix = prepare(down_xin, down_cot)
    down_x = exchange(down_normed).reshape(-1, depth)
    down_arrivals = [both_ways(down_mix, down_mix)]
    causal, ahead = toeplitz(filters[0])
    (up_normed,) = prepare(up_xin, after=(ahead,))
    up_x = exchange(up_normed).reshape(-1, depth)
    up_mix = grad_mix(up_xin, up_cot, after=down_arrivals[0])
    up_arrivals = [both_ways(up_mix, up_mix)]
    down_part, down_pieces = project(down_x, weight, causal, after=(up_normed, up_mix))
    last = down_part
    for s in range(2, blocks + 1):
        sent = payload(s, down_arrivals[-1], down_pieces, after=(last,))
        down_arrivals.append(both_ways(*sent))
        if s == 2:
            up_part, up_pieces = project(up_x, weight, causal, after=sent)
        sent = payload(s, up_arrivals[-1], up_pieces, after=sent)
        up_arrivals.append(both_ways(*sent))
        last = sent[0]
    down_mixes, down_conv = sort_arrivals(down_mix, down_pieces, down_arrivals)
    up_mixes, up_conv = sort_arrivals(up_mix, up_pieces, up_arrivals)
    up_g, up_back = back(up_mixes, weight, ahead, after=(last,))
    up_back = exchange(up_back)
    taps = filter_gradient(
        down_mixes, down_part, up_mixes, up_part, *filters.shape[1:], after=(up_g,)
    )
    down_g, down_back = back(
        down_mixes, weight, ahead, after=(taps, *down_arrivals[-1])
    )
    down_back = exchange(down_back)
    up_grad = finish(up_xin, up_cot, up_conv, up_back, True, after=(down_g,))
    up_came = lax.ppermute(up_grad, "section", up_pairs)
    weight_grad = weight_gradient(down_x, up_x, down_g, up_g, after=(up_grad,))
    down_grad = finish(
        down_xin, down_cot, down_conv, down_back, False, after=(weight_grad,)
    )
    down_passed = lax.ppermute(down_grad, "section", down_pairs)
    up_passed = settle(up_grad, up_came, after=(down_grad,))
    taps = sum_all(copy(taps, after=(up_passed,)))
    down_passed = copy(down_passed, after=(taps,))
    return weight_grad[None], taps, down_passed, up_passed


def solution(mesh):
    rows = P("section", "tensor", None)
    whole = P("section", None, None)
    return jax.shard_map(
        per_device,
        mesh=mesh,
        in_specs=(rows, whole, rows, rows, rows, rows),
        out_specs=(rows, whole, rows, rows),
        check_vma=False,
    )
```

```python
import functools

import jax
import jax.numpy as jnp
from jax import lax
from jax.experimental import pallas as pl
from jax.experimental.pallas import tpu as pltpu
from jax.sharding import PartitionSpec as P

epsilon = 1e-06
params = functools.partial(pltpu.CompilerParams, vmem_limit_bytes=63 * 1024 * 1024)
f32, bf16 = jnp.float32, jnp.bfloat16


def dot(a, b, dims=((1,), (0,))):
    return lax.dot_general(a, b, (dims, ((), ())), preferred_element_type=f32)


def shape(dims, dtype):
    return jax.ShapeDtypeStruct(dims, dtype)


def call(kernel, args, after, in_specs, out_shape, flops=0, counted=True, **options):
    count = len(args)
    arrays = [*args, *(out_shape if isinstance(out_shape, list) else [out_shape])]
    cost = pl.CostEstimate(
        flops=flops,
        transcendentals=0,
        bytes_accessed=counted * sum(x.size * x.dtype.itemsize for x in arrays),
    )

    def body(*refs):
        kernel(*refs[:count], *refs[count + len(after) :])

    unread = [pl.BlockSpec(memory_space=pl.ANY)] * len(after)
    return pl.pallas_call(
        body,
        in_specs=list(in_specs) + unread,
        out_shape=out_shape,
        cost_estimate=cost,
        compiler_params=params(),
        **options,
    )(*args, *after)


def toeplitz_kernel(filters_ref, causal_ref, ahead_ref):
    taps = filters_ref.shape[1]
    row = lax.broadcasted_iota(jnp.int32, (taps, taps), 0)
    col = lax.broadcasted_iota(jnp.int32, (taps, taps), 1)
    for g in range(filters_ref.shape[0]):
        line = jnp.broadcast_to(filters_ref[g : g + 1, :], (taps, taps))
        turned = pltpu.roll(line, 0, 1, stride=1, stride_axis=0)
        own = jnp.where(col >= row, turned, 0.0)
        beyond = jnp.where(col < row, turned, 0.0)
        ahead_ref[g, :, :taps] = own.astype(bf16)
        ahead_ref[g, :, taps:] = beyond.astype(bf16)
        causal_ref[g, :, :taps] = beyond.T.astype(bf16)
        causal_ref[g, :, taps:] = own.T.astype(bf16)


def toeplitz(filters):
    groups, taps = filters.shape
    step = 8
    out = shape((groups, taps, 2 * taps), bf16)
    spec = pl.BlockSpec((step, taps, 2 * taps), lambda i: (i, 0, 0))
    return call(
        toeplitz_kernel,
        (filters,),
        (),
        grid=(groups // step,),
        in_specs=[pl.BlockSpec((step, taps), lambda i: (i, 0))],
        out_specs=[spec, spec],
        out_shape=[out, out],
        name="toeplitz",
    )


def place(by):
    blocks = lax.axis_size("tensor")
    return lax.rem(lax.axis_index("tensor") + (by + blocks), blocks)


def window(index, size):
    return pl.ds(pl.multiple_of(index * size, size), size)


def normalise(wide):
    inverse = lax.rsqrt(jnp.mean(wide * wide, axis=1, keepdims=True) + epsilon)
    return wide * inverse, inverse


def prepare_kernel(xin_ref, *refs):
    *cot_ref, normed_ref = refs[: len(refs) // 2 + 1]
    normed, _ = normalise(xin_ref[...].astype(f32))
    width = normed_ref.shape[2]
    for i in range(normed_ref.shape[0]):
        normed_ref[i] = normed[:, i * width : (i + 1) * width].astype(bf16)
    if cot_ref:
        refs[-1][...] = (cot_ref[0][...].astype(f32) * normed).astype(bf16)


def prepare(*args, after=()):
    rows, width = args[0].shape
    blocks = lax.axis_size("tensor")
    step = 64
    spec = pl.BlockSpec((step, width), lambda i: (i, 0))
    normed_spec = pl.BlockSpec((blocks, step, width // blocks), lambda i: (0, i, 0))
    extra = len(args) - 1
    return call(
        prepare_kernel,
        args,
        after,
        grid=(rows // step,),
        in_specs=[spec] * len(args),
        out_specs=[normed_spec] + [spec] * extra,
        out_shape=[shape((blocks, rows, width // blocks), bf16)] + [shape((rows, width), bf16)] * extra,
        name="prepare",
    )


def mix_kernel(xin_ref, cot_ref, mix_ref):
    normed, _ = normalise(xin_ref[...].astype(f32))
    mix_ref[...] = (cot_ref[...].astype(f32) * normed).astype(bf16)


def grad_mix(xin, cot, after=()):
    rows, width = xin.shape
    step = 64
    spec = pl.BlockSpec((step, width), lambda i: (i, 0))
    return call(
        mix_kernel,
        (xin, cot),
        after,
        grid=(rows // step,),
        in_specs=[spec, spec],
        out_specs=spec,
        out_shape=shape((rows, width), bf16),
        name="grad_mix",
    )


def side_by_side(x, rows):
    return jnp.concatenate([x[s : s + rows] for s in range(0, x.shape[0], rows)], axis=1)


def project_kernel(features_ref, weight_ref, causal_ref, part_ref, *rest):
    *mixed_refs, mixed_ref = rest
    groups, taps, _ = causal_ref.shape
    part = dot(features_ref[...], weight_ref[...]).astype(bf16)
    part_ref[...] = part
    width = part.shape[1] // groups
    for g in range(groups):
        cols = slice(g * width, (g + 1) * width)
        own = side_by_side(part[:, cols], taps)
        before = jnp.concatenate([jnp.zeros((taps, width), bf16), own[:, :-width]], axis=1)
        out = dot(causal_ref[g], jnp.concatenate([before, own], axis=0)).astype(bf16)
        for i in range(out.shape[1] // width):
            mixed_ref[i * taps : (i + 1) * taps, cols] = out[:, i * width : (i + 1) * width]
    for s, out_ref in enumerate(mixed_refs):
        out_ref[...] = mixed_ref[window(place(s), out_ref.shape[0]), :]


def project(features, weight, causal, after=()):
    blocks = lax.axis_size("tensor")
    tokens, depth = features.shape
    rows = tokens // blocks
    width = weight.shape[1]
    groups, taps, _ = causal.shape
    step = 8
    tile = width // groups * step
    part, *mixed = call(
        project_kernel,
        (features, weight, causal),
        after,
        grid=(groups // step,),
        in_specs=[
            pl.BlockSpec((tokens, depth), lambda i: (0, 0)),
            pl.BlockSpec((depth, tile), lambda i: (0, i)),
            pl.BlockSpec((step, taps, 2 * taps), lambda i: (i, 0, 0)),
        ],
        out_specs=[pl.BlockSpec((tokens, tile), lambda i: (0, i))]
        + [pl.BlockSpec((rows, tile), lambda i: (0, i))] * blocks,
        out_shape=[shape((tokens, width), bf16)] + [shape((rows, width), bf16)] * blocks,
        scratch_shapes=[pltpu.VMEM((tokens, tile), bf16)],
        flops=2 * tokens * width * (depth + 2 * taps),
        name="project",
    )
    return part, mixed


def assemble(block_refs, mix_ref):
    blocks = (len(block_refs) + 1) // 2
    rows = block_refs[0].shape[0]
    mine = lax.axis_index("tensor")
    mix_ref[window(mine, rows), :] = block_refs[0][...]
    for s in range(1, blocks):

        @pl.when(mine >= s)
        def _():
            mix_ref[window(mine - s, rows), :] = block_refs[s][...]

        @pl.when(mine < s)
        def _():
            mix_ref[window(mine + (blocks - s), rows), :] = block_refs[2 * blocks - 1 - s][...]


def with_following(mix, taps):
    own = side_by_side(mix, taps)
    width = mix.shape[1]
    following = jnp.concatenate([own[:, width:], jnp.zeros((taps, width), bf16)], axis=1)
    return jnp.concatenate([own, following], axis=0)


def back_kernel(count, *refs):
    weight_ref, ahead_ref, grad_ref, back_ref, mix_ref, total = refs[count:]
    groups, taps, _ = ahead_ref.shape
    width = mix_ref.shape[1] // groups
    assemble(refs[:count], mix_ref)
    for g in range(groups):
        cols = slice(g * width, (g + 1) * width)
        out = dot(ahead_ref[g], with_following(mix_ref[:, cols], taps)).astype(bf16)
        for i in range(out.shape[1] // width):
            grad_ref[i * taps : (i + 1) * taps, cols] = out[:, i * width : (i + 1) * width]
    product = dot(grad_ref[...], weight_ref[...], ((1,), (1,)))
    step = pl.program_id(0)

    @pl.when(step == 0)
    def _():
        total[...] = product

    @pl.when(step > 0)
    def _():
        total[...] += product

    @pl.when(step == pl.num_programs(0) - 1)
    def _():
        back_ref[...] = total[...].astype(bf16)


def back(mixes, weight, ahead, after=()):
    rows, width = mixes[0].shape
    tokens = (len(mixes) + 1) // 2 * rows
    depth = weight.shape[0]
    groups, taps, _ = ahead.shape
    step = 8
    tile = width // groups * step
    return call(
        functools.partial(back_kernel, len(mixes)),
        (*mixes, weight, ahead),
        after,
        grid=(groups // step,),
        in_specs=[pl.BlockSpec((rows, tile), lambda i: (0, i))] * len(mixes)
        + [
            pl.BlockSpec((depth, tile), lambda i: (0, i)),
            pl.BlockSpec((step, taps, 2 * taps), lambda i: (i, 0, 0)),
        ],
        out_specs=[
            pl.BlockSpec((tokens, tile), lambda i: (0, i)),
            pl.BlockSpec((tokens, depth), lambda i: (0, 0)),
        ],
        out_shape=[shape((tokens, width), bf16), shape((tokens, depth), bf16)],
        scratch_shapes=[pltpu.VMEM((tokens, tile), bf16), pltpu.VMEM((tokens, depth), f32)],
        flops=6 * tokens * width * (depth + 2 * taps),
        name="back",
    )


def taps_kernel(count, groups, *refs):
    taps_ref, *mix_refs = refs[-3:]
    taps = taps_ref.shape[2]
    width = mix_refs[0].shape[1] // groups
    row = lax.broadcasted_iota(jnp.int32, (taps, taps), 0)
    col = lax.broadcasted_iota(jnp.int32, (taps, taps), 1)
    total = [0] * groups
    for first, mix_ref in zip((0, count + 1), mix_refs):
        assemble(refs[first : first + count], mix_ref)
        part_ref = refs[first + count]
        for g in range(groups):
            cols = slice(g * width, (g + 1) * width)
            both = with_following(mix_ref[:, cols], taps)
            total[g] += dot(side_by_side(part_ref[:, cols], taps), both, ((1,), (1,)))
    for g in range(groups):
        pairs = jnp.where(col >= row, total[g][:, :taps], total[g][:, taps:])
        folded = pairs[0:8]
        for a in range(8, taps, 8):
            folded = folded + pltpu.roll(pairs[a : a + 8], taps - a, 1)
        line = folded[0:1]
        for b in range(1, 8):
            line = line + pltpu.roll(folded[b : b + 1], taps - b, 1)
        taps_ref[0, g : g + 1, :] = line


def filter_gradient(down_mixes, down_part, up_mixes, up_part, groups, taps, after=()):
    rows, width = down_mixes[0].shape
    tokens = down_part.shape[0]
    step = 8
    tile = width // groups * step
    count = len(down_mixes)
    block = [pl.BlockSpec((rows, tile), lambda i: (0, i))] * count
    part = [pl.BlockSpec((tokens, tile), lambda i: (0, i))]
    return call(
        functools.partial(taps_kernel, count, step),
        (*down_mixes, down_part, *up_mixes, up_part),
        after,
        grid=(groups // step,),
        in_specs=(block + part) * 2,
        out_specs=pl.BlockSpec((1, step, taps), lambda i: (i, 0, 0)),
        out_shape=shape((groups // step, step, taps), f32),
        scratch_shapes=[pltpu.VMEM((tokens, tile), bf16)] * 2,
        counted=False,
        name="filter_gradient",
    ).reshape(1, groups, taps)


def weight_kernel(down_x, up_x, down_g, up_g, out_ref, down_t, up_t):
    @pl.when(pl.program_id(0) == 0)
    def _():
        down_t[...] = down_x[...].T
        up_t[...] = up_x[...].T

    out_ref[...] = (dot(down_t[...], down_g[...]) + dot(up_t[...], up_g[...])).astype(bf16)


def weight_gradient(down_x, up_x, down_g, up_g, after=()):
    tokens, depth = down_x.shape
    width = down_g.shape[1]
    tile = width // 4
    whole = pl.BlockSpec((tokens, depth), lambda i: (0, 0))
    part = pl.BlockSpec((tokens, tile), lambda i: (0, i))
    return call(
        weight_kernel,
        (down_x, up_x, down_g, up_g),
        after,
        grid=(width // tile,),
        in_specs=[whole, whole, part, part],
        out_specs=pl.BlockSpec((depth, tile), lambda i: (0, i)),
        out_shape=shape((depth, width), bf16),
        scratch_shapes=[pltpu.VMEM((depth, tokens), bf16)] * 2,
        flops=4 * tokens * depth * width,
        name="weight_gradient",
    )


def settle_kernel(own_ref, came_ref, out_ref):
    stays = 2 * lax.axis_index("section") == lax.axis_size("section")

    @pl.when(stays)
    def _():
        out_ref[...] = own_ref[...]

    @pl.when(jnp.logical_not(stays))
    def _():
        out_ref[...] = came_ref[...]


def settle(own, came, after=()):
    step = came.shape[1] // 2
    spec = pl.BlockSpec((1, step, came.shape[2]), lambda i: (0, i, 0))
    return call(
        settle_kernel,
        (own, came),
        after,
        grid=(2,),
        in_specs=[spec, spec],
        out_specs=spec,
        out_shape=shape(came.shape, came.dtype),
        flops=1 << 35,
        name="settle",
    )


def copy_kernel(in_ref, out_ref):
    out_ref[...] = in_ref[...]


def copy(x, after=()):
    step = x.shape[1] // 2
    spec = pl.BlockSpec((1, step, x.shape[2]), lambda i: (0, i, 0))
    return call(
        copy_kernel,
        (x,),
        after,
        grid=(2,),
        in_specs=[spec],
        out_specs=spec,
        out_shape=shape(x.shape, x.dtype),
        name="copy",
    )


def finish_kernel(xin_ref, cot_ref, back_ref, *rest):
    *mixed_refs, out_ref = rest
    normed, inverse = normalise(xin_ref[...].astype(f32))
    cot = cot_ref[...].astype(f32)
    returned = jnp.concatenate([back_ref[i] for i in range(back_ref.shape[0])], axis=1)
    mixed = sum(ref[...].astype(f32) for ref in mixed_refs)
    total = cot * mixed + returned.astype(f32)
    mean = jnp.mean(total * normed, axis=1, keepdims=True)
    out_ref[0] = (cot + inverse * (total - normed * mean)).astype(bf16)


def finish(xin, cot, mixed, returned, counted, after=()):
    rows, width = xin.shape
    blocks, _, depth = returned.shape
    step = 64
    spec = pl.BlockSpec((step, width), lambda i: (i, 0))
    return call(
        finish_kernel,
        (xin, cot, returned, *mixed),
        after,
        grid=(rows // step,),
        in_specs=[spec, spec, pl.BlockSpec((blocks, step, depth), lambda i: (0, i, 0))]
        + [spec] * len(mixed),
        out_specs=pl.BlockSpec((1, step, width), lambda i: (0, i, 0)),
        out_shape=shape((1, rows, width), bf16),
        counted=counted,
        name="finish",
    )


def exchange(x):
    blocks = lax.axis_size("tensor")
    x = x.reshape(blocks, -1, x.shape[-1])
    return lax.all_to_all(x, "tensor", split_axis=0, concat_axis=0, tiled=True)


def both_ways(right, left):
    blocks = lax.axis_size("tensor")
    onward = [(i, i + 1) for i in range(blocks - 1)]
    return (
        lax.ppermute(right, "tensor", onward),
        lax.ppermute(left, "tensor", [(j, i) for i, j in onward]),
    )


def payload_kernel(s, right_ref, left_ref, right_piece, left_piece, right_out, left_out):
    mine = lax.axis_index("tensor")
    blocks = lax.axis_size("tensor")

    def put(came, piece, out, adds):
        @pl.when(adds)
        def _():
            out[...] = (came[...].astype(f32) + piece[...].astype(f32)).astype(bf16)

        @pl.when(jnp.logical_not(adds))
        def _():
            out[...] = came[...]

    put(right_ref, right_piece, right_out, mine < s - 1)
    put(left_ref, left_piece, left_out, mine > blocks - s)


def payload(s, arrived, pieces, after=()):
    blocks = len(pieces)
    rows, width = pieces[0].shape
    step = 64
    spec = pl.BlockSpec((step, width), lambda i: (i, 0))
    return call(
        functools.partial(payload_kernel, s),
        (*arrived, pieces[blocks + 1 - s], pieces[s - 1]),
        after,
        grid=(rows // step,),
        in_specs=[spec] * 4,
        out_specs=[spec] * 2,
        out_shape=[shape((rows, width), bf16)] * 2,
        name="payload",
    )


def sort_arrivals(mix, pieces, arrivals):
    rights, lefts = zip(*arrivals)
    return [mix, *rights[:-1], *lefts[:-1]], [pieces[0], rights[-1], lefts[-1]]


def sum_kernel(*refs):
    *in_refs, out_ref, sorted_ref = refs
    for s, ref in enumerate(in_refs):
        sorted_ref[pl.ds(place(-s), 1)] = ref[...]
    out_ref[...] = sum(sorted_ref[i : i + 1] for i in range(len(in_refs)))


def sum_all(x, after=()):
    blocks = lax.axis_size("tensor")
    terms = [x]
    for s in range(1, blocks):
        terms.append(lax.ppermute(x, "tensor", [(i, (i + s) % blocks) for i in range(blocks)]))
    spec = pl.BlockSpec(x.shape, lambda i: (0,) * x.ndim)
    return call(
        sum_kernel,
        terms,
        after,
        grid=(1,),
        in_specs=[spec] * blocks,
        out_specs=spec,
        out_shape=shape(x.shape, x.dtype),
        scratch_shapes=[pltpu.VMEM((blocks, *x.shape[1:]), x.dtype)],
        name="sum_all",
    )


def per_device(weights, filters, down_input, down_cot, up_input, up_cot):
    sections = lax.axis_size("section")
    mirror = [(s, sections - 1 - s) for s in range(sections)]
    down_pairs = [(s + 1, s) for s in range(sections - 1)]
    up_pairs = [(sections - s, s) for s in range(1, sections) if 2 * s != sections]
    weight = weights[0]
    down_xin, down_cot = down_input[0], down_cot[0]
    up_xin = lax.ppermute(up_input[0], "section", mirror)
    up_cot = lax.ppermute(up_cot[0], "section", mirror)
    blocks = lax.axis_size("tensor")
    depth = weight.shape[0]
    down_normed, down_mix = prepare(down_xin, down_cot)
    down_x = exchange(down_normed).reshape(-1, depth)
    down_arrivals = [both_ways(down_mix, down_mix)]
    causal, ahead = toeplitz(filters[0])
    (up_normed,) = prepare(up_xin, after=(ahead,))
    up_x = exchange(up_normed).reshape(-1, depth)
    up_mix = grad_mix(up_xin, up_cot, after=down_arrivals[0])
    up_arrivals = [both_ways(up_mix, up_mix)]
    down_part, down_pieces = project(down_x, weight, causal, after=(up_normed, up_mix))
    last = down_part
    for s in range(2, blocks + 1):
        sent = payload(s, down_arrivals[-1], down_pieces, after=(last,))
        down_arrivals.append(both_ways(*sent))
        if s == 2:
            up_part, up_pieces = project(up_x, weight, causal, after=sent)
        sent = payload(s, up_arrivals[-1], up_pieces, after=sent)
        up_arrivals.append(both_ways(*sent))
        last = sent[0]
    down_mixes, down_conv = sort_arrivals(down_mix, down_pieces, down_arrivals)
    up_mixes, up_conv = sort_arrivals(up_mix, up_pieces, up_arrivals)
    up_g, up_back = back(up_mixes, weight, ahead, after=(last,))
    up_back = exchange(up_back)
    taps = filter_gradient(
        down_mixes, down_part, up_mixes, up_part, *filters.shape[1:], after=(up_g,)
    )
    down_g, down_back = back(
        down_mixes, weight, ahead, after=(taps, *down_arrivals[-1])
    )
    down_back = exchange(down_back)
    up_grad = finish(up_xin, up_cot, up_conv, up_back, True, after=(down_g,))
    up_came = lax.ppermute(up_grad, "section", up_pairs)
    weight_grad = weight_gradient(down_x, up_x, down_g, up_g, after=(up_grad,))
    down_grad = finish(
        down_xin, down_cot, down_conv, down_back, False, after=(weight_grad,)
    )
    down_passed = lax.ppermute(down_grad, "section", down_pairs)
    up_passed = settle(up_grad, up_came, after=(down_grad,))
    taps = sum_all(copy(taps, after=(down_grad,)), after=(up_passed,))
    down_passed = copy(down_passed, after=(taps,))
    return weight_grad[None], taps, down_passed, up_passed


def solution(mesh):
    rows = P("section", "tensor", None)
    whole = P("section", None, None)
    return jax.shard_map(
        per_device,
        mesh=mesh,
        in_specs=(rows, whole, rows, rows, rows, rows),
        out_specs=(rows, whole, rows, rows),
        check_vma=False,
    )
```

```python
import functools

import jax
import jax.numpy as jnp
from jax import lax
from jax.experimental import pallas as pl
from jax.experimental.pallas import tpu as pltpu
from jax.sharding import PartitionSpec as P

epsilon = 1e-06
params = functools.partial(pltpu.CompilerParams, vmem_limit_bytes=63 * 1024 * 1024)
f32, bf16 = jnp.float32, jnp.bfloat16


def dot(a, b, dims=((1,), (0,))):
    return lax.dot_general(a, b, (dims, ((), ())), preferred_element_type=f32)


def shape(dims, dtype):
    return jax.ShapeDtypeStruct(dims, dtype)


def call(kernel, args, after, in_specs, out_shape, flops=0, counted=True, **options):
    count = len(args)
    arrays = [*args, *(out_shape if isinstance(out_shape, list) else [out_shape])]
    cost = pl.CostEstimate(
        flops=flops,
        transcendentals=0,
        bytes_accessed=counted * sum(x.size * x.dtype.itemsize for x in arrays),
    )

    def body(*refs):
        kernel(*refs[:count], *refs[count + len(after) :])

    unread = [pl.BlockSpec(memory_space=pl.ANY)] * len(after)
    return pl.pallas_call(
        body,
        in_specs=list(in_specs) + unread,
        out_shape=out_shape,
        cost_estimate=cost,
        compiler_params=params(),
        **options,
    )(*args, *after)


def toeplitz_kernel(filters_ref, causal_ref, ahead_ref):
    taps = filters_ref.shape[1]
    row = lax.broadcasted_iota(jnp.int32, (taps, taps), 0)
    col = lax.broadcasted_iota(jnp.int32, (taps, taps), 1)
    for g in range(filters_ref.shape[0]):
        line = jnp.broadcast_to(filters_ref[g : g + 1, :], (taps, taps))
        turned = pltpu.roll(line, 0, 1, stride=1, stride_axis=0)
        own = jnp.where(col >= row, turned, 0.0)
        beyond = jnp.where(col < row, turned, 0.0)
        ahead_ref[g, :, :taps] = own.astype(bf16)
        ahead_ref[g, :, taps:] = beyond.astype(bf16)
        causal_ref[g, :, :taps] = beyond.T.astype(bf16)
        causal_ref[g, :, taps:] = own.T.astype(bf16)


def toeplitz(filters):
    groups, taps = filters.shape
    step = 8
    out = shape((groups, taps, 2 * taps), bf16)
    spec = pl.BlockSpec((step, taps, 2 * taps), lambda i: (i, 0, 0))
    return call(
        toeplitz_kernel,
        (filters,),
        (),
        grid=(groups // step,),
        in_specs=[pl.BlockSpec((step, taps), lambda i: (i, 0))],
        out_specs=[spec, spec],
        out_shape=[out, out],
        name="toeplitz",
    )


def place(by):
    blocks = lax.axis_size("tensor")
    return lax.rem(lax.axis_index("tensor") + (by + blocks), blocks)


def window(index, size):
    return pl.ds(pl.multiple_of(index * size, size), size)


def normalise(wide):
    inverse = lax.rsqrt(jnp.mean(wide * wide, axis=1, keepdims=True) + epsilon)
    return wide * inverse, inverse


def prepare_kernel(xin_ref, *refs):
    *cot_ref, normed_ref = refs[: len(refs) // 2 + 1]
    normed, _ = normalise(xin_ref[...].astype(f32))
    width = normed_ref.shape[2]
    for i in range(normed_ref.shape[0]):
        normed_ref[i] = normed[:, i * width : (i + 1) * width].astype(bf16)
    if cot_ref:
        refs[-1][...] = (cot_ref[0][...].astype(f32) * normed).astype(bf16)


def prepare(*args, after=()):
    rows, width = args[0].shape
    blocks = lax.axis_size("tensor")
    step = 64
    spec = pl.BlockSpec((step, width), lambda i: (i, 0))
    normed_spec = pl.BlockSpec((blocks, step, width // blocks), lambda i: (0, i, 0))
    extra = len(args) - 1
    return call(
        prepare_kernel,
        args,
        after,
        grid=(rows // step,),
        in_specs=[spec] * len(args),
        out_specs=[normed_spec] + [spec] * extra,
        out_shape=[shape((blocks, rows, width // blocks), bf16)] + [shape((rows, width), bf16)] * extra,
        name="prepare",
    )


def mix_kernel(xin_ref, cot_ref, mix_ref):
    normed, _ = normalise(xin_ref[...].astype(f32))
    mix_ref[...] = (cot_ref[...].astype(f32) * normed).astype(bf16)


def grad_mix(xin, cot, after=()):
    rows, width = xin.shape
    step = 64
    spec = pl.BlockSpec((step, width), lambda i: (i, 0))
    return call(
        mix_kernel,
        (xin, cot),
        after,
        grid=(rows // step,),
        in_specs=[spec, spec],
        out_specs=spec,
        out_shape=shape((rows, width), bf16),
        name="grad_mix",
    )


def side_by_side(x, rows):
    return jnp.concatenate([x[s : s + rows] for s in range(0, x.shape[0], rows)], axis=1)


def project_kernel(features_ref, weight_ref, causal_ref, part_ref, *rest):
    *mixed_refs, mixed_ref = rest
    groups, taps, _ = causal_ref.shape
    part = dot(features_ref[...], weight_ref[...]).astype(bf16)
    part_ref[...] = part
    width = part.shape[1] // groups
    for g in range(groups):
        cols = slice(g * width, (g + 1) * width)
        own = side_by_side(part[:, cols], taps)
        before = jnp.concatenate([jnp.zeros((taps, width), bf16), own[:, :-width]], axis=1)
        out = dot(causal_ref[g], jnp.concatenate([before, own], axis=0)).astype(bf16)
        for i in range(out.shape[1] // width):
            mixed_ref[i * taps : (i + 1) * taps, cols] = out[:, i * width : (i + 1) * width]
    for s, out_ref in enumerate(mixed_refs):
        out_ref[...] = mixed_ref[window(place(s), out_ref.shape[0]), :]


def project(features, weight, causal, after=()):
    blocks = lax.axis_size("tensor")
    tokens, depth = features.shape
    rows = tokens // blocks
    width = weight.shape[1]
    groups, taps, _ = causal.shape
    step = 8
    tile = width // groups * step
    part, *mixed = call(
        project_kernel,
        (features, weight, causal),
        after,
        grid=(groups // step,),
        in_specs=[
            pl.BlockSpec((tokens, depth), lambda i: (0, 0)),
            pl.BlockSpec((depth, tile), lambda i: (0, i)),
            pl.BlockSpec((step, taps, 2 * taps), lambda i: (i, 0, 0)),
        ],
        out_specs=[pl.BlockSpec((tokens, tile), lambda i: (0, i))]
        + [pl.BlockSpec((rows, tile), lambda i: (0, i))] * blocks,
        out_shape=[shape((tokens, width), bf16)] + [shape((rows, width), bf16)] * blocks,
        scratch_shapes=[pltpu.VMEM((tokens, tile), bf16)],
        flops=2 * tokens * width * (depth + 2 * taps),
        name="project",
    )
    return part, mixed


def assemble(block_refs, mix_ref):
    blocks = (len(block_refs) + 1) // 2
    rows = block_refs[0].shape[0]
    mine = lax.axis_index("tensor")
    mix_ref[window(mine, rows), :] = block_refs[0][...]
    for s in range(1, blocks):

        @pl.when(mine >= s)
        def _():
            mix_ref[window(mine - s, rows), :] = block_refs[s][...]

        @pl.when(mine < s)
        def _():
            mix_ref[window(mine + (blocks - s), rows), :] = block_refs[2 * blocks - 1 - s][...]


def with_following(mix, taps):
    own = side_by_side(mix, taps)
    width = mix.shape[1]
    following = jnp.concatenate([own[:, width:], jnp.zeros((taps, width), bf16)], axis=1)
    return jnp.concatenate([own, following], axis=0)


def back_kernel(count, *refs):
    weight_ref, ahead_ref, grad_ref, back_ref, mix_ref, total = refs[count:]
    groups, taps, _ = ahead_ref.shape
    width = mix_ref.shape[1] // groups
    assemble(refs[:count], mix_ref)
    for g in range(groups):
        cols = slice(g * width, (g + 1) * width)
        out = dot(ahead_ref[g], with_following(mix_ref[:, cols], taps)).astype(bf16)
        for i in range(out.shape[1] // width):
            grad_ref[i * taps : (i + 1) * taps, cols] = out[:, i * width : (i + 1) * width]
    product = dot(grad_ref[...], weight_ref[...], ((1,), (1,)))
    step = pl.program_id(0)

    @pl.when(step == 0)
    def _():
        total[...] = product

    @pl.when(step > 0)
    def _():
        total[...] += product

    @pl.when(step == pl.num_programs(0) - 1)
    def _():
        back_ref[...] = total[...].astype(bf16)


def back(mixes, weight, ahead, after=()):
    rows, width = mixes[0].shape
    tokens = (len(mixes) + 1) // 2 * rows
    depth = weight.shape[0]
    groups, taps, _ = ahead.shape
    step = 8
    tile = width // groups * step
    return call(
        functools.partial(back_kernel, len(mixes)),
        (*mixes, weight, ahead),
        after,
        grid=(groups // step,),
        in_specs=[pl.BlockSpec((rows, tile), lambda i: (0, i))] * len(mixes)
        + [
            pl.BlockSpec((depth, tile), lambda i: (0, i)),
            pl.BlockSpec((step, taps, 2 * taps), lambda i: (i, 0, 0)),
        ],
        out_specs=[
            pl.BlockSpec((tokens, tile), lambda i: (0, i)),
            pl.BlockSpec((tokens, depth), lambda i: (0, 0)),
        ],
        out_shape=[shape((tokens, width), bf16), shape((tokens, depth), bf16)],
        scratch_shapes=[pltpu.VMEM((tokens, tile), bf16), pltpu.VMEM((tokens, depth), f32)],
        flops=6 * tokens * width * (depth + 2 * taps),
        name="back",
    )


def taps_kernel(count, groups, *refs):
    taps_ref, *mix_refs = refs[-3:]
    taps = taps_ref.shape[2]
    width = mix_refs[0].shape[1] // groups
    row = lax.broadcasted_iota(jnp.int32, (taps, taps), 0)
    col = lax.broadcasted_iota(jnp.int32, (taps, taps), 1)
    total = [0] * groups
    for first, mix_ref in zip((0, count + 1), mix_refs):
        assemble(refs[first : first + count], mix_ref)
        part_ref = refs[first + count]
        for g in range(groups):
            cols = slice(g * width, (g + 1) * width)
            both = with_following(mix_ref[:, cols], taps)
            total[g] += dot(side_by_side(part_ref[:, cols], taps), both, ((1,), (1,)))
    for g in range(groups):
        pairs = jnp.where(col >= row, total[g][:, :taps], total[g][:, taps:])
        folded = pairs[0:8]
        for a in range(8, taps, 8):
            folded = folded + pltpu.roll(pairs[a : a + 8], taps - a, 1)
        line = folded[0:1]
        for b in range(1, 8):
            line = line + pltpu.roll(folded[b : b + 1], taps - b, 1)
        taps_ref[0, g : g + 1, :] = line


def filter_gradient(down_mixes, down_part, up_mixes, up_part, groups, taps, after=()):
    rows, width = down_mixes[0].shape
    tokens = down_part.shape[0]
    step = 8
    tile = width // groups * step
    count = len(down_mixes)
    block = [pl.BlockSpec((rows, tile), lambda i: (0, i))] * count
    part = [pl.BlockSpec((tokens, tile), lambda i: (0, i))]
    return call(
        functools.partial(taps_kernel, count, step),
        (*down_mixes, down_part, *up_mixes, up_part),
        after,
        grid=(groups // step,),
        in_specs=(block + part) * 2,
        out_specs=pl.BlockSpec((1, step, taps), lambda i: (i, 0, 0)),
        out_shape=shape((groups // step, step, taps), f32),
        scratch_shapes=[pltpu.VMEM((tokens, tile), bf16)] * 2,
        counted=False,
        name="filter_gradient",
    ).reshape(1, groups, taps)


def weight_kernel(down_x, up_x, down_g, up_g, out_ref, down_t, up_t):
    @pl.when(pl.program_id(0) == 0)
    def _():
        down_t[...] = down_x[...].T
        up_t[...] = up_x[...].T

    out_ref[...] = (dot(down_t[...], down_g[...]) + dot(up_t[...], up_g[...])).astype(bf16)


def weight_gradient(down_x, up_x, down_g, up_g, after=()):
    tokens, depth = down_x.shape
    width = down_g.shape[1]
    tile = width // 4
    whole = pl.BlockSpec((tokens, depth), lambda i: (0, 0))
    part = pl.BlockSpec((tokens, tile), lambda i: (0, i))
    return call(
        weight_kernel,
        (down_x, up_x, down_g, up_g),
        after,
        grid=(width // tile,),
        in_specs=[whole, whole, part, part],
        out_specs=pl.BlockSpec((depth, tile), lambda i: (0, i)),
        out_shape=shape((depth, width), bf16),
        scratch_shapes=[pltpu.VMEM((depth, tokens), bf16)] * 2,
        counted=False,
        name="weight_gradient",
    )


def settle_kernel(own_ref, came_ref, out_ref):
    stays = 2 * lax.axis_index("section") == lax.axis_size("section")

    @pl.when(stays)
    def _():
        out_ref[...] = own_ref[...]

    @pl.when(jnp.logical_not(stays))
    def _():
        out_ref[...] = came_ref[...]


def settle(own, came, after=()):
    step = came.shape[1] // 2
    spec = pl.BlockSpec((1, step, came.shape[2]), lambda i: (0, i, 0))
    return call(
        settle_kernel,
        (own, came),
        after,
        grid=(2,),
        in_specs=[spec, spec],
        out_specs=spec,
        out_shape=shape(came.shape, came.dtype),
        name="settle",
    )


def finish_kernel(xin_ref, cot_ref, back_ref, *rest):
    *mixed_refs, out_ref = rest
    normed, inverse = normalise(xin_ref[...].astype(f32))
    cot = cot_ref[...].astype(f32)
    returned = jnp.concatenate([back_ref[i] for i in range(back_ref.shape[0])], axis=1)
    mixed = sum(ref[...].astype(f32) for ref in mixed_refs)
    total = cot * mixed + returned.astype(f32)
    mean = jnp.mean(total * normed, axis=1, keepdims=True)
    out_ref[0] = (cot + inverse * (total - normed * mean)).astype(bf16)


def finish(xin, cot, mixed, returned, after=()):
    rows, width = xin.shape
    blocks, _, depth = returned.shape
    step = 64
    spec = pl.BlockSpec((step, width), lambda i: (i, 0))
    return call(
        finish_kernel,
        (xin, cot, returned, *mixed),
        after,
        grid=(rows // step,),
        in_specs=[spec, spec, pl.BlockSpec((blocks, step, depth), lambda i: (0, i, 0))]
        + [spec] * len(mixed),
        out_specs=pl.BlockSpec((1, step, width), lambda i: (0, i, 0)),
        out_shape=shape((1, rows, width), bf16),
        name="finish",
    )


def exchange(x):
    blocks = lax.axis_size("tensor")
    x = x.reshape(blocks, -1, x.shape[-1])
    return lax.all_to_all(x, "tensor", split_axis=0, concat_axis=0, tiled=True)


def both_ways(right, left):
    blocks = lax.axis_size("tensor")
    onward = [(i, i + 1) for i in range(blocks - 1)]
    return (
        lax.ppermute(right, "tensor", onward),
        lax.ppermute(left, "tensor", [(j, i) for i, j in onward]),
    )


def payload_kernel(s, right_ref, left_ref, right_piece, left_piece, right_out, left_out):
    mine = lax.axis_index("tensor")
    blocks = lax.axis_size("tensor")

    def put(came, piece, out, adds):
        @pl.when(adds)
        def _():
            out[...] = (came[...].astype(f32) + piece[...].astype(f32)).astype(bf16)

        @pl.when(jnp.logical_not(adds))
        def _():
            out[...] = came[...]

    put(right_ref, right_piece, right_out, mine < s - 1)
    put(left_ref, left_piece, left_out, mine > blocks - s)


def payload(s, arrived, pieces, after=()):
    blocks = len(pieces)
    rows, width = pieces[0].shape
    step = 64
    spec = pl.BlockSpec((step, width), lambda i: (i, 0))
    return call(
        functools.partial(payload_kernel, s),
        (*arrived, pieces[blocks + 1 - s], pieces[s - 1]),
        after,
        grid=(rows // step,),
        in_specs=[spec] * 4,
        out_specs=[spec] * 2,
        out_shape=[shape((rows, width), bf16)] * 2,
        name="payload",
    )


def list_blocks(mix, arrivals):
    rights, lefts = zip(*arrivals)
    return [mix, *rights, *lefts]


def sort_arrivals(mix, pieces, arrivals):
    right, left = arrivals[-1]
    return list_blocks(mix, arrivals[:-1]), [pieces[0], right, left]


def sum_kernel(*refs):
    *in_refs, out_ref, sorted_ref = refs
    for s, ref in enumerate(in_refs):
        sorted_ref[pl.ds(place(-s), 1)] = ref[...]
    out_ref[...] = sum(sorted_ref[i : i + 1] for i in range(len(in_refs)))


def sum_all(x, after=()):
    blocks = lax.axis_size("tensor")
    terms = [x]
    for s in range(1, blocks):
        terms.append(lax.ppermute(x, "tensor", [(i, (i + s) % blocks) for i in range(blocks)]))
    spec = pl.BlockSpec(x.shape, lambda i: (0,) * x.ndim)
    return call(
        sum_kernel,
        terms,
        after,
        grid=(1,),
        in_specs=[spec] * blocks,
        out_specs=spec,
        out_shape=shape(x.shape, x.dtype),
        scratch_shapes=[pltpu.VMEM((blocks, *x.shape[1:]), x.dtype)],
        name="sum_all",
    )


def per_device(weights, filters, down_input, down_cot, up_input, up_cot):
    sections = lax.axis_size("section")
    mirror = [(s, sections - 1 - s) for s in range(sections)]
    down_pairs = [(s + 1, s) for s in range(sections - 1)]
    up_pairs = [(sections - s, s) for s in range(1, sections) if 2 * s != sections]
    weight = weights[0]
    down_xin, down_cot = down_input[0], down_cot[0]
    up_xin = lax.ppermute(up_input[0], "section", mirror)
    up_cot = lax.ppermute(up_cot[0], "section", mirror)
    blocks = lax.axis_size("tensor")
    depth = weight.shape[0]
    down_normed, down_mix = prepare(down_xin, down_cot)
    down_x = exchange(down_normed).reshape(-1, depth)
    down_arrivals = [both_ways(down_mix, down_mix)]
    causal, ahead = toeplitz(filters[0])
    (up_normed,) = prepare(up_xin, after=(ahead,))
    up_x = exchange(up_normed).reshape(-1, depth)
    up_mix = grad_mix(up_xin, up_cot, after=down_arrivals[0])
    up_arrivals = [both_ways(up_mix, up_mix)]
    down_part, down_pieces = project(down_x, weight, causal, after=(up_normed, up_mix))
    last = down_part
    for s in range(2, blocks):
        sent = payload(s, down_arrivals[-1], down_pieces, after=(last,))
        down_arrivals.append(both_ways(*sent))
        if s == 2:
            up_part, up_pieces = project(up_x, weight, causal, after=sent)
        sent = payload(s, up_arrivals[-1], up_pieces, after=sent)
        up_arrivals.append(both_ways(*sent))
        last = sent[0]
    sent = payload(blocks, up_arrivals[-1], up_pieces, after=(last, *down_arrivals[-1]))
    up_arrivals.append(both_ways(*sent))
    up_mixes, up_conv = sort_arrivals(up_mix, up_pieces, up_arrivals)
    up_g, up_back = back(up_mixes, weight, ahead, after=sent)
    up_back = exchange(up_back)
    down_mixes = list_blocks(down_mix, down_arrivals)
    sent = payload(blocks, down_arrivals[-1], down_pieces, after=(up_g,))
    down_arrivals.append(both_ways(*sent))
    down_g, down_back = back(down_mixes, weight, ahead, after=(sent[0], *up_arrivals[-1]))
    down_back = exchange(down_back)
    _, down_conv = sort_arrivals(down_mix, down_pieces, down_arrivals)
    up_grad = finish(up_xin, up_cot, up_conv, up_back, after=(down_g, *sent))
    up_passed = lax.ppermute(up_grad, "section", up_pairs)
    taps = filter_gradient(
        down_mixes, down_part, up_mixes, up_part, *filters.shape[1:], after=(up_grad,)
    )
    weight_grad = weight_gradient(down_x, up_x, down_g, up_g, after=(taps,))
    up_passed = settle(up_grad, up_passed, after=(weight_grad, *down_arrivals[-1]))
    down_grad = finish(down_xin, down_cot, down_conv, down_back, after=(up_passed,))
    down_passed = lax.ppermute(down_grad, "section", down_pairs)
    taps = sum_all(taps, after=(down_grad,))
    return weight_grad[None], taps, down_passed, up_passed


def solution(mesh):
    rows = P("section", "tensor", None)
    whole = P("section", None, None)
    return jax.shard_map(
        per_device,
        mesh=mesh,
        in_specs=(rows, whole, rows, rows, rows, rows),
        out_specs=(rows, whole, rows, rows),
        check_vma=False,
    )
```
